32 devices in a mesh: seq: 8 (over z, y), chan: 4 (over x, core).
Axes of the slice: x: 2, y: 2, z: 4, core: 2. Of those that a mesh axis runs over, the one named last changes fastest.
Arguments:
- hyena_query: bfloat16 [4096, 2048], P('chan', 'seq'), may hold values from -36 to 36
- hyena_key: bfloat16 [4096, 2048], P('chan', 'seq'), may hold values from -6 to 6
- hyena_value: bfloat16 [4096, 2048], P('chan', 'seq'), may hold values from -6 to 6
- long_filter: float32 [4096, 2048], P(('chan', 'seq')), may hold values from -4 to 4
- skip_weight: float32 [4096], P(('chan', 'seq')), may hold values from 0.5 to 1.5
- stripe_order: int32 [2048], replicated, may hold values from 0 to 2047, as said below
- query_rows: bfloat16 [2048, 4096], P('seq', 'chan'), may hold values from -6 to 6
- key_rows: bfloat16 [2048, 4096], P('seq', 'chan'), may hold values from -6 to 6
- norm_gain: float32 [4096], P('chan'), may hold values from 0.1 to 1.9
Outputs:
- hyena_output: bfloat16 [4096, 2048], P('chan', 'seq')
- attended: bfloat16 [2048, 4096], P('seq', 'chan')
The draws below stay inside these ranges and needn't reach their ends.
Inputs may be any that keep to these rules, and one draw needn't show every extreme that they name: stripe_order[256 * s + j] = 8 * j + sigma(s) for 0 <= j < 256 and 0 <= s < 8, where sigma is a permutation of 0 to 7.
All inputs are finite; a program needn't handle non-finite values.
Results may differ from the reference program's by a relative error of at most 0.012.
Values may be sent and summed in bfloat16 or wider, within the bound.
A program may use at most 128 MiB of HBM per device.

```python
import math
import jax
import jax.numpy as jnp
from jax import lax

D = 4096
HEADS = 32
HEAD_DIM = 128
ROWS = 256
SEQ_LEN = 2048


def stripe_layout(key):
    stripes = SEQ_LEN // ROWS
    sigma = jax.random.permutation(jax.random.fold_in(key, 11), stripes).astype(jnp.int32)
    local = jnp.arange(ROWS, dtype=jnp.int32)
    return (stripes * local[None, :] + sigma[:, None]).reshape(SEQ_LEN).astype(jnp.int32)


def draw_stripe_order(key, part):
    return stripe_layout(key)


def attention_pair(key):
    first, second = jax.random.split(jax.random.fold_in(key, 21), 2)
    query_drawn = jnp.clip(1.73 * jax.random.normal(first, (SEQ_LEN, D), jnp.float32), -6.0, 6.0)
    key_drawn = jnp.clip(1.73 * jax.random.normal(second, (SEQ_LEN, D), jnp.float32), -6.0, 6.0)
    places = stripe_layout(key)
    return (jnp.take(query_drawn, places, axis=0), jnp.take(key_drawn, places, axis=0))


def draw_query_rows(key, part):
    return attention_pair(key)[0].astype(jnp.bfloat16)


def draw_key_rows(key, part):
    return attention_pair(key)[1].astype(jnp.bfloat16)


def draw_hyena_query(key, part):
    first, second, third = jax.random.split(jax.random.fold_in(key, 31), 3)
    channel = jnp.arange(D, dtype=jnp.float32)
    column = 0.3 * jnp.exp(math.log(3.0) * channel / D + jax.random.uniform(first, (D,), jnp.float32, 0.0, math.log(10.0 / 3.0)))
    row_scale = 0.3 * jnp.exp(jax.random.uniform(second, (SEQ_LEN,), jnp.float32, 0.0, math.log(10.0)))
    noise = jnp.clip(jax.random.normal(third, (D, SEQ_LEN), jnp.float32), -4.0, 4.0)
    return (column[:, None] * row_scale[None, :] * noise).astype(jnp.bfloat16)


def draw_long_filter(key, part):
    first, second, third, fourth = jax.random.split(jax.random.fold_in(key, 41), 4)
    delay_steps = jnp.arange(SEQ_LEN, dtype=jnp.float32)
    window_extent = jnp.exp(jax.random.uniform(first, (D,), jnp.float32, math.log(32.0), math.log(4.0 * SEQ_LEN)))
    split_points = jax.random.randint(second, (3,), 1, SEQ_LEN).astype(jnp.float32)
    multiplier_list = jax.random.uniform(third, (3,), jnp.float32, 0.5, 0.8)
    impulse_train = jnp.prod(jnp.where(delay_steps[None, :] >= split_points[:, None], multiplier_list[:, None], 1.0), axis=0)
    decay_window = jnp.exp(-delay_steps[None, :] / window_extent[:, None]) * impulse_train[None, :]
    norm_value = jnp.sqrt(jnp.sum(decay_window * decay_window, axis=1, keepdims=True))
    noise = jnp.clip(jax.random.normal(fourth, (D, SEQ_LEN), jnp.float32), -4.0, 4.0)
    return noise * decay_window / norm_value


def levels(own_key, extent, cuts, low, top_value):
    gain = 1.0
    for position, shards_of in cuts:
        steps = jax.random.uniform(jax.random.fold_in(jax.random.fold_in(own_key, 6), position), (shards_of,), jnp.float32, low / len(cuts), top_value / len(cuts))
        gain = gain * jnp.repeat(jnp.exp(steps), extent[position] // shards_of).reshape((-1,) + (1,) * (len(extent) - 1 - position))
    return gain


def bell_draw(own_key, dims, deviation, limit, cuts=(), kind=jnp.bfloat16):
    values = jax.random.normal(own_key, dims, jnp.float32) * deviation
    if len(cuts) > 0:
        values = levels(own_key, dims, cuts, -0.22, 0.18) * values
    return jnp.clip(values, min=-limit, max=limit).astype(kind)


def setup_inputs(seed: int = 0) -> dict:
    key_of = jax.random.split(jax.random.key(seed), 10)
    return {
        "hyena_query": draw_hyena_query(jax.random.fold_in(key_of[9], 71), 0),
        "hyena_key": bell_draw(key_of[1], (D, SEQ_LEN), 1.0, 6.0, ((0, 4), (1, 8))),
        "hyena_value": bell_draw(key_of[2], (D, SEQ_LEN), 1.0, 6.0, ((0, 4), (1, 8))),
        "long_filter": draw_long_filter(jax.random.fold_in(key_of[9], 71), 0),
        "skip_weight": jnp.clip(0.5 + 1.0 * jax.random.uniform(key_of[4], (D,), jnp.float32) ** levels(key_of[4], (D,), ((0, 32),), -0.2, 0.2), 0.5, 1.5),
        "stripe_order": draw_stripe_order(jax.random.fold_in(key_of[9], 71), 0),
        "query_rows": draw_query_rows(jax.random.fold_in(key_of[9], 71), 0),
        "key_rows": draw_key_rows(jax.random.fold_in(key_of[9], 71), 0),
        "norm_gain": jnp.clip(1.0 + 0.18 * jax.random.normal(key_of[8], (D,), jnp.float32), 0.1, 1.9),
    }


def reference(hyena_query, hyena_key, hyena_value, long_filter, skip_weight, stripe_order, query_rows, key_rows, norm_gain):
    product = (hyena_key.astype(jnp.float32) * hyena_value.astype(jnp.float32)).astype(jnp.bfloat16)
    widened = lax.optimization_barrier(product).astype(jnp.float32)
    padded_length = 2 * SEQ_LEN
    spectrum = jnp.fft.rfft(widened, n=padded_length, axis=1) * jnp.fft.rfft(long_filter, n=padded_length, axis=1)
    convolved = jnp.fft.irfft(spectrum, n=padded_length, axis=1)[:, :SEQ_LEN]
    gated = (hyena_query.astype(jnp.float32) * (convolved + skip_weight[:, None] * widened)).astype(jnp.bfloat16)
    hyena_output = jnp.take(gated, stripe_order, axis=1)
    output_wide = lax.optimization_barrier(hyena_output).astype(jnp.float32)
    inverse_rms = lax.rsqrt(lax.optimization_barrier(jnp.mean(output_wide * output_wide, axis=0)) + 1e-05)
    normed = (output_wide * inverse_rms[None, :] * norm_gain[:, None]).astype(jnp.bfloat16).T
    block = math.gcd(SEQ_LEN, 512)
    scale = 1.0 / math.sqrt(HEAD_DIM)

    def one_head(inputs):
        head_query, head_key, head_value = inputs
        key_wide = head_key.astype(jnp.float32)
        value_expanded = head_value.astype(jnp.float32)

        def one_block(index):
            start = index * block
            query_wide = lax.dynamic_slice_in_dim(head_query, start, block).astype(jnp.float32)
            query_places = lax.dynamic_slice_in_dim(stripe_order, start, block)
            scores = jnp.dot(query_wide, key_wide.T, precision=lax.Precision.HIGHEST) * scale
            allowed = stripe_order[None, :] <= query_places[:, None]
            scores = jnp.where(allowed, scores, -1e+30)
            highest = lax.optimization_barrier(jnp.max(scores, axis=1, keepdims=True))
            weights = jnp.where(allowed, jnp.exp(scores - highest), 0.0)
            totals = lax.optimization_barrier(jnp.sum(weights, axis=1, keepdims=True))
            rounded = lax.optimization_barrier(weights.astype(jnp.bfloat16)).astype(jnp.float32)
            return jnp.dot(rounded, value_expanded, precision=lax.Precision.HIGHEST) / totals
        blocks = lax.map(one_block, jnp.arange(SEQ_LEN // block, dtype=jnp.int32))
        return blocks.reshape(SEQ_LEN, HEAD_DIM)
    head_queries = query_rows.reshape(SEQ_LEN, HEADS, HEAD_DIM).transpose(1, 0, 2)
    head_keys = key_rows.reshape(SEQ_LEN, HEADS, HEAD_DIM).transpose(1, 0, 2)
    head_values = normed.reshape(SEQ_LEN, HEADS, HEAD_DIM).transpose(1, 0, 2)
    results = lax.map(one_head, (head_queries, head_keys, head_values))
    attended = results.transpose(1, 0, 2).reshape(SEQ_LEN, D).astype(jnp.bfloat16)
    return (hyena_output, attended)
```

```python
import functools
import math

import jax
import jax.numpy as jnp
import ml_dtypes
import numpy as np
from jax import lax
from jax.experimental import pallas as pl
from jax.experimental.pallas import tpu as pltpu
from jax.sharding import PartitionSpec as P

D = 4096
HEAD_DIM = 128
TILES = 4
MESH = pl.DeviceIdType.MESH
PRODUCT, QUERIES, KEYS, GATES, BANDED, ATTENDED, SQUARES = range(7)
TRANSPOSED = (((1,), (1,)), ((), ()))


def high_low(table):
    high = table.astype(ml_dtypes.bfloat16)
    low = (table - high.astype(np.float64)).astype(ml_dtypes.bfloat16)
    return np.stack((high, low))


def odd_tables(stripes, rows):
    frequency = np.arange(rows, dtype=np.float64) + 0.5
    angle = 2.0 * np.pi * frequency[:, None] * np.arange(rows)[None, :] / (2 * rows)
    dense = np.concatenate((np.cos(angle), -np.sin(angle)), axis=0)
    twist = 2.0 * np.pi * frequency[:, None] * np.arange(stripes)[None, :] / (2 * rows * stripes)
    turns = np.zeros((rows, 128), np.float32)
    turns[:, :stripes] = np.cos(twist)
    turns[:, stripes : 2 * stripes] = np.sin(twist)
    return high_low(dense), high_low(dense.T), turns


def small_dft(parts, sign):
    count = len(parts)
    if count == 1:
        return parts
    even = small_dft(parts[0::2], sign)
    odd = small_dft(parts[1::2], sign)
    first, second = [], []
    for k in range(count // 2):
        real, imag = odd[k]
        cos = math.cos(2.0 * math.pi * k / count)
        sin = sign * math.sin(2.0 * math.pi * k / count)
        if k == 0:
            turned = (real, imag)
        elif 4 * k == count:
            turned = (-sign * imag, sign * real)
        else:
            turned = (real * cos - imag * sin, real * sin + imag * cos)
        first.append((even[k][0] + turned[0], even[k][1] + turned[1]))
        second.append((even[k][0] - turned[0], even[k][1] - turned[1]))
    return first + second


def dot(left, right):
    return jnp.dot(left, right, preferred_element_type=jnp.float32)


def split(wide):
    high = wide.astype(jnp.bfloat16)
    return high, (wide - high.astype(jnp.float32)).astype(jnp.bfloat16)


def fused_kernel(
    n,
    chans,
    order_ref,
    hk_ref,
    hv_ref,
    skip_ref,
    gain_ref,
    hq_hbm,
    filter_hbm,
    q_hbm,
    k_hbm,
    forward_hbm,
    inverse_hbm,
    turns_hbm,
    banded_ref,
    attended_ref,
    product_out,
    product_in,
    gate_in,
    q_in,
    k_in,
    filter_ref,
    forward_ref,
    inverse_ref,
    turns_ref,
    upright,
    signal,
    section,
    spectrum,
    back,
    convolved,
    gated,
    gated_out,
    weights,
    totals,
    values,
    result,
    squares,
    squares_chan,
    squares_sum,
    squares_seq,
    bias,
    send_sem,
    recv_sem,
    chan_send,
    chan_recv,
    local_sem,
):
    me = lax.axis_index("seq")
    my_chan = lax.axis_index("chan")
    pencil, rows = product_in.shape[1:]
    tile = rows // TILES
    wide_tile = n * tile

    def peer(offset):
        return lax.rem(me + offset, n)

    def block(ref, index):
        return ref.at[pl.ds(pl.multiple_of(index * pencil, pencil), pencil), :]

    def column(ref, index):
        return ref.at[:, pl.ds(pl.multiple_of(index * pencil, pencil), pencil)]

    def exchange(kind, source, target):
        return [
            pltpu.make_async_remote_copy(
                src_ref=source(peer(offset)),
                dst_ref=target,
                send_sem=send_sem.at[kind, offset],
                recv_sem=recv_sem.at[kind, offset],
                device_id={"seq": peer(offset)},
                device_id_type=MESH,
            )
            for offset in range(1, n)
        ]

    barrier = pltpu.get_barrier_semaphore()
    for offset in range(1, n):
        pl.semaphore_signal(barrier, inc=1, device_id={"seq": peer(offset)}, device_id_type=MESH)
    for offset in range(1, chans):
        other = lax.rem(my_chan + offset, chans)
        pl.semaphore_signal(barrier, inc=1, device_id={"chan": other}, device_id_type=MESH)

    staged = [
        (filter_hbm, filter_ref),
        (forward_hbm, forward_ref),
        (inverse_hbm, inverse_ref),
        (turns_hbm, turns_ref),
        (column(q_hbm, me), q_in.at[me]),
        (column(k_hbm, me), k_in.at[me]),
        (block(hq_hbm, me), gate_in.at[me]),
    ]
    staged = [
        pltpu.make_async_copy(source, target, local_sem.at[index])
        for index, (source, target) in enumerate(staged)
    ]
    for copy in staged:
        copy.start()

    def make_product(index, unused):
        part = pl.ds(pl.multiple_of(index * pencil, pencil), pencil)
        product_out[index] = (
            hk_ref[part, :].astype(jnp.float32) * hv_ref[part, :].astype(jnp.float32)
        ).astype(jnp.bfloat16)
        return unused

    lax.fori_loop(0, n, make_product, 0)
    pl.semaphore_wait(barrier, n - 1 + chans - 1)
    products = exchange(PRODUCT, lambda d: product_out.at[d], product_in.at[me])
    for copy in products:
        copy.start()
    product_in[me] = product_out[me]

    for copy in staged[:4]:
        copy.wait()

    def turned_sections(part):
        cos = turns_ref[part, :]
        parts = []
        for t in range(n):
            real = section[part, t * pencil : (t + 1) * pencil]
            below = pl.ds(pl.multiple_of(rows + part.start, part.size), part.size)
            imag = section[below, t * pencil : (t + 1) * pencil]
            c, s = cos[:, t : t + 1], cos[:, n + t : n + t + 1]
            parts.append((real * c + imag * s, imag * c - real * s))
        return small_dft(parts, -1.0)

    step = 16

    def filter_spectrum(index, unused):
        part = pl.ds(pl.multiple_of(index * step, step), step)
        scale = 1.0 / (rows * n)
        for k, (real, imag) in enumerate(turned_sections(part)):
            spectrum[0, part, k * pencil : (k + 1) * pencil] = real * scale
            spectrum[1, part, k * pencil : (k + 1) * pencil] = imag * scale
        return unused

    def signal_spectrum(index, unused):
        part = pl.ds(pl.multiple_of(index * step, step), step)
        below = pl.ds(pl.multiple_of(rows + index * step, step), step)
        parts = []
        for k, (real, imag) in enumerate(turned_sections(part)):
            other_real = spectrum[0, part, k * pencil : (k + 1) * pencil]
            other_imag = spectrum[1, part, k * pencil : (k + 1) * pencil]
            parts.append(
                (real * other_real - imag * other_imag, real * other_imag + imag * other_real)
            )
        cos = turns_ref[part, :]
        for t, (real, imag) in enumerate(small_dft(parts, 1.0)):
            c, s = cos[:, t : t + 1], cos[:, n + t : n + t + 1]
            lanes = slice(t * pencil, (t + 1) * pencil)
            for place, value in ((part, real * c - imag * s), (below, real * s + imag * c)):
                high, low = split(value)
                back[0, place, lanes] = high
                back[1, place, lanes] = low
        return unused

    for s in range(n):
        upright[s * rows : (s + 1) * rows, :] = filter_ref[:, s * rows : (s + 1) * rows].T
    for t in range(0, n, 2):
        pair = jnp.concatenate(
            [upright[pl.ds(t + u, rows, stride=n), :] for u in range(2)], axis=1
        )
        high, low = split(pair)
        section[:, t * pencil : (t + 2) * pencil] = (
            dot(forward_ref[0], high) + dot(forward_ref[1], high) + dot(forward_ref[0], low)
        )
    lax.fori_loop(0, rows // step, filter_spectrum, 0)

    def place_of(index, count):
        inner = lax.rem(index, tile)
        place = n * inner
        for s in range(n):
            place = place + jnp.where(index // tile == s, order_ref[s * rows], 0)
        return place

    key_place = place_of(lax.broadcasted_iota(jnp.int32, (8, wide_tile), 1), wide_tile)[:1]
    query_place = place_of(lax.broadcasted_iota(jnp.int32, (wide_tile, 128), 0), wide_tile)[:, :1]
    bias[...] = jnp.where(key_place <= query_place, 0.0, -1e30)

    for copy in products:
        copy.wait()

    queries = exchange(QUERIES, lambda d: column(q_hbm, d), q_in.at[me])
    keys = exchange(KEYS, lambda d: column(k_hbm, d), k_in.at[me])
    gates = exchange(GATES, lambda d: block(hq_hbm, d), gate_in.at[me])
    for copy in queries + keys + gates:
        copy.start()

    def stand_up(source):
        for s in range(n):
            upright[s * rows : (s + 1) * rows, :] = source[s].astype(jnp.float32).T

    stand_up(product_in)
    for t in range(0, n, 2):
        pair = [upright[pl.ds(t + u, rows, stride=n), :] for u in range(2)]
        signal[t] = pair[0]
        signal[t + 1] = pair[1]
        exact = jnp.concatenate(pair, axis=1).astype(jnp.bfloat16)
        section[:, t * pencil : (t + 2) * pencil] = dot(forward_ref[0], exact) + dot(
            forward_ref[1], exact
        )
    lax.fori_loop(0, rows // step, signal_spectrum, 0)
    for t in range(0, n, 2):
        lanes = slice(t * pencil, (t + 2) * pencil)
        high, low = back[0, :, lanes], back[1, :, lanes]
        pair = dot(inverse_ref[0], high) + dot(inverse_ref[1], high) + dot(inverse_ref[0], low)
        for u in range(2):
            convolved[t + u] = (
                pair[:, u * pencil : (u + 1) * pencil] + skip_ref[...] * signal[t + u]
            )

    for copy in queries + keys:
        copy.wait()
    for copy in staged[4:]:
        copy.wait()

    factor = math.log2(math.e) / math.sqrt(HEAD_DIM)
    half = n // 2
    for jt in range(TILES):
        for h in range(2):
            mine = slice(h * half * tile, (h + 1) * half * tile)
            query = q_in[h * half : (h + 1) * half, jt * tile : (jt + 1) * tile, :]
            query = query.reshape(half * tile, pencil)
            scores = []
            for kt in range(jt + 1):
                key = k_in[:, kt * tile : (kt + 1) * tile, :].reshape(wide_tile, pencil)
                score = lax.dot_general(
                    query, key, TRANSPOSED, preferred_element_type=jnp.float32
                )
                scores.append(score + bias[mine, :] if kt == jt else score)
            top = functools.reduce(jnp.maximum, [jnp.max(s, axis=1, keepdims=True) for s in scores])
            total = jnp.zeros((half * tile, 1), jnp.float32)
            for kt, score in enumerate(scores):
                weight = jnp.exp2((score - top) * factor)
                total = total + jnp.sum(weight, axis=1, keepdims=True)
                weights[jt, mine, kt * wide_tile : (kt + 1) * wide_tile] = weight.astype(
                    jnp.bfloat16
                )
            totals[jt, mine, :] = jnp.broadcast_to(total, (half * tile, pencil))

    for copy in gates:
        copy.wait()
    stand_up(gate_in)
    for t in range(n):
        gated[t] = (upright[pl.ds(t, rows, stride=n), :] * convolved[t]).astype(jnp.bfloat16)

    banded = exchange(BANDED, lambda d: gated_out.at[d], block(banded_ref, me))
    ones = jnp.ones((8, pencil), jnp.float32)
    for offset in list(range(1, n)) + [0]:
        to = peer(offset)
        mine = gated[order_ref[to * rows]].astype(jnp.float32)
        gated_out[to] = mine.T.astype(jnp.bfloat16)
        if offset:
            banded[offset - 1].start()
    own_banded = pltpu.make_async_copy(gated_out.at[me], block(banded_ref, me), local_sem.at[0])
    own_banded.start()
    for s in range(n):
        mine = gated[order_ref[s * rows]].astype(jnp.float32)
        values[s] = mine.astype(jnp.bfloat16)
        squares[s : s + 1, :] = lax.dot_general(
            ones,
            mine * mine,
            TRANSPOSED,
            precision=lax.Precision.HIGHEST,
            preferred_element_type=jnp.float32,
        )[:1]
    across = [
        pltpu.make_async_remote_copy(
            src_ref=squares,
            dst_ref=squares_chan.at[offset],
            send_sem=chan_send.at[offset],
            recv_sem=chan_recv.at[offset],
            device_id={"chan": lax.rem(my_chan + offset, chans)},
            device_id_type=MESH,
        )
        for offset in range(1, chans)
    ]
    for copy in across:
        copy.start()
    for copy in across:
        copy.wait()
    squares_sum[...] = functools.reduce(
        jnp.add, [squares[...]] + [squares_chan[offset] for offset in range(1, chans)]
    )
    along = exchange(SQUARES, lambda d: squares_sum, squares_seq.at[me])
    for copy in along:
        copy.start()
    squares_seq[me] = squares_sum[...]
    for copy in along:
        copy.wait()
    inverse_rms = lax.rsqrt(
        functools.reduce(jnp.add, [squares_seq[s] for s in range(n)]) / D + 1e-05
    )
    gain = gain_ref[pl.ds(me, 1), :]
    for s in range(n):
        scale = jnp.broadcast_to(inverse_rms[s : s + 1, :], (pencil, rows)).T
        values[s] = (values[s].astype(jnp.float32) * scale * gain).astype(jnp.bfloat16)

    for h in range(2):
        mine = slice(h * half * tile, (h + 1) * half * tile)
        for jt in range(TILES):
            total = jnp.zeros((half * tile, pencil), jnp.float32)
            for kt in range(jt + 1):
                value = values[:, kt * tile : (kt + 1) * tile, :].reshape(wide_tile, pencil)
                total = total + dot(weights[jt, mine, kt * wide_tile : (kt + 1) * wide_tile], value)
            part = (total / totals[jt, mine, :]).astype(jnp.bfloat16)
            result[h * half : (h + 1) * half, jt * tile : (jt + 1) * tile, :] = part.reshape(
                half, tile, pencil
            )
    attended = exchange(ATTENDED, lambda d: result.at[d], column(attended_ref, me))
    for copy in attended:
        copy.start()
    own_attended = pltpu.make_async_copy(result.at[me], column(attended_ref, me), local_sem.at[1])
    own_attended.start()
    for copy in banded + attended + [own_banded, own_attended]:
        copy.wait()


def fused(
    hyena_query,
    hyena_key,
    hyena_value,
    long_filter,
    skip_weight,
    stripe_order,
    query_rows,
    key_rows,
    norm_gain,
):
    n = lax.axis_size("seq")
    chans = lax.axis_size("chan")
    channels, rows = hyena_query.shape
    pencil = long_filter.shape[0]
    forward_table, inverse_table, turns = odd_tables(n, rows)
    vmem = pl.BlockSpec(memory_space=pltpu.VMEM)
    anywhere = pl.BlockSpec(memory_space=pl.ANY)
    bf16, f32 = jnp.bfloat16, jnp.float32
    wide = n * pencil
    tile = rows // TILES
    return pl.pallas_call(
        functools.partial(fused_kernel, n, chans),
        out_shape=(
            jax.ShapeDtypeStruct((channels, rows), bf16),
            jax.ShapeDtypeStruct((rows, channels), bf16),
        ),
        in_specs=[pl.BlockSpec(memory_space=pltpu.SMEM)] + [vmem] * 4 + [anywhere] * 7,
        out_specs=(anywhere, anywhere),
        scratch_shapes=[
            pltpu.VMEM((n, pencil, rows), bf16),
            pltpu.VMEM((n, pencil, rows), bf16),
            pltpu.VMEM((n, pencil, rows), bf16),
            pltpu.VMEM((n, rows, pencil), bf16),
            pltpu.VMEM((n, rows, pencil), bf16),
            pltpu.VMEM(long_filter.shape, f32),
            pltpu.VMEM(forward_table.shape, bf16),
            pltpu.VMEM(inverse_table.shape, bf16),
            pltpu.VMEM(turns.shape, f32),
            pltpu.VMEM((n * rows, pencil), f32),
            pltpu.VMEM((n, rows, pencil), f32),
            pltpu.VMEM((2 * rows, wide), f32),
            pltpu.VMEM((2, rows, wide), f32),
            pltpu.VMEM((2, 2 * rows, wide), bf16),
            pltpu.VMEM((n, rows, pencil), f32),
            pltpu.VMEM((n, rows, pencil), bf16),
            pltpu.VMEM((n, pencil, rows), bf16),
            pltpu.VMEM((TILES, n * tile, n * rows), bf16),
            pltpu.VMEM((TILES, n * tile, pencil), f32),
            pltpu.VMEM((n, rows, pencil), bf16),
            pltpu.VMEM((n, rows, pencil), bf16),
            pltpu.VMEM((n, rows), f32),
            pltpu.VMEM((chans, n, rows), f32),
            pltpu.VMEM((n, rows), f32),
            pltpu.VMEM((n, n, rows), f32),
            pltpu.VMEM((n * tile, n * tile), f32),
            pltpu.SemaphoreType.DMA((7, n)),
            pltpu.SemaphoreType.DMA((7, n)),
            pltpu.SemaphoreType.DMA((chans,)),
            pltpu.SemaphoreType.DMA((chans,)),
            pltpu.SemaphoreType.DMA((7,)),
        ],
        compiler_params=pltpu.CompilerParams(
            collective_id=0, has_side_effects=True, vmem_limit_bytes=56 * 1024 * 1024
        ),
    )(
        stripe_order,
        hyena_key,
        hyena_value,
        skip_weight.reshape(1, pencil),
        norm_gain.reshape(n, pencil),
        hyena_query,
        long_filter,
        query_rows,
        key_rows,
        jnp.asarray(forward_table),
        jnp.asarray(inverse_table),
        jnp.asarray(turns),
    )


def passed_along(block, axis, distance):
    devices = range(lax.axis_size(axis))
    route = [((i - distance) % len(devices), i) for i in devices]
    return lax.ppermute(block, axis, route)


def angle_table(first, second, modulus):
    left = jnp.arange(first, dtype=jnp.int32)[:, None]
    right = jnp.arange(second, dtype=jnp.int32)[None, :]
    theta = 2.0 * math.pi / modulus * (left * right % modulus).astype(jnp.float32)
    return (jnp.cos(theta), jnp.sin(theta))


def transform_tables(length):
    outer = 2 * length // 128
    first_cos, first_sin = angle_table(outer, outer // 2, outer)
    twist_cos, twist_sin = angle_table(outer, 128, 2 * length)
    inner_cos, inner_sin = angle_table(128, 128, 128)
    return (first_cos, first_sin, twist_cos, twist_sin, inner_cos, inner_sin)


def contract(form, left, right):
    return jnp.einsum(form, left, right, precision=lax.Precision.HIGHEST)


def forward(signal, tables):
    first_cos, first_sin, twist_cos, twist_sin, inner_cos, inner_sin = tables
    section_real = contract("kt,cts->cks", first_cos, signal)
    section_imag = -contract("kt,cts->cks", first_sin, signal)
    turned_real = section_real * twist_cos + section_imag * twist_sin
    turned_imag = section_imag * twist_cos - section_real * twist_sin
    out_real = contract("cks,sm->ckm", turned_real, inner_cos) + contract(
        "cks,sm->ckm", turned_imag, inner_sin
    )
    out_imag = contract("cks,sm->ckm", turned_imag, inner_cos) - contract(
        "cks,sm->ckm", turned_real, inner_sin
    )
    return (out_real, out_imag)


def inverse(spectrum_real, spectrum_imag, tables):
    first_cos, first_sin, twist_cos, twist_sin, inner_cos, inner_sin = tables
    back_real = contract("ckm,sm->cks", spectrum_real, inner_cos) - contract(
        "ckm,sm->cks", spectrum_imag, inner_sin
    )
    back_imag = contract("ckm,sm->cks", spectrum_real, inner_sin) + contract(
        "ckm,sm->cks", spectrum_imag, inner_cos
    )
    turned_real = back_real * twist_cos - back_imag * twist_sin
    turned_imag = back_real * twist_sin + back_imag * twist_cos
    signal = contract("kt,cks->cts", first_cos, turned_real) - contract(
        "kt,cks->cts", first_sin, turned_imag
    )
    return signal * (1.0 / (first_cos.shape[0] * 128))


def convolve(signal, filter_parts, tables):
    pencil, length = signal.shape
    widened = signal.astype(jnp.float32).reshape(pencil, length // 128, 128)
    signal_real, signal_imag = forward(widened, tables)
    filter_real, filter_imag = filter_parts
    product_real = signal_real * filter_real - signal_imag * filter_imag
    product_imag = signal_real * filter_imag + signal_imag * filter_real
    return inverse(product_real, product_imag, tables).reshape(pencil, length)


def fold_keys(carry, queries, own_places, key_piece, value_piece, places, scale):
    count = key_piece.shape[0]
    heads = queries.shape[1]
    depth = queries.shape[2]
    block = math.gcd(count, 512)
    place_blocks = places.reshape(count // block, block)
    key_blocks = key_piece.reshape(count // block, block, heads, depth)
    value_blocks = value_piece.reshape(count // block, block, heads, depth)

    def one_block(state, inputs):
        running, totals, sums = state
        key_block, value_block, key_places = inputs
        scores = (
            jnp.einsum("qhd,khd->hqk", queries, key_block, preferred_element_type=jnp.float32)
            * scale
        )
        allowed = key_places[None, None, :] <= own_places[None, :, None]
        scores = jnp.where(allowed, scores, -1e30)
        highest = jnp.maximum(running, jnp.max(scores, axis=2))
        weights = jnp.where(allowed, jnp.exp(scores - highest[:, :, None]), 0.0)
        factor = jnp.exp(running - highest)
        totals = totals * factor + jnp.sum(weights, axis=2)
        update = jnp.einsum(
            "hqk,khd->hqd",
            weights.astype(jnp.bfloat16),
            value_block,
            preferred_element_type=jnp.float32,
        )
        sums = sums * factor[:, :, None] + update
        return ((highest, totals, sums), None)

    carry, unused = lax.scan(one_block, carry, (key_blocks, value_blocks, place_blocks))
    return carry


def general(
    hyena_query,
    hyena_key,
    hyena_value,
    long_filter,
    skip_weight,
    stripe_order,
    query_rows,
    key_rows,
    norm_gain,
):
    stripes = lax.axis_size("seq")
    channels, rows = hyena_query.shape
    pencil, length = long_filter.shape
    sigma = stripe_order.reshape(stripes, rows)[:, 0]
    product = (hyena_key.astype(jnp.float32) * hyena_value.astype(jnp.float32)).astype(jnp.bfloat16)
    tables = transform_tables(length)
    filter_parts = forward(long_filter.reshape(pencil, length // 128, 128), tables)
    spread = lax.all_to_all(product, "seq", split_axis=0, concat_axis=1, tiled=True)
    summed = convolve(spread, filter_parts, tables) + skip_weight[:, None] * spread.astype(
        jnp.float32
    )
    returned = lax.all_to_all(
        summed.astype(jnp.bfloat16), "seq", split_axis=1, concat_axis=0, tiled=True
    ).astype(summed.dtype)
    gated = (hyena_query.astype(jnp.float32) * returned).astype(jnp.bfloat16)
    per_stripe = rows // stripes
    columns = stripes * jnp.arange(per_stripe, dtype=jnp.int32)[None, :] + sigma[:, None]
    arranged = jnp.take(gated, columns.reshape(rows), axis=1).reshape(channels, stripes, per_stripe)
    banded = lax.all_to_all(arranged, "seq", split_axis=1, concat_axis=2, tiled=True).reshape(
        channels, rows
    )
    output_wide = banded.astype(jnp.float32)
    squares = lax.psum(jnp.sum(output_wide * output_wide, axis=0), "chan")
    inverse_rms = lax.rsqrt(squares / D + 1e-05)
    normed = (output_wide * inverse_rms[None, :] * norm_gain[:, None]).astype(jnp.bfloat16)
    value_rows = normed.T
    local_heads = channels // HEAD_DIM
    scale = 1.0 / math.sqrt(HEAD_DIM)
    seq_index = lax.axis_index("seq")
    own_head = seq_index % local_heads
    group_index = seq_index // local_heads
    group_count = stripes // local_heads
    span = local_heads * rows
    stacked_local = jnp.stack((query_rows, key_rows, value_rows)).reshape(
        3, rows, local_heads, HEAD_DIM
    )
    collected = [lax.dynamic_index_in_dim(stacked_local, own_head, 2, keepdims=False)]
    for offset in range(1, local_heads):
        payload = lax.dynamic_index_in_dim(
            stacked_local, (own_head + offset) % local_heads, 2, keepdims=False
        )
        from_below = passed_along(payload, "seq", offset)
        from_above = passed_along(payload, "seq", offset - local_heads)
        collected.append(jnp.where(own_head >= offset, from_below, from_above))
    ordering = (own_head - jnp.arange(local_heads, dtype=jnp.int32)) % local_heads
    sources = jnp.take(jnp.stack(collected), ordering, axis=0)
    combined = sources.transpose(1, 0, 2, 3).reshape(3, span, HEAD_DIM)
    group_places = lax.dynamic_slice_in_dim(stripe_order, group_index * span, span)
    group_queries = combined[0].reshape(span, 1, HEAD_DIM)

    def visit(state, kv_pair, source):
        places = lax.dynamic_slice_in_dim(stripe_order, source * span, span)
        return fold_keys(
            state,
            group_queries,
            group_places,
            kv_pair[0].reshape(span, 1, HEAD_DIM),
            kv_pair[1].reshape(span, 1, HEAD_DIM),
            places,
            scale,
        )

    initial_group = (
        jnp.full((1, span), -1e30, jnp.float32),
        jnp.zeros((1, span), jnp.float32),
        jnp.zeros((1, span, HEAD_DIM), jnp.float32),
    )

    def cycle_turn(turn, loop_state):
        state, kv_pair = loop_state
        state = visit(state, kv_pair, (group_index - turn) % group_count)
        kv_pair = passed_along(kv_pair, "seq", local_heads)
        return (state, kv_pair)

    state, kv_pair = lax.fori_loop(0, group_count - 1, cycle_turn, (initial_group, combined[1:]))
    running, totals, sums = visit(state, kv_pair, (group_index - (group_count - 1)) % group_count)
    result = (sums[0] / totals[0][:, None]).astype(jnp.bfloat16)
    pieces = result.reshape(local_heads, rows, HEAD_DIM)
    returned_heads = [lax.dynamic_index_in_dim(pieces, own_head, 0, keepdims=False)]
    for offset in range(1, local_heads):
        payload = lax.dynamic_index_in_dim(
            pieces, (own_head + offset) % local_heads, 0, keepdims=False
        )
        back_below = passed_along(payload, "seq", offset)
        back_above = passed_along(payload, "seq", offset - local_heads)
        returned_heads.append(jnp.where(own_head >= offset, back_below, back_above))
    by_head = jnp.take(jnp.stack(returned_heads), ordering, axis=0)
    attended = by_head.transpose(1, 0, 2).reshape(rows, channels)
    return (banded, attended)


def local(*arrays):
    pencil = arrays[3].shape[0]
    rows = arrays[0].shape[1]
    stripes = lax.axis_size("seq")
    even = stripes % 2 == 0 and stripes & (stripes - 1) == 0 and 2 * stripes <= HEAD_DIM
    one_head = pencil == HEAD_DIM and even and rows % (16 * TILES) == 0
    return fused(*arrays) if one_head else general(*arrays)


def solution(mesh):
    placed = (
        P("chan", "seq"),
        P("chan", "seq"),
        P("chan", "seq"),
        P(("chan", "seq"), None),
        P(("chan", "seq")),
        P(),
        P("seq", "chan"),
        P("seq", "chan"),
        P("chan"),
    )
    return jax.shard_map(
        local,
        mesh=mesh,
        in_specs=placed,
        out_specs=(P("chan", "seq"), P("seq", "chan")),
        check_vma=False,
    )
```

```python
import functools
import math

import jax
import jax.numpy as jnp
import ml_dtypes
import numpy as np
from jax import lax
from jax.experimental import pallas as pl
from jax.experimental.pallas import tpu as pltpu
from jax.sharding import PartitionSpec as P

D = 4096
HEAD_DIM = 128
TILES = 4
MESH = pl.DeviceIdType.MESH
PRODUCT, QUERIES, KEYS, GATES, BANDED, ATTENDED, SQUARES = range(7)
TRANSPOSED = (((1,), (1,)), ((), ()))


def high_low(table):
    high = table.astype(ml_dtypes.bfloat16)
    low = (table - high.astype(np.float64)).astype(ml_dtypes.bfloat16)
    return np.stack((high, low))


def odd_tables(stripes, rows):
    frequency = np.arange(rows, dtype=np.float64) + 0.5
    angle = 2.0 * np.pi * frequency[:, None] * np.arange(rows)[None, :] / (2 * rows)
    dense = np.concatenate((np.cos(angle), -np.sin(angle)), axis=0)
    twist = 2.0 * np.pi * frequency[:, None] * np.arange(stripes)[None, :] / (2 * rows * stripes)
    turns = np.zeros((rows, 128), np.float32)
    turns[:, :stripes] = np.cos(twist)
    turns[:, stripes : 2 * stripes] = np.sin(twist)
    return high_low(dense), high_low(dense.T), turns


def small_dft(parts, sign):
    count = len(parts)
    if count == 1:
        return parts
    even = small_dft(parts[0::2], sign)
    odd = small_dft(parts[1::2], sign)
    first, second = [], []
    for k in range(count // 2):
        real, imag = odd[k]
        cos = math.cos(2.0 * math.pi * k / count)
        sin = sign * math.sin(2.0 * math.pi * k / count)
        if k == 0:
            turned = (real, imag)
        elif 4 * k == count:
            turned = (-sign * imag, sign * real)
        else:
            turned = (real * cos - imag * sin, real * sin + imag * cos)
        first.append((even[k][0] + turned[0], even[k][1] + turned[1]))
        second.append((even[k][0] - turned[0], even[k][1] - turned[1]))
    return first + second


def dot(left, right):
    return jnp.dot(left, right, preferred_element_type=jnp.float32)


def split(wide):
    high = wide.astype(jnp.bfloat16)
    return high, (wide - high.astype(jnp.float32)).astype(jnp.bfloat16)


def fused_kernel(
    n,
    chans,
    order_ref,
    hk_ref,
    hv_ref,
    skip_ref,
    gain_ref,
    hq_hbm,
    filter_hbm,
    q_hbm,
    k_hbm,
    forward_hbm,
    inverse_hbm,
    turns_hbm,
    banded_ref,
    attended_ref,
    product_out,
    product_in,
    gate_in,
    q_in,
    k_in,
    filter_ref,
    forward_ref,
    inverse_ref,
    turns_ref,
    upright,
    signal,
    section,
    spectrum,
    back,
    convolved,
    gated,
    gated_out,
    values,
    result,
    squares,
    squares_chan,
    squares_sum,
    squares_seq,
    bias,
    send_sem,
    recv_sem,
    chan_send,
    chan_recv,
    local_sem,
):
    me = lax.axis_index("seq")
    my_chan = lax.axis_index("chan")
    pencil, rows = product_in.shape[1:]
    tile = rows // TILES
    wide_tile = n * tile

    def peer(offset):
        return lax.rem(me + offset, n)

    def block(ref, index):
        return ref.at[pl.ds(pl.multiple_of(index * pencil, pencil), pencil), :]

    def column(ref, index):
        return ref.at[:, pl.ds(pl.multiple_of(index * pencil, pencil), pencil)]

    def exchange(kind, source, target):
        return [
            pltpu.make_async_remote_copy(
                src_ref=source(peer(offset)),
                dst_ref=target,
                send_sem=send_sem.at[kind, offset],
                recv_sem=recv_sem.at[kind, offset],
                device_id={"seq": peer(offset)},
                device_id_type=MESH,
            )
            for offset in range(1, n)
        ]

    barrier = pltpu.get_barrier_semaphore()
    for offset in range(1, n):
        pl.semaphore_signal(barrier, inc=1, device_id={"seq": peer(offset)}, device_id_type=MESH)
    for offset in range(1, chans):
        other = lax.rem(my_chan + offset, chans)
        pl.semaphore_signal(barrier, inc=1, device_id={"chan": other}, device_id_type=MESH)

    staged = [
        (filter_hbm, filter_ref),
        (forward_hbm, forward_ref),
        (inverse_hbm, inverse_ref),
        (turns_hbm, turns_ref),
        (column(q_hbm, me), q_in.at[me]),
        (column(k_hbm, me), k_in.at[me]),
        (block(hq_hbm, me), gate_in.at[me]),
    ]
    staged = [
        pltpu.make_async_copy(source, target, local_sem.at[index])
        for index, (source, target) in enumerate(staged)
    ]
    for copy in staged:
        copy.start()

    def make_product(index, unused):
        part = pl.ds(pl.multiple_of(index * pencil, pencil), pencil)
        product_out[index] = (
            hk_ref[part, :].astype(jnp.float32) * hv_ref[part, :].astype(jnp.float32)
        ).astype(jnp.bfloat16)
        return unused

    lax.fori_loop(0, n, make_product, 0)
    pl.semaphore_wait(barrier, n - 1 + chans - 1)
    products = exchange(PRODUCT, lambda d: product_out.at[d], product_in.at[me])
    queries = exchange(QUERIES, lambda d: column(q_hbm, d), q_in.at[me])
    keys = exchange(KEYS, lambda d: column(k_hbm, d), k_in.at[me])
    gates = exchange(GATES, lambda d: block(hq_hbm, d), gate_in.at[me])
    for copy in products + gates:
        copy.start()
    product_in[me] = product_out[me]

    for copy in staged[:4]:
        copy.wait()

    def turned_sections(part):
        cos = turns_ref[part, :]
        parts = []
        for t in range(n):
            real = section[part, t * pencil : (t + 1) * pencil]
            below = pl.ds(pl.multiple_of(rows + part.start, part.size), part.size)
            imag = section[below, t * pencil : (t + 1) * pencil]
            c, s = cos[:, t : t + 1], cos[:, n + t : n + t + 1]
            parts.append((real * c + imag * s, imag * c - real * s))
        return small_dft(parts, -1.0)

    step = 16

    def filter_spectrum(index, unused):
        part = pl.ds(pl.multiple_of(index * step, step), step)
        scale = 1.0 / (rows * n)
        for k, (real, imag) in enumerate(turned_sections(part)):
            spectrum[0, part, k * pencil : (k + 1) * pencil] = real * scale
            spectrum[1, part, k * pencil : (k + 1) * pencil] = imag * scale
        return unused

    def signal_spectrum(index, unused):
        part = pl.ds(pl.multiple_of(index * step, step), step)
        below = pl.ds(pl.multiple_of(rows + index * step, step), step)
        parts = []
        for k, (real, imag) in enumerate(turned_sections(part)):
            other_real = spectrum[0, part, k * pencil : (k + 1) * pencil]
            other_imag = spectrum[1, part, k * pencil : (k + 1) * pencil]
            parts.append(
                (real * other_real - imag * other_imag, real * other_imag + imag * other_real)
            )
        cos = turns_ref[part, :]
        for t, (real, imag) in enumerate(small_dft(parts, 1.0)):
            c, s = cos[:, t : t + 1], cos[:, n + t : n + t + 1]
            lanes = slice(t * pencil, (t + 1) * pencil)
            for place, value in ((part, real * c - imag * s), (below, real * s + imag * c)):
                high, low = split(value)
                back[0, place, lanes] = high
                back[1, place, lanes] = low
        return unused

    for s in range(n):
        upright[s * rows : (s + 1) * rows, :] = filter_ref[:, s * rows : (s + 1) * rows].T
    for t in range(0, n, 2):
        pair = jnp.concatenate(
            [upright[pl.ds(t + u, rows, stride=n), :] for u in range(2)], axis=1
        )
        high, low = split(pair)
        section[:, t * pencil : (t + 2) * pencil] = (
            dot(forward_ref[0], high) + dot(forward_ref[1], high) + dot(forward_ref[0], low)
        )
    lax.fori_loop(0, rows // step, filter_spectrum, 0)
    for copy in queries:
        copy.start()

    def place_of(index, count):
        inner = lax.rem(index, tile)
        place = n * inner
        for s in range(n):
            place = place + jnp.where(index // tile == s, order_ref[s * rows], 0)
        return place

    key_place = place_of(lax.broadcasted_iota(jnp.int32, (8, wide_tile), 1), wide_tile)[:1]
    query_place = place_of(lax.broadcasted_iota(jnp.int32, (wide_tile, 128), 0), wide_tile)[:, :1]
    bias[...] = jnp.where(key_place <= query_place, 0.0, -1e30)

    for copy in products:
        copy.wait()

    for copy in keys:
        copy.start()

    def stand_up(source):
        for s in range(n):
            upright[s * rows : (s + 1) * rows, :] = source[s].astype(jnp.float32).T

    stand_up(product_in)
    for t in range(0, n, 2):
        pair = [upright[pl.ds(t + u, rows, stride=n), :] for u in range(2)]
        signal[t] = pair[0]
        signal[t + 1] = pair[1]
        exact = jnp.concatenate(pair, axis=1).astype(jnp.bfloat16)
        section[:, t * pencil : (t + 2) * pencil] = dot(forward_ref[0], exact) + dot(
            forward_ref[1], exact
        )
    lax.fori_loop(0, rows // step, signal_spectrum, 0)
    for t in range(0, n, 2):
        lanes = slice(t * pencil, (t + 2) * pencil)
        high, low = back[0, :, lanes], back[1, :, lanes]
        pair = dot(inverse_ref[0], high) + dot(inverse_ref[1], high) + dot(inverse_ref[0], low)
        for u in range(2):
            convolved[t + u] = (
                pair[:, u * pencil : (u + 1) * pencil] + skip_ref[...] * signal[t + u]
            )

    for copy in staged[4:]:
        copy.wait()
    for copy in gates:
        copy.wait()
    stand_up(gate_in)
    for t in range(n):
        gated[t] = (upright[pl.ds(t, rows, stride=n), :] * convolved[t]).astype(jnp.bfloat16)

    banded = exchange(BANDED, lambda d: gated_out.at[d], block(banded_ref, me))
    ones = jnp.ones((8, pencil), jnp.float32)
    for offset in list(range(1, n)) + [0]:
        to = peer(offset)
        mine = gated[order_ref[to * rows]].astype(jnp.float32)
        gated_out[to] = mine.T.astype(jnp.bfloat16)
    for s in range(n):
        mine = gated[order_ref[s * rows]].astype(jnp.float32)
        values[s] = mine.astype(jnp.bfloat16)
        squares[s : s + 1, :] = lax.dot_general(
            ones,
            mine * mine,
            TRANSPOSED,
            precision=lax.Precision.HIGHEST,
            preferred_element_type=jnp.float32,
        )[:1]
    across = [
        pltpu.make_async_remote_copy(
            src_ref=squares,
            dst_ref=squares_chan.at[offset],
            send_sem=chan_send.at[offset],
            recv_sem=chan_recv.at[offset],
            device_id={"chan": lax.rem(my_chan + offset, chans)},
            device_id_type=MESH,
        )
        for offset in range(1, chans)
    ]
    for copy in across:
        copy.start()
    for copy in across:
        copy.wait()
    squares_sum[...] = functools.reduce(
        jnp.add, [squares[...]] + [squares_chan[offset] for offset in range(1, chans)]
    )
    along = exchange(SQUARES, lambda d: squares_sum, squares_seq.at[me])
    for copy in along:
        copy.start()
    squares_seq[me] = squares_sum[...]
    for copy in along:
        copy.wait()
    inverse_rms = lax.rsqrt(
        functools.reduce(jnp.add, [squares_seq[s] for s in range(n)]) / D + 1e-05
    )
    gain = gain_ref[pl.ds(me, 1), :]
    for s in range(n):
        scale = jnp.broadcast_to(inverse_rms[s : s + 1, :], (pencil, rows)).T
        values[s] = (values[s].astype(jnp.float32) * scale * gain).astype(jnp.bfloat16)

    for copy in keys:
        copy.wait_send()
    for copy in banded:
        copy.start()
    own_banded = pltpu.make_async_copy(gated_out.at[me], block(banded_ref, me), local_sem.at[0])
    own_banded.start()
    for copy in queries:
        copy.wait()
    for copy in keys:
        copy.wait_recv()

    factor = math.log2(math.e) / math.sqrt(HEAD_DIM)
    half = n // 2
    height = half * tile
    attended = exchange(ATTENDED, lambda d: result.at[d], column(attended_ref, me))

    def attend_half(turn, unused):
        h = lax.rem(1 - me // half + turn, 2)
        first = pl.multiple_of(h * half, half)
        for jt in range(TILES):
            query = q_in[pl.ds(first, half), jt * tile : (jt + 1) * tile, :]
            query = query.reshape(height, pencil)
            scores = []
            for kt in range(jt + 1):
                key = k_in[:, kt * tile : (kt + 1) * tile, :].reshape(wide_tile, pencil)
                score = lax.dot_general(
                    query, key, TRANSPOSED, preferred_element_type=jnp.float32
                )
                if kt == jt:
                    score = score + bias[pl.ds(pl.multiple_of(h * height, height), height), :]
                scores.append(score)
            top = functools.reduce(jnp.maximum, [jnp.max(s, axis=1, keepdims=True) for s in scores])
            total = jnp.zeros((height, 1), jnp.float32)
            summed = jnp.zeros((height, pencil), jnp.float32)
            for kt, score in enumerate(scores):
                weight = jnp.exp2((score - top) * factor)
                total = total + jnp.sum(weight, axis=1, keepdims=True)
                value = values[:, kt * tile : (kt + 1) * tile, :].reshape(wide_tile, pencil)
                summed = summed + dot(weight.astype(jnp.bfloat16), value)
            part = (summed / total).astype(jnp.bfloat16)
            result[pl.ds(first, half), jt * tile : (jt + 1) * tile, :] = part.reshape(
                half, tile, pencil
            )
        for offset in range(1, n):

            @pl.when(peer(offset) // half == h)
            def send():
                attended[offset - 1].start()

        return unused

    lax.fori_loop(0, 2, attend_half, 0)
    own_attended = pltpu.make_async_copy(result.at[me], column(attended_ref, me), local_sem.at[1])
    own_attended.start()
    for copy in banded + attended + [own_banded, own_attended]:
        copy.wait()


def settle_kernel(banded_ref, attended_ref, banded_out, attended_out, sems):
    copies = []
    for source, target in ((banded_ref, banded_out), (attended_ref, attended_out)):
        part = source.shape[0] // 4
        for index in range(4):
            rows = pl.ds(index * part, part)
            copies.append(
                pltpu.make_async_copy(source.at[rows], target.at[rows], sems.at[len(copies)])
            )
    for copy in copies:
        copy.start()
    for copy in copies:
        copy.wait()


def settled(*arrays):
    anywhere = pl.BlockSpec(memory_space=pl.ANY)
    return pl.pallas_call(
        settle_kernel,
        out_shape=tuple(jax.ShapeDtypeStruct(a.shape, a.dtype) for a in arrays),
        in_specs=[anywhere] * 2,
        out_specs=(anywhere, anywhere),
        scratch_shapes=[pltpu.SemaphoreType.DMA((8,))],
    )(*arrays)


def fused(
    hyena_query,
    hyena_key,
    hyena_value,
    long_filter,
    skip_weight,
    stripe_order,
    query_rows,
    key_rows,
    norm_gain,
):
    n = lax.axis_size("seq")
    chans = lax.axis_size("chan")
    channels, rows = hyena_query.shape
    pencil = long_filter.shape[0]
    forward_table, inverse_table, turns = odd_tables(n, rows)
    vmem = pl.BlockSpec(memory_space=pltpu.VMEM)
    anywhere = pl.BlockSpec(memory_space=pl.ANY)
    bf16, f32 = jnp.bfloat16, jnp.float32
    wide = n * pencil
    tile = rows // TILES
    outputs = pl.pallas_call(
        functools.partial(fused_kernel, n, chans),
        out_shape=(
            jax.ShapeDtypeStruct((channels, rows), bf16),
            jax.ShapeDtypeStruct((rows, channels), bf16),
        ),
        in_specs=[pl.BlockSpec(memory_space=pltpu.SMEM)] + [vmem] * 4 + [anywhere] * 7,
        out_specs=(anywhere, anywhere),
        scratch_shapes=[
            pltpu.VMEM((n, pencil, rows), bf16),
            pltpu.VMEM((n, pencil, rows), bf16),
            pltpu.VMEM((n, pencil, rows), bf16),
            pltpu.VMEM((n, rows, pencil), bf16),
            pltpu.VMEM((n, rows, pencil), bf16),
            pltpu.VMEM(long_filter.shape, f32),
            pltpu.VMEM(forward_table.shape, bf16),
            pltpu.VMEM(inverse_table.shape, bf16),
            pltpu.VMEM(turns.shape, f32),
            pltpu.VMEM((n * rows, pencil), f32),
            pltpu.VMEM((n, rows, pencil), f32),
            pltpu.VMEM((2 * rows, wide), f32),
            pltpu.VMEM((2, rows, wide), f32),
            pltpu.VMEM((2, 2 * rows, wide), bf16),
            pltpu.VMEM((n, rows, pencil), f32),
            pltpu.VMEM((n, rows, pencil), bf16),
            pltpu.VMEM((n, pencil, rows), bf16),
            pltpu.VMEM((n, rows, pencil), bf16),
            pltpu.VMEM((n, rows, pencil), bf16),
            pltpu.VMEM((n, rows), f32),
            pltpu.VMEM((chans, n, rows), f32),
            pltpu.VMEM((n, rows), f32),
            pltpu.VMEM((n, n, rows), f32),
            pltpu.VMEM((n * tile, n * tile), f32),
            pltpu.SemaphoreType.DMA((7, n)),
            pltpu.SemaphoreType.DMA((7, n)),
            pltpu.SemaphoreType.DMA((chans,)),
            pltpu.SemaphoreType.DMA((chans,)),
            pltpu.SemaphoreType.DMA((7,)),
        ],
        compiler_params=pltpu.CompilerParams(
            collective_id=0, has_side_effects=True, vmem_limit_bytes=56 * 1024 * 1024
        ),
    )(
        stripe_order,
        hyena_key,
        hyena_value,
        skip_weight.reshape(1, pencil),
        norm_gain.reshape(n, pencil),
        hyena_query,
        long_filter,
        query_rows,
        key_rows,
        jnp.asarray(forward_table),
        jnp.asarray(inverse_table),
        jnp.asarray(turns),
    )
    return settled(*outputs)


def passed_along(block, axis, distance):
    devices = range(lax.axis_size(axis))
    route = [((i - distance) % len(devices), i) for i in devices]
    return lax.ppermute(block, axis, route)


def angle_table(first, second, modulus):
    left = jnp.arange(first, dtype=jnp.int32)[:, None]
    right = jnp.arange(second, dtype=jnp.int32)[None, :]
    theta = 2.0 * math.pi / modulus * (left * right % modulus).astype(jnp.float32)
    return (jnp.cos(theta), jnp.sin(theta))


def transform_tables(length):
    outer = 2 * length // 128
    first_cos, first_sin = angle_table(outer, outer // 2, outer)
    twist_cos, twist_sin = angle_table(outer, 128, 2 * length)
    inner_cos, inner_sin = angle_table(128, 128, 128)
    return (first_cos, first_sin, twist_cos, twist_sin, inner_cos, inner_sin)


def contract(form, left, right):
    return jnp.einsum(form, left, right, precision=lax.Precision.HIGHEST)


def forward(signal, tables):
    first_cos, first_sin, twist_cos, twist_sin, inner_cos, inner_sin = tables
    section_real = contract("kt,cts->cks", first_cos, signal)
    section_imag = -contract("kt,cts->cks", first_sin, signal)
    turned_real = section_real * twist_cos + section_imag * twist_sin
    turned_imag = section_imag * twist_cos - section_real * twist_sin
    out_real = contract("cks,sm->ckm", turned_real, inner_cos) + contract(
        "cks,sm->ckm", turned_imag, inner_sin
    )
    out_imag = contract("cks,sm->ckm", turned_imag, inner_cos) - contract(
        "cks,sm->ckm", turned_real, inner_sin
    )
    return (out_real, out_imag)


def inverse(spectrum_real, spectrum_imag, tables):
    first_cos, first_sin, twist_cos, twist_sin, inner_cos, inner_sin = tables
    back_real = contract("ckm,sm->cks", spectrum_real, inner_cos) - contract(
        "ckm,sm->cks", spectrum_imag, inner_sin
    )
    back_imag = contract("ckm,sm->cks", spectrum_real, inner_sin) + contract(
        "ckm,sm->cks", spectrum_imag, inner_cos
    )
    turned_real = back_real * twist_cos - back_imag * twist_sin
    turned_imag = back_real * twist_sin + back_imag * twist_cos
    signal = contract("kt,cks->cts", first_cos, turned_real) - contract(
        "kt,cks->cts", first_sin, turned_imag
    )
    return signal * (1.0 / (first_cos.shape[0] * 128))


def convolve(signal, filter_parts, tables):
    pencil, length = signal.shape
    widened = signal.astype(jnp.float32).reshape(pencil, length // 128, 128)
    signal_real, signal_imag = forward(widened, tables)
    filter_real, filter_imag = filter_parts
    product_real = signal_real * filter_real - signal_imag * filter_imag
    product_imag = signal_real * filter_imag + signal_imag * filter_real
    return inverse(product_real, product_imag, tables).reshape(pencil, length)


def fold_keys(carry, queries, own_places, key_piece, value_piece, places, scale):
    count = key_piece.shape[0]
    heads = queries.shape[1]
    depth = queries.shape[2]
    block = math.gcd(count, 512)
    place_blocks = places.reshape(count // block, block)
    key_blocks = key_piece.reshape(count // block, block, heads, depth)
    value_blocks = value_piece.reshape(count // block, block, heads, depth)

    def one_block(state, inputs):
        running, totals, sums = state
        key_block, value_block, key_places = inputs
        scores = (
            jnp.einsum("qhd,khd->hqk", queries, key_block, preferred_element_type=jnp.float32)
            * scale
        )
        allowed = key_places[None, None, :] <= own_places[None, :, None]
        scores = jnp.where(allowed, scores, -1e30)
        highest = jnp.maximum(running, jnp.max(scores, axis=2))
        weights = jnp.where(allowed, jnp.exp(scores - highest[:, :, None]), 0.0)
        factor = jnp.exp(running - highest)
        totals = totals * factor + jnp.sum(weights, axis=2)
        update = jnp.einsum(
            "hqk,khd->hqd",
            weights.astype(jnp.bfloat16),
            value_block,
            preferred_element_type=jnp.float32,
        )
        sums = sums * factor[:, :, None] + update
        return ((highest, totals, sums), None)

    carry, unused = lax.scan(one_block, carry, (key_blocks, value_blocks, place_blocks))
    return carry


def general(
    hyena_query,
    hyena_key,
    hyena_value,
    long_filter,
    skip_weight,
    stripe_order,
    query_rows,
    key_rows,
    norm_gain,
):
    stripes = lax.axis_size("seq")
    channels, rows = hyena_query.shape
    pencil, length = long_filter.shape
    sigma = stripe_order.reshape(stripes, rows)[:, 0]
    product = (hyena_key.astype(jnp.float32) * hyena_value.astype(jnp.float32)).astype(jnp.bfloat16)
    tables = transform_tables(length)
    filter_parts = forward(long_filter.reshape(pencil, length // 128, 128), tables)
    spread = lax.all_to_all(product, "seq", split_axis=0, concat_axis=1, tiled=True)
    summed = convolve(spread, filter_parts, tables) + skip_weight[:, None] * spread.astype(
        jnp.float32
    )
    returned = lax.all_to_all(
        summed.astype(jnp.bfloat16), "seq", split_axis=1, concat_axis=0, tiled=True
    ).astype(summed.dtype)
    gated = (hyena_query.astype(jnp.float32) * returned).astype(jnp.bfloat16)
    per_stripe = rows // stripes
    columns = stripes * jnp.arange(per_stripe, dtype=jnp.int32)[None, :] + sigma[:, None]
    arranged = jnp.take(gated, columns.reshape(rows), axis=1).reshape(channels, stripes, per_stripe)
    banded = lax.all_to_all(arranged, "seq", split_axis=1, concat_axis=2, tiled=True).reshape(
        channels, rows
    )
    output_wide = banded.astype(jnp.float32)
    squares = lax.psum(jnp.sum(output_wide * output_wide, axis=0), "chan")
    inverse_rms = lax.rsqrt(squares / D + 1e-05)
    normed = (output_wide * inverse_rms[None, :] * norm_gain[:, None]).astype(jnp.bfloat16)
    value_rows = normed.T
    local_heads = channels // HEAD_DIM
    scale = 1.0 / math.sqrt(HEAD_DIM)
    seq_index = lax.axis_index("seq")
    own_head = seq_index % local_heads
    group_index = seq_index // local_heads
    group_count = stripes // local_heads
    span = local_heads * rows
    stacked_local = jnp.stack((query_rows, key_rows, value_rows)).reshape(
        3, rows, local_heads, HEAD_DIM
    )
    collected = [lax.dynamic_index_in_dim(stacked_local, own_head, 2, keepdims=False)]
    for offset in range(1, local_heads):
        payload = lax.dynamic_index_in_dim(
            stacked_local, (own_head + offset) % local_heads, 2, keepdims=False
        )
        from_below = passed_along(payload, "seq", offset)
        from_above = passed_along(payload, "seq", offset - local_heads)
        collected.append(jnp.where(own_head >= offset, from_below, from_above))
    ordering = (own_head - jnp.arange(local_heads, dtype=jnp.int32)) % local_heads
    sources = jnp.take(jnp.stack(collected), ordering, axis=0)
    combined = sources.transpose(1, 0, 2, 3).reshape(3, span, HEAD_DIM)
    group_places = lax.dynamic_slice_in_dim(stripe_order, group_index * span, span)
    group_queries = combined[0].reshape(span, 1, HEAD_DIM)

    def visit(state, kv_pair, source):
        places = lax.dynamic_slice_in_dim(stripe_order, source * span, span)
        return fold_keys(
            state,
            group_queries,
            group_places,
            kv_pair[0].reshape(span, 1, HEAD_DIM),
            kv_pair[1].reshape(span, 1, HEAD_DIM),
            places,
            scale,
        )

    initial_group = (
        jnp.full((1, span), -1e30, jnp.float32),
        jnp.zeros((1, span), jnp.float32),
        jnp.zeros((1, span, HEAD_DIM), jnp.float32),
    )

    def cycle_turn(turn, loop_state):
        state, kv_pair = loop_state
        state = visit(state, kv_pair, (group_index - turn) % group_count)
        kv_pair = passed_along(kv_pair, "seq", local_heads)
        return (state, kv_pair)

    state, kv_pair = lax.fori_loop(0, group_count - 1, cycle_turn, (initial_group, combined[1:]))
    running, totals, sums = visit(state, kv_pair, (group_index - (group_count - 1)) % group_count)
    result = (sums[0] / totals[0][:, None]).astype(jnp.bfloat16)
    pieces = result.reshape(local_heads, rows, HEAD_DIM)
    returned_heads = [lax.dynamic_index_in_dim(pieces, own_head, 0, keepdims=False)]
    for offset in range(1, local_heads):
        payload = lax.dynamic_index_in_dim(
            pieces, (own_head + offset) % local_heads, 0, keepdims=False
        )
        back_below = passed_along(payload, "seq", offset)
        back_above = passed_along(payload, "seq", offset - local_heads)
        returned_heads.append(jnp.where(own_head >= offset, back_below, back_above))
    by_head = jnp.take(jnp.stack(returned_heads), ordering, axis=0)
    attended = by_head.transpose(1, 0, 2).reshape(rows, channels)
    return (banded, attended)


def local(*arrays):
    pencil = arrays[3].shape[0]
    rows = arrays[0].shape[1]
    stripes = lax.axis_size("seq")
    even = stripes % 2 == 0 and stripes & (stripes - 1) == 0 and 2 * stripes <= HEAD_DIM
    one_head = pencil == HEAD_DIM and even and rows % (16 * TILES) == 0
    return fused(*arrays) if one_head else general(*arrays)


def solution(mesh):
    placed = (
        P("chan", "seq"),
        P("chan", "seq"),
        P("chan", "seq"),
        P(("chan", "seq"), None),
        P(("chan", "seq")),
        P(),
        P("seq", "chan"),
        P("seq", "chan"),
        P("chan"),
    )
    return jax.shard_map(
        local,
        mesh=mesh,
        in_specs=placed,
        out_specs=(P("chan", "seq"), P("seq", "chan")),
        check_vma=False,
    )
```

```python
import functools
import math

import jax
import jax.numpy as jnp
import ml_dtypes
import numpy as np
from jax import lax
from jax.experimental import pallas as pl
from jax.experimental.pallas import tpu as pltpu
from jax.sharding import PartitionSpec as P

D = 4096
HEAD_DIM = 128
TILES = 4
MESH = pl.DeviceIdType.MESH
PRODUCT, QUERIES, KEYS, GATES, BANDED, ATTENDED, SQUARES = range(7)
TRANSPOSED = (((1,), (1,)), ((), ()))


def high_low(table):
    high = table.astype(ml_dtypes.bfloat16)
    low = (table - high.astype(np.float64)).astype(ml_dtypes.bfloat16)
    return np.stack((high, low))


def odd_tables(stripes, rows):
    frequency = np.arange(rows, dtype=np.float64) + 0.5
    angle = 2.0 * np.pi * frequency[:, None] * np.arange(rows)[None, :] / (2 * rows)
    dense = np.concatenate((np.cos(angle), -np.sin(angle)), axis=0)
    twist = 2.0 * np.pi * frequency[:, None] * np.arange(stripes)[None, :] / (2 * rows * stripes)
    turns = np.zeros((rows, 128), np.float32)
    turns[:, :stripes] = np.cos(twist)
    turns[:, stripes : 2 * stripes] = np.sin(twist)
    return high_low(dense), high_low(dense.T), turns


def small_dft(parts, sign):
    count = len(parts)
    if count == 1:
        return parts
    even = small_dft(parts[0::2], sign)
    odd = small_dft(parts[1::2], sign)
    first, second = [], []
    for k in range(count // 2):
        real, imag = odd[k]
        cos = math.cos(2.0 * math.pi * k / count)
        sin = sign * math.sin(2.0 * math.pi * k / count)
        if k == 0:
            turned = (real, imag)
        elif 4 * k == count:
            turned = (-sign * imag, sign * real)
        else:
            turned = (real * cos - imag * sin, real * sin + imag * cos)
        first.append((even[k][0] + turned[0], even[k][1] + turned[1]))
        second.append((even[k][0] - turned[0], even[k][1] - turned[1]))
    return first + second


def dot(left, right):
    return jnp.dot(left, right, preferred_element_type=jnp.float32)


def split(wide):
    high = wide.astype(jnp.bfloat16)
    return high, (wide - high.astype(jnp.float32)).astype(jnp.bfloat16)


def fused_kernel(
    n,
    chans,
    order_ref,
    hk_ref,
    hv_ref,
    skip_ref,
    gain_ref,
    hq_hbm,
    filter_hbm,
    q_hbm,
    k_hbm,
    forward_hbm,
    inverse_hbm,
    turns_hbm,
    banded_ref,
    attended_ref,
    gate_all,
    q_all,
    k_all,
    product_out,
    product_in,
    gate_in,
    q_in,
    k_in,
    filter_ref,
    forward_ref,
    inverse_ref,
    turns_ref,
    upright,
    signal,
    section,
    spectrum,
    back,
    convolved,
    gated,
    gated_out,
    values,
    result,
    squares,
    squares_chan,
    squares_sum,
    squares_seq,
    bias,
    send_sem,
    recv_sem,
    chan_send,
    chan_recv,
    local_sem,
):
    me = lax.axis_index("seq")
    my_chan = lax.axis_index("chan")
    pencil, rows = product_in.shape[1:]
    tile = rows // TILES
    wide_tile = n * tile

    def peer(offset):
        return lax.rem(me + offset, n)

    def block(ref, index):
        return ref.at[pl.ds(pl.multiple_of(index * pencil, pencil), pencil), :]

    def column(ref, index):
        return ref.at[:, pl.ds(pl.multiple_of(index * pencil, pencil), pencil)]

    def exchange(kind, source, target):
        return [
            pltpu.make_async_remote_copy(
                src_ref=source(peer(offset)),
                dst_ref=target,
                send_sem=send_sem.at[kind, offset],
                recv_sem=recv_sem.at[kind, offset],
                device_id={"seq": peer(offset)},
                device_id_type=MESH,
            )
            for offset in range(1, n)
        ]

    barrier = pltpu.get_barrier_semaphore()
    for offset in range(1, n):
        pl.semaphore_signal(barrier, inc=1, device_id={"seq": peer(offset)}, device_id_type=MESH)
    for offset in range(1, chans):
        other = lax.rem(my_chan + offset, chans)
        pl.semaphore_signal(barrier, inc=1, device_id={"chan": other}, device_id_type=MESH)

    staged = [
        (filter_hbm, filter_ref),
        (forward_hbm, forward_ref),
        (inverse_hbm, inverse_ref),
        (turns_hbm, turns_ref),
        (hq_hbm, gate_all),
        (q_hbm, q_all),
        (k_hbm, k_all),
    ]
    staged = [
        pltpu.make_async_copy(source, target, local_sem.at[index])
        for index, (source, target) in enumerate(staged)
    ]
    for copy in staged:
        copy.start()

    def make_product(index, unused):
        part = pl.ds(pl.multiple_of(index * pencil, pencil), pencil)
        product_out[index] = (
            hk_ref[part, :].astype(jnp.float32) * hv_ref[part, :].astype(jnp.float32)
        ).astype(jnp.bfloat16)
        return unused

    lax.fori_loop(0, n, make_product, 0)
    pl.semaphore_wait(barrier, n - 1 + chans - 1)
    staged[4].wait()
    products = exchange(PRODUCT, lambda d: product_out.at[d], product_in.at[me])
    queries = exchange(QUERIES, lambda d: column(q_all, d), q_in.at[me])
    keys = exchange(KEYS, lambda d: column(k_all, d), k_in.at[me])
    gates = exchange(GATES, lambda d: block(gate_all, d), gate_in.at[me])
    for copy in products + gates:
        copy.start()
    product_in[me] = product_out[me]
    gate_in[me] = block(gate_all, me)[...]

    for copy in staged[:4] + staged[5:]:
        copy.wait()
    q_in[me] = column(q_all, me)[...]
    k_in[me] = column(k_all, me)[...]

    def turned_sections(part):
        cos = turns_ref[part, :]
        parts = []
        for t in range(n):
            real = section[part, t * pencil : (t + 1) * pencil]
            below = pl.ds(pl.multiple_of(rows + part.start, part.size), part.size)
            imag = section[below, t * pencil : (t + 1) * pencil]
            c, s = cos[:, t : t + 1], cos[:, n + t : n + t + 1]
            parts.append((real * c + imag * s, imag * c - real * s))
        return small_dft(parts, -1.0)

    step = 16

    def filter_spectrum(index, unused):
        part = pl.ds(pl.multiple_of(index * step, step), step)
        scale = 1.0 / (rows * n)
        for k, (real, imag) in enumerate(turned_sections(part)):
            spectrum[0, part, k * pencil : (k + 1) * pencil] = real * scale
            spectrum[1, part, k * pencil : (k + 1) * pencil] = imag * scale
        return unused

    def signal_spectrum(index, unused):
        part = pl.ds(pl.multiple_of(index * step, step), step)
        below = pl.ds(pl.multiple_of(rows + index * step, step), step)
        parts = []
        for k, (real, imag) in enumerate(turned_sections(part)):
            other_real = spectrum[0, part, k * pencil : (k + 1) * pencil]
            other_imag = spectrum[1, part, k * pencil : (k + 1) * pencil]
            parts.append(
                (real * other_real - imag * other_imag, real * other_imag + imag * other_real)
            )
        cos = turns_ref[part, :]
        for t, (real, imag) in enumerate(small_dft(parts, 1.0)):
            c, s = cos[:, t : t + 1], cos[:, n + t : n + t + 1]
            lanes = slice(t * pencil, (t + 1) * pencil)
            for place, value in ((part, real * c - imag * s), (below, real * s + imag * c)):
                high, low = split(value)
                back[0, place, lanes] = high
                back[1, place, lanes] = low
        return unused

    for s in range(n):
        upright[s * rows : (s + 1) * rows, :] = filter_ref[:, s * rows : (s + 1) * rows].T
    for t in range(0, n, 2):
        pair = jnp.concatenate(
            [upright[pl.ds(t + u, rows, stride=n), :] for u in range(2)], axis=1
        )
        high, low = split(pair)
        section[:, t * pencil : (t + 2) * pencil] = (
            dot(forward_ref[0], high) + dot(forward_ref[1], high) + dot(forward_ref[0], low)
        )
    lax.fori_loop(0, rows // step, filter_spectrum, 0)
    for copy in queries:
        copy.start()

    def place_of(index, count):
        inner = lax.rem(index, tile)
        place = n * inner
        for s in range(n):
            place = place + jnp.where(index // tile == s, order_ref[s * rows], 0)
        return place

    key_place = place_of(lax.broadcasted_iota(jnp.int32, (8, wide_tile), 1), wide_tile)[:1]
    query_place = place_of(lax.broadcasted_iota(jnp.int32, (wide_tile, 128), 0), wide_tile)[:, :1]
    bias[...] = jnp.where(key_place <= query_place, 0.0, -1e30)

    for copy in products:
        copy.wait()

    for copy in keys:
        copy.start()

    def stand_up(source):
        for s in range(n):
            upright[s * rows : (s + 1) * rows, :] = source[s].astype(jnp.float32).T

    stand_up(product_in)
    for t in range(0, n, 2):
        pair = [upright[pl.ds(t + u, rows, stride=n), :] for u in range(2)]
        signal[t] = pair[0]
        signal[t + 1] = pair[1]
        exact = jnp.concatenate(pair, axis=1).astype(jnp.bfloat16)
        section[:, t * pencil : (t + 2) * pencil] = dot(forward_ref[0], exact) + dot(
            forward_ref[1], exact
        )
    lax.fori_loop(0, rows // step, signal_spectrum, 0)
    for t in range(0, n, 2):
        lanes = slice(t * pencil, (t + 2) * pencil)
        high, low = back[0, :, lanes], back[1, :, lanes]
        pair = dot(inverse_ref[0], high) + dot(inverse_ref[1], high) + dot(inverse_ref[0], low)
        for u in range(2):
            convolved[t + u] = (
                pair[:, u * pencil : (u + 1) * pencil] + skip_ref[...] * signal[t + u]
            )

    for copy in gates:
        copy.wait()
    stand_up(gate_in)
    for t in range(n):
        gated[t] = (upright[pl.ds(t, rows, stride=n), :] * convolved[t]).astype(jnp.bfloat16)

    banded = exchange(BANDED, lambda d: gated_out.at[d], block(banded_ref, me))
    ones = jnp.ones((8, pencil), jnp.float32)
    for offset in list(range(1, n)) + [0]:
        to = peer(offset)
        mine = gated[order_ref[to * rows]].astype(jnp.float32)
        gated_out[to] = mine.T.astype(jnp.bfloat16)
    for s in range(n):
        mine = gated[order_ref[s * rows]].astype(jnp.float32)
        values[s] = mine.astype(jnp.bfloat16)
        squares[s : s + 1, :] = lax.dot_general(
            ones,
            mine * mine,
            TRANSPOSED,
            precision=lax.Precision.HIGHEST,
            preferred_element_type=jnp.float32,
        )[:1]
    across = [
        pltpu.make_async_remote_copy(
            src_ref=squares,
            dst_ref=squares_chan.at[offset],
            send_sem=chan_send.at[offset],
            recv_sem=chan_recv.at[offset],
            device_id={"chan": lax.rem(my_chan + offset, chans)},
            device_id_type=MESH,
        )
        for offset in range(1, chans)
    ]
    for copy in across:
        copy.start()
    for copy in across:
        copy.wait()
    squares_sum[...] = functools.reduce(
        jnp.add, [squares[...]] + [squares_chan[offset] for offset in range(1, chans)]
    )
    along = exchange(SQUARES, lambda d: squares_sum, squares_seq.at[me])
    for copy in along:
        copy.start()
    squares_seq[me] = squares_sum[...]
    for copy in along:
        copy.wait()
    inverse_rms = lax.rsqrt(
        functools.reduce(jnp.add, [squares_seq[s] for s in range(n)]) / D + 1e-05
    )
    gain = gain_ref[pl.ds(me, 1), :]
    for s in range(n):
        scale = jnp.broadcast_to(inverse_rms[s : s + 1, :], (pencil, rows)).T
        values[s] = (values[s].astype(jnp.float32) * scale * gain).astype(jnp.bfloat16)

    for copy in keys:
        copy.wait_send()
    for copy in banded:
        copy.start()
    block(banded_ref, me)[...] = gated_out[me]
    for copy in queries:
        copy.wait()
    for copy in keys:
        copy.wait_recv()

    factor = math.log2(math.e) / math.sqrt(HEAD_DIM)
    half = n // 2
    height = half * tile
    attended = exchange(ATTENDED, lambda d: result.at[d], column(attended_ref, me))

    def attend_half(turn, unused):
        h = lax.rem(1 - me // half + turn, 2)
        first = pl.multiple_of(h * half, half)
        for jt in range(TILES):
            query = q_in[pl.ds(first, half), jt * tile : (jt + 1) * tile, :]
            query = query.reshape(height, pencil)
            scores = []
            for kt in range(jt + 1):
                key = k_in[:, kt * tile : (kt + 1) * tile, :].reshape(wide_tile, pencil)
                score = lax.dot_general(
                    query, key, TRANSPOSED, preferred_element_type=jnp.float32
                )
                if kt == jt:
                    score = score + bias[pl.ds(pl.multiple_of(h * height, height), height), :]
                scores.append(score)
            top = functools.reduce(jnp.maximum, [jnp.max(s, axis=1, keepdims=True) for s in scores])
            total = jnp.zeros((height, 1), jnp.float32)
            summed = jnp.zeros((height, pencil), jnp.float32)
            for kt, score in enumerate(scores):
                weight = jnp.exp2((score - top) * factor)
                total = total + jnp.sum(weight, axis=1, keepdims=True)
                value = values[:, kt * tile : (kt + 1) * tile, :].reshape(wide_tile, pencil)
                summed = summed + dot(weight.astype(jnp.bfloat16), value)
            part = (summed / total).astype(jnp.bfloat16)
            result[pl.ds(first, half), jt * tile : (jt + 1) * tile, :] = part.reshape(
                half, tile, pencil
            )
        for offset in range(1, n):

            @pl.when(peer(offset) // half == h)
            def send():
                attended[offset - 1].start()

        return unused

    lax.fori_loop(0, 2, attend_half, 0)
    column(attended_ref, me)[...] = result[me]
    for copy in banded + attended:
        copy.wait()


def settle_kernel(banded_ref, attended_ref, banded_out, attended_out):
    banded_out[...] = banded_ref[...]
    attended_out[...] = attended_ref[...]


def settled(*arrays):
    specs = [
        pl.BlockSpec((a.shape[0] // 4, a.shape[1]), lambda index: (index, 0)) for a in arrays
    ]
    return pl.pallas_call(
        settle_kernel,
        out_shape=tuple(jax.ShapeDtypeStruct(a.shape, a.dtype) for a in arrays),
        grid=(4,),
        in_specs=specs,
        out_specs=specs,
    )(*arrays)


def fused(
    hyena_query,
    hyena_key,
    hyena_value,
    long_filter,
    skip_weight,
    stripe_order,
    query_rows,
    key_rows,
    norm_gain,
):
    n = lax.axis_size("seq")
    chans = lax.axis_size("chan")
    channels, rows = hyena_query.shape
    pencil = long_filter.shape[0]
    forward_table, inverse_table, turns = odd_tables(n, rows)
    vmem = pl.BlockSpec(memory_space=pltpu.VMEM)
    anywhere = pl.BlockSpec(memory_space=pl.ANY)
    bf16, f32 = jnp.bfloat16, jnp.float32
    wide = n * pencil
    tile = rows // TILES
    outputs = pl.pallas_call(
        functools.partial(fused_kernel, n, chans),
        out_shape=(
            jax.ShapeDtypeStruct((channels, rows), bf16),
            jax.ShapeDtypeStruct((rows, channels), bf16),
        ),
        in_specs=[pl.BlockSpec(memory_space=pltpu.SMEM)] + [vmem] * 4 + [anywhere] * 7,
        out_specs=(vmem, vmem),
        scratch_shapes=[
            pltpu.VMEM((channels, rows), bf16),
            pltpu.VMEM((rows, channels), bf16),
            pltpu.VMEM((rows, channels), bf16),
            pltpu.VMEM((n, pencil, rows), bf16),
            pltpu.VMEM((n, pencil, rows), bf16),
            pltpu.VMEM((n, pencil, rows), bf16),
            pltpu.VMEM((n, rows, pencil), bf16),
            pltpu.VMEM((n, rows, pencil), bf16),
            pltpu.VMEM(long_filter.shape, f32),
            pltpu.VMEM(forward_table.shape, bf16),
            pltpu.VMEM(inverse_table.shape, bf16),
            pltpu.VMEM(turns.shape, f32),
            pltpu.VMEM((n * rows, pencil), f32),
            pltpu.VMEM((n, rows, pencil), f32),
            pltpu.VMEM((2 * rows, wide), f32),
            pltpu.VMEM((2, rows, wide), f32),
            pltpu.VMEM((2, 2 * rows, wide), bf16),
            pltpu.VMEM((n, rows, pencil), f32),
            pltpu.VMEM((n, rows, pencil), bf16),
            pltpu.VMEM((n, pencil, rows), bf16),
            pltpu.VMEM((n, rows, pencil), bf16),
            pltpu.VMEM((n, rows, pencil), bf16),
            pltpu.VMEM((n, rows), f32),
            pltpu.VMEM((chans, n, rows), f32),
            pltpu.VMEM((n, rows), f32),
            pltpu.VMEM((n, n, rows), f32),
            pltpu.VMEM((n * tile, n * tile), f32),
            pltpu.SemaphoreType.DMA((7, n)),
            pltpu.SemaphoreType.DMA((7, n)),
            pltpu.SemaphoreType.DMA((chans,)),
            pltpu.SemaphoreType.DMA((chans,)),
            pltpu.SemaphoreType.DMA((7,)),
        ],
        compiler_params=pltpu.CompilerParams(
            collective_id=0, has_side_effects=True, vmem_limit_bytes=56 * 1024 * 1024
        ),
    )(
        stripe_order,
        hyena_key,
        hyena_value,
        skip_weight.reshape(1, pencil),
        norm_gain.reshape(n, pencil),
        hyena_query,
        long_filter,
        query_rows,
        key_rows,
        jnp.asarray(forward_table),
        jnp.asarray(inverse_table),
        jnp.asarray(turns),
    )
    return settled(*outputs)


def passed_along(block, axis, distance):
    devices = range(lax.axis_size(axis))
    route = [((i - distance) % len(devices), i) for i in devices]
    return lax.ppermute(block, axis, route)


def angle_table(first, second, modulus):
    left = jnp.arange(first, dtype=jnp.int32)[:, None]
    right = jnp.arange(second, dtype=jnp.int32)[None, :]
    theta = 2.0 * math.pi / modulus * (left * right % modulus).astype(jnp.float32)
    return (jnp.cos(theta), jnp.sin(theta))


def transform_tables(length):
    outer = 2 * length // 128
    first_cos, first_sin = angle_table(outer, outer // 2, outer)
    twist_cos, twist_sin = angle_table(outer, 128, 2 * length)
    inner_cos, inner_sin = angle_table(128, 128, 128)
    return (first_cos, first_sin, twist_cos, twist_sin, inner_cos, inner_sin)


def contract(form, left, right):
    return jnp.einsum(form, left, right, precision=lax.Precision.HIGHEST)


def forward(signal, tables):
    first_cos, first_sin, twist_cos, twist_sin, inner_cos, inner_sin = tables
    section_real = contract("kt,cts->cks", first_cos, signal)
    section_imag = -contract("kt,cts->cks", first_sin, signal)
    turned_real = section_real * twist_cos + section_imag * twist_sin
    turned_imag = section_imag * twist_cos - section_real * twist_sin
    out_real = contract("cks,sm->ckm", turned_real, inner_cos) + contract(
        "cks,sm->ckm", turned_imag, inner_sin
    )
    out_imag = contract("cks,sm->ckm", turned_imag, inner_cos) - contract(
        "cks,sm->ckm", turned_real, inner_sin
    )
    return (out_real, out_imag)


def inverse(spectrum_real, spectrum_imag, tables):
    first_cos, first_sin, twist_cos, twist_sin, inner_cos, inner_sin = tables
    back_real = contract("ckm,sm->cks", spectrum_real, inner_cos) - contract(
        "ckm,sm->cks", spectrum_imag, inner_sin
    )
    back_imag = contract("ckm,sm->cks", spectrum_real, inner_sin) + contract(
        "ckm,sm->cks", spectrum_imag, inner_cos
    )
    turned_real = back_real * twist_cos - back_imag * twist_sin
    turned_imag = back_real * twist_sin + back_imag * twist_cos
    signal = contract("kt,cks->cts", first_cos, turned_real) - contract(
        "kt,cks->cts", first_sin, turned_imag
    )
    return signal * (1.0 / (first_cos.shape[0] * 128))


def convolve(signal, filter_parts, tables):
    pencil, length = signal.shape
    widened = signal.astype(jnp.float32).reshape(pencil, length // 128, 128)
    signal_real, signal_imag = forward(widened, tables)
    filter_real, filter_imag = filter_parts
    product_real = signal_real * filter_real - signal_imag * filter_imag
    product_imag = signal_real * filter_imag + signal_imag * filter_real
    return inverse(product_real, product_imag, tables).reshape(pencil, length)


def fold_keys(carry, queries, own_places, key_piece, value_piece, places, scale):
    count = key_piece.shape[0]
    heads = queries.shape[1]
    depth = queries.shape[2]
    block = math.gcd(count, 512)
    place_blocks = places.reshape(count // block, block)
    key_blocks = key_piece.reshape(count // block, block, heads, depth)
    value_blocks = value_piece.reshape(count // block, block, heads, depth)

    def one_block(state, inputs):
        running, totals, sums = state
        key_block, value_block, key_places = inputs
        scores = (
            jnp.einsum("qhd,khd->hqk", queries, key_block, preferred_element_type=jnp.float32)
            * scale
        )
        allowed = key_places[None, None, :] <= own_places[None, :, None]
        scores = jnp.where(allowed, scores, -1e30)
        highest = jnp.maximum(running, jnp.max(scores, axis=2))
        weights = jnp.where(allowed, jnp.exp(scores - highest[:, :, None]), 0.0)
        factor = jnp.exp(running - highest)
        totals = totals * factor + jnp.sum(weights, axis=2)
        update = jnp.einsum(
            "hqk,khd->hqd",
            weights.astype(jnp.bfloat16),
            value_block,
            preferred_element_type=jnp.float32,
        )
        sums = sums * factor[:, :, None] + update
        return ((highest, totals, sums), None)

    carry, unused = lax.scan(one_block, carry, (key_blocks, value_blocks, place_blocks))
    return carry


def general(
    hyena_query,
    hyena_key,
    hyena_value,
    long_filter,
    skip_weight,
    stripe_order,
    query_rows,
    key_rows,
    norm_gain,
):
    stripes = lax.axis_size("seq")
    channels, rows = hyena_query.shape
    pencil, length = long_filter.shape
    sigma = stripe_order.reshape(stripes, rows)[:, 0]
    product = (hyena_key.astype(jnp.float32) * hyena_value.astype(jnp.float32)).astype(jnp.bfloat16)
    tables = transform_tables(length)
    filter_parts = forward(long_filter.reshape(pencil, length // 128, 128), tables)
    spread = lax.all_to_all(product, "seq", split_axis=0, concat_axis=1, tiled=True)
    summed = convolve(spread, filter_parts, tables) + skip_weight[:, None] * spread.astype(
        jnp.float32
    )
    returned = lax.all_to_all(
        summed.astype(jnp.bfloat16), "seq", split_axis=1, concat_axis=0, tiled=True
    ).astype(summed.dtype)
    gated = (hyena_query.astype(jnp.float32) * returned).astype(jnp.bfloat16)
    per_stripe = rows // stripes
    columns = stripes * jnp.arange(per_stripe, dtype=jnp.int32)[None, :] + sigma[:, None]
    arranged = jnp.take(gated, columns.reshape(rows), axis=1).reshape(channels, stripes, per_stripe)
    banded = lax.all_to_all(arranged, "seq", split_axis=1, concat_axis=2, tiled=True).reshape(
        channels, rows
    )
    output_wide = banded.astype(jnp.float32)
    squares = lax.psum(jnp.sum(output_wide * output_wide, axis=0), "chan")
    inverse_rms = lax.rsqrt(squares / D + 1e-05)
    normed = (output_wide * inverse_rms[None, :] * norm_gain[:, None]).astype(jnp.bfloat16)
    value_rows = normed.T
    local_heads = channels // HEAD_DIM
    scale = 1.0 / math.sqrt(HEAD_DIM)
    seq_index = lax.axis_index("seq")
    own_head = seq_index % local_heads
    group_index = seq_index // local_heads
    group_count = stripes // local_heads
    span = local_heads * rows
    stacked_local = jnp.stack((query_rows, key_rows, value_rows)).reshape(
        3, rows, local_heads, HEAD_DIM
    )
    collected = [lax.dynamic_index_in_dim(stacked_local, own_head, 2, keepdims=False)]
    for offset in range(1, local_heads):
        payload = lax.dynamic_index_in_dim(
            stacked_local, (own_head + offset) % local_heads, 2, keepdims=False
        )
        from_below = passed_along(payload, "seq", offset)
        from_above = passed_along(payload, "seq", offset - local_heads)
        collected.append(jnp.where(own_head >= offset, from_below, from_above))
    ordering = (own_head - jnp.arange(local_heads, dtype=jnp.int32)) % local_heads
    sources = jnp.take(jnp.stack(collected), ordering, axis=0)
    combined = sources.transpose(1, 0, 2, 3).reshape(3, span, HEAD_DIM)
    group_places = lax.dynamic_slice_in_dim(stripe_order, group_index * span, span)
    group_queries = combined[0].reshape(span, 1, HEAD_DIM)

    def visit(state, kv_pair, source):
        places = lax.dynamic_slice_in_dim(stripe_order, source * span, span)
        return fold_keys(
            state,
            group_queries,
            group_places,
            kv_pair[0].reshape(span, 1, HEAD_DIM),
            kv_pair[1].reshape(span, 1, HEAD_DIM),
            places,
            scale,
        )

    initial_group = (
        jnp.full((1, span), -1e30, jnp.float32),
        jnp.zeros((1, span), jnp.float32),
        jnp.zeros((1, span, HEAD_DIM), jnp.float32),
    )

    def cycle_turn(turn, loop_state):
        state, kv_pair = loop_state
        state = visit(state, kv_pair, (group_index - turn) % group_count)
        kv_pair = passed_along(kv_pair, "seq", local_heads)
        return (state, kv_pair)

    state, kv_pair = lax.fori_loop(0, group_count - 1, cycle_turn, (initial_group, combined[1:]))
    running, totals, sums = visit(state, kv_pair, (group_index - (group_count - 1)) % group_count)
    result = (sums[0] / totals[0][:, None]).astype(jnp.bfloat16)
    pieces = result.reshape(local_heads, rows, HEAD_DIM)
    returned_heads = [lax.dynamic_index_in_dim(pieces, own_head, 0, keepdims=False)]
    for offset in range(1, local_heads):
        payload = lax.dynamic_index_in_dim(
            pieces, (own_head + offset) % local_heads, 0, keepdims=False
        )
        back_below = passed_along(payload, "seq", offset)
        back_above = passed_along(payload, "seq", offset - local_heads)
        returned_heads.append(jnp.where(own_head >= offset, back_below, back_above))
    by_head = jnp.take(jnp.stack(returned_heads), ordering, axis=0)
    attended = by_head.transpose(1, 0, 2).reshape(rows, channels)
    return (banded, attended)


def local(*arrays):
    pencil = arrays[3].shape[0]
    rows = arrays[0].shape[1]
    stripes = lax.axis_size("seq")
    even = stripes % 2 == 0 and stripes & (stripes - 1) == 0 and 2 * stripes <= HEAD_DIM
    one_head = pencil == HEAD_DIM and even and rows % (16 * TILES) == 0
    return fused(*arrays) if one_head else general(*arrays)


def solution(mesh):
    placed = (
        P("chan", "seq"),
        P("chan", "seq"),
        P("chan", "seq"),
        P(("chan", "seq"), None),
        P(("chan", "seq")),
        P(),
        P("seq", "chan"),
        P("seq", "chan"),
        P("chan"),
    )
    return jax.shard_map(
        local,
        mesh=mesh,
        in_specs=placed,
        out_specs=(P("chan", "seq"), P("seq", "chan")),
        check_vma=False,
    )
```

```python
import functools
import math

import jax
import jax.numpy as jnp
import ml_dtypes
import numpy as np
from jax import lax
from jax.experimental import pallas as pl
from jax.experimental.pallas import tpu as pltpu
from jax.sharding import PartitionSpec as P

D = 4096
HEAD_DIM = 128
TILES = 4
MESH = pl.DeviceIdType.MESH
PRODUCT, QUERIES, KEYS, GATES, BANDED, ATTENDED, SQUARES = range(7)
TRANSPOSED = (((1,), (1,)), ((), ()))


def high_low(table):
    high = table.astype(ml_dtypes.bfloat16)
    low = (table - high.astype(np.float64)).astype(ml_dtypes.bfloat16)
    return np.stack((high, low))


def odd_tables(stripes, rows):
    frequency = np.arange(rows, dtype=np.float64) + 0.5
    angle = 2.0 * np.pi * frequency[:, None] * np.arange(rows)[None, :] / (2 * rows)
    dense = np.concatenate((np.cos(angle), -np.sin(angle)), axis=0)
    twist = 2.0 * np.pi * frequency[:, None] * np.arange(stripes)[None, :] / (2 * rows * stripes)
    turns = np.zeros((rows, 128), np.float32)
    turns[:, :stripes] = np.cos(twist)
    turns[:, stripes : 2 * stripes] = np.sin(twist)
    return high_low(dense), high_low(dense.T), turns


def small_dft(parts, sign):
    count = len(parts)
    if count == 1:
        return parts
    even = small_dft(parts[0::2], sign)
    odd = small_dft(parts[1::2], sign)
    first, second = [], []
    for k in range(count // 2):
        real, imag = odd[k]
        cos = math.cos(2.0 * math.pi * k / count)
        sin = sign * math.sin(2.0 * math.pi * k / count)
        if k == 0:
            turned = (real, imag)
        elif 4 * k == count:
            turned = (-sign * imag, sign * real)
        else:
            turned = (real * cos - imag * sin, real * sin + imag * cos)
        first.append((even[k][0] + turned[0], even[k][1] + turned[1]))
        second.append((even[k][0] - turned[0], even[k][1] - turned[1]))
    return first + second


def dot(left, right):
    return jnp.dot(left, right, preferred_element_type=jnp.float32)


def split(wide):
    high = wide.astype(jnp.bfloat16)
    return high, (wide - high.astype(jnp.float32)).astype(jnp.bfloat16)


def fused_kernel(
    n,
    chans,
    order_ref,
    skip_ref,
    gain_ref,
    hk_hbm,
    hv_hbm,
    hq_hbm,
    filter_hbm,
    q_hbm,
    k_hbm,
    forward_hbm,
    inverse_hbm,
    turns_hbm,
    banded_ref,
    attended_ref,
    hk_ref,
    hv_ref,
    gate_all,
    q_all,
    k_all,
    product_out,
    product_in,
    gate_in,
    q_in,
    k_in,
    filter_ref,
    forward_ref,
    inverse_ref,
    turns_ref,
    upright,
    signal,
    section,
    spectrum,
    back,
    convolved,
    gated,
    gated_out,
    values,
    result,
    squares,
    squares_chan,
    squares_sum,
    squares_seq,
    bias,
    send_sem,
    recv_sem,
    chan_send,
    chan_recv,
    local_sem,
):
    me = lax.axis_index("seq")
    my_chan = lax.axis_index("chan")
    pencil, rows = product_in.shape[1:]
    tile = rows // TILES
    wide_tile = n * tile

    def peer(offset):
        return lax.rem(me + offset, n)

    def block(ref, index):
        return ref.at[pl.ds(pl.multiple_of(index * pencil, pencil), pencil), :]

    def column(ref, index):
        return ref.at[:, pl.ds(pl.multiple_of(index * pencil, pencil), pencil)]

    def exchange(kind, source, target):
        return [
            pltpu.make_async_remote_copy(
                src_ref=source(peer(offset)),
                dst_ref=target,
                send_sem=send_sem.at[kind, offset],
                recv_sem=recv_sem.at[kind, offset],
                device_id={"seq": peer(offset)},
                device_id_type=MESH,
            )
            for offset in range(1, n)
        ]

    barrier = pltpu.get_barrier_semaphore()
    for offset in range(1, n):
        pl.semaphore_signal(barrier, inc=1, device_id={"seq": peer(offset)}, device_id_type=MESH)
    for offset in range(1, chans):
        other = lax.rem(my_chan + offset, chans)
        pl.semaphore_signal(barrier, inc=1, device_id={"chan": other}, device_id_type=MESH)

    staged = [
        (hk_hbm, hk_ref),
        (hv_hbm, hv_ref),
        (hq_hbm, gate_all),
        (filter_hbm, filter_ref),
        (forward_hbm, forward_ref),
        (inverse_hbm, inverse_ref),
        (turns_hbm, turns_ref),
        (q_hbm, q_all),
        (k_hbm, k_all),
    ]
    staged = [
        pltpu.make_async_copy(source, target, local_sem.at[index])
        for index, (source, target) in enumerate(staged)
    ]
    for copy in staged:
        copy.start()

    products = exchange(PRODUCT, lambda d: product_out.at[d], product_in.at[me])
    queries = exchange(QUERIES, lambda d: column(q_all, d), q_in.at[me])
    keys = exchange(KEYS, lambda d: column(k_all, d), k_in.at[me])
    gates = exchange(GATES, lambda d: block(gate_all, d), gate_in.at[me])

    def product_of(index):
        return (
            block(hk_ref, index)[...].astype(jnp.float32)
            * block(hv_ref, index)[...].astype(jnp.float32)
        ).astype(jnp.bfloat16)

    staged[2].wait()
    pl.semaphore_wait(barrier, n - 1 + chans - 1)
    for copy in gates:
        copy.start()
    for copy in staged[:2]:
        copy.wait()
    for offset in range(1, n):
        product_out[peer(offset)] = product_of(peer(offset))
        products[offset - 1].start()
    product_in[me] = product_of(me)
    gate_in[me] = block(gate_all, me)[...]

    for copy in staged[3:]:
        copy.wait()
    q_in[me] = column(q_all, me)[...]
    k_in[me] = column(k_all, me)[...]

    def turned_sections(part):
        cos = turns_ref[part, :]
        parts = []
        for t in range(n):
            real = section[part, t * pencil : (t + 1) * pencil]
            below = pl.ds(pl.multiple_of(rows + part.start, part.size), part.size)
            imag = section[below, t * pencil : (t + 1) * pencil]
            c, s = cos[:, t : t + 1], cos[:, n + t : n + t + 1]
            parts.append((real * c + imag * s, imag * c - real * s))
        return small_dft(parts, -1.0)

    step = 16

    def filter_spectrum(index, unused):
        part = pl.ds(pl.multiple_of(index * step, step), step)
        scale = 1.0 / (rows * n)
        for k, (real, imag) in enumerate(turned_sections(part)):
            spectrum[0, part, k * pencil : (k + 1) * pencil] = real * scale
            spectrum[1, part, k * pencil : (k + 1) * pencil] = imag * scale
        return unused

    def signal_spectrum(index, unused):
        part = pl.ds(pl.multiple_of(index * step, step), step)
        below = pl.ds(pl.multiple_of(rows + index * step, step), step)
        parts = []
        for k, (real, imag) in enumerate(turned_sections(part)):
            other_real = spectrum[0, part, k * pencil : (k + 1) * pencil]
            other_imag = spectrum[1, part, k * pencil : (k + 1) * pencil]
            parts.append(
                (real * other_real - imag * other_imag, real * other_imag + imag * other_real)
            )
        cos = turns_ref[part, :]
        for t, (real, imag) in enumerate(small_dft(parts, 1.0)):
            c, s = cos[:, t : t + 1], cos[:, n + t : n + t + 1]
            lanes = slice(t * pencil, (t + 1) * pencil)
            for place, value in ((part, real * c - imag * s), (below, real * s + imag * c)):
                high, low = split(value)
                back[0, place, lanes] = high
                back[1, place, lanes] = low
        return unused

    for s in range(n):
        upright[s * rows : (s + 1) * rows, :] = filter_ref[:, s * rows : (s + 1) * rows].T
    for t in range(0, n, 2):
        pair = jnp.concatenate(
            [upright[pl.ds(t + u, rows, stride=n), :] for u in range(2)], axis=1
        )
        high, low = split(pair)
        section[:, t * pencil : (t + 2) * pencil] = (
            dot(forward_ref[0], high) + dot(forward_ref[1], high) + dot(forward_ref[0], low)
        )
    lax.fori_loop(0, rows // step, filter_spectrum, 0)
    for copy in queries:
        copy.start()

    def place_of(index, count):
        inner = lax.rem(index, tile)
        place = n * inner
        for s in range(n):
            place = place + jnp.where(index // tile == s, order_ref[s * rows], 0)
        return place

    key_place = place_of(lax.broadcasted_iota(jnp.int32, (8, wide_tile), 1), wide_tile)[:1]
    query_place = place_of(lax.broadcasted_iota(jnp.int32, (wide_tile, 128), 0), wide_tile)[:, :1]
    bias[...] = jnp.where(key_place <= query_place, 0.0, -1e30)

    for copy in products:
        copy.wait()

    for copy in keys:
        copy.start()

    def stand_up(source):
        for s in range(n):
            upright[s * rows : (s + 1) * rows, :] = source[s].astype(jnp.float32).T

    stand_up(product_in)
    for t in range(0, n, 2):
        pair = [upright[pl.ds(t + u, rows, stride=n), :] for u in range(2)]
        signal[t] = pair[0]
        signal[t + 1] = pair[1]
        exact = jnp.concatenate(pair, axis=1).astype(jnp.bfloat16)
        section[:, t * pencil : (t + 2) * pencil] = dot(forward_ref[0], exact) + dot(
            forward_ref[1], exact
        )
    lax.fori_loop(0, rows // step, signal_spectrum, 0)
    for t in range(0, n, 2):
        lanes = slice(t * pencil, (t + 2) * pencil)
        high, low = back[0, :, lanes], back[1, :, lanes]
        pair = dot(inverse_ref[0], high) + dot(inverse_ref[1], high) + dot(inverse_ref[0], low)
        for u in range(2):
            convolved[t + u] = (
                pair[:, u * pencil : (u + 1) * pencil] + skip_ref[...] * signal[t + u]
            )

    for copy in gates:
        copy.wait()
    stand_up(gate_in)
    for t in range(n):
        gated[t] = (upright[pl.ds(t, rows, stride=n), :] * convolved[t]).astype(jnp.bfloat16)

    banded = exchange(BANDED, lambda d: gated_out.at[d], block(banded_ref, me))
    ones = jnp.ones((8, pencil), jnp.float32)
    for offset in list(range(1, n)) + [0]:
        to = peer(offset)
        mine = gated[order_ref[to * rows]].astype(jnp.float32)
        gated_out[to] = mine.T.astype(jnp.bfloat16)
    for s in range(n):
        mine = gated[order_ref[s * rows]].astype(jnp.float32)
        values[s] = mine.astype(jnp.bfloat16)
        squares[s : s + 1, :] = lax.dot_general(
            ones,
            mine * mine,
            TRANSPOSED,
            precision=lax.Precision.HIGHEST,
            preferred_element_type=jnp.float32,
        )[:1]
    across = [
        pltpu.make_async_remote_copy(
            src_ref=squares,
            dst_ref=squares_chan.at[offset],
            send_sem=chan_send.at[offset],
            recv_sem=chan_recv.at[offset],
            device_id={"chan": lax.rem(my_chan + offset, chans)},
            device_id_type=MESH,
        )
        for offset in range(1, chans)
    ]
    for copy in across:
        copy.start()
    for copy in across:
        copy.wait()
    squares_sum[...] = functools.reduce(
        jnp.add, [squares[...]] + [squares_chan[offset] for offset in range(1, chans)]
    )
    along = exchange(SQUARES, lambda d: squares_sum, squares_seq.at[me])
    for copy in along:
        copy.start()
    squares_seq[me] = squares_sum[...]
    for copy in along:
        copy.wait()
    inverse_rms = lax.rsqrt(
        functools.reduce(jnp.add, [squares_seq[s] for s in range(n)]) / D + 1e-05
    )
    gain = gain_ref[pl.ds(me, 1), :]
    for s in range(n):
        scale = jnp.broadcast_to(inverse_rms[s : s + 1, :], (pencil, rows)).T
        values[s] = (values[s].astype(jnp.float32) * scale * gain).astype(jnp.bfloat16)

    for copy in keys:
        copy.wait_send()
    for copy in banded:
        copy.start()
    block(banded_ref, me)[...] = gated_out[me]
    for copy in queries:
        copy.wait()
    for copy in keys:
        copy.wait_recv()

    factor = math.log2(math.e) / math.sqrt(HEAD_DIM)
    half = n // 2
    height = half * tile
    attended = exchange(ATTENDED, lambda d: result.at[d], column(attended_ref, me))

    def attend_half(turn, unused):
        h = lax.rem(1 - me // half + turn, 2)
        first = pl.multiple_of(h * half, half)
        for jt in range(TILES):
            query = q_in[pl.ds(first, half), jt * tile : (jt + 1) * tile, :]
            query = query.reshape(height, pencil)
            scores = []
            for kt in range(jt + 1):
                key = k_in[:, kt * tile : (kt + 1) * tile, :].reshape(wide_tile, pencil)
                score = lax.dot_general(
                    query, key, TRANSPOSED, preferred_element_type=jnp.float32
                )
                if kt == jt:
                    score = score + bias[pl.ds(pl.multiple_of(h * height, height), height), :]
                scores.append(score)
            top = functools.reduce(jnp.maximum, [jnp.max(s, axis=1, keepdims=True) for s in scores])
            total = jnp.zeros((height, 1), jnp.float32)
            summed = jnp.zeros((height, pencil), jnp.float32)
            for kt, score in enumerate(scores):
                weight = jnp.exp2((score - top) * factor)
                total = total + jnp.sum(weight, axis=1, keepdims=True)
                value = values[:, kt * tile : (kt + 1) * tile, :].reshape(wide_tile, pencil)
                summed = summed + dot(weight.astype(jnp.bfloat16), value)
            part = (summed / total).astype(jnp.bfloat16)
            result[pl.ds(first, half), jt * tile : (jt + 1) * tile, :] = part.reshape(
                half, tile, pencil
            )
        for offset in range(1, n):

            @pl.when(peer(offset) // half == h)
            def send():
                attended[offset - 1].start()

        return unused

    lax.fori_loop(0, 2, attend_half, 0)
    column(attended_ref, me)[...] = result[me]
    for copy in banded + attended:
        copy.wait()


def fused(
    hyena_query,
    hyena_key,
    hyena_value,
    long_filter,
    skip_weight,
    stripe_order,
    query_rows,
    key_rows,
    norm_gain,
):
    n = lax.axis_size("seq")
    chans = lax.axis_size("chan")
    channels, rows = hyena_query.shape
    pencil = long_filter.shape[0]
    forward_table, inverse_table, turns = odd_tables(n, rows)
    vmem = pl.BlockSpec(memory_space=pltpu.VMEM)
    far = pl.BlockSpec(memory_space=pl.ANY)
    bf16, f32 = jnp.bfloat16, jnp.float32
    wide = n * pencil
    tile = rows // TILES
    return pl.pallas_call(
        functools.partial(fused_kernel, n, chans),
        out_shape=(
            jax.ShapeDtypeStruct((channels, rows), bf16),
            jax.ShapeDtypeStruct((rows, channels), bf16),
        ),
        in_specs=[pl.BlockSpec(memory_space=pltpu.SMEM)] + [vmem] * 2 + [far] * 9,
        out_specs=(vmem, vmem),
        scratch_shapes=[
            pltpu.VMEM((channels, rows), bf16),
            pltpu.VMEM((channels, rows), bf16),
            pltpu.VMEM((channels, rows), bf16),
            pltpu.VMEM((rows, channels), bf16),
            pltpu.VMEM((rows, channels), bf16),
            pltpu.VMEM((n, pencil, rows), bf16),
            pltpu.VMEM((n, pencil, rows), bf16),
            pltpu.VMEM((n, pencil, rows), bf16),
            pltpu.VMEM((n, rows, pencil), bf16),
            pltpu.VMEM((n, rows, pencil), bf16),
            pltpu.VMEM(long_filter.shape, f32),
            pltpu.VMEM(forward_table.shape, bf16),
            pltpu.VMEM(inverse_table.shape, bf16),
            pltpu.VMEM(turns.shape, f32),
            pltpu.VMEM((n * rows, pencil), f32),
            pltpu.VMEM((n, rows, pencil), f32),
            pltpu.VMEM((2 * rows, wide), f32),
            pltpu.VMEM((2, rows, wide), f32),
            pltpu.VMEM((2, 2 * rows, wide), bf16),
            pltpu.VMEM((n, rows, pencil), f32),
            pltpu.VMEM((n, rows, pencil), bf16),
            pltpu.VMEM((n, pencil, rows), bf16),
            pltpu.VMEM((n, rows, pencil), bf16),
            pltpu.VMEM((n, rows, pencil), bf16),
            pltpu.VMEM((n, rows), f32),
            pltpu.VMEM((chans, n, rows), f32),
            pltpu.VMEM((n, rows), f32),
            pltpu.VMEM((n, n, rows), f32),
            pltpu.VMEM((n * tile, n * tile), f32),
            pltpu.SemaphoreType.DMA((7, n)),
            pltpu.SemaphoreType.DMA((7, n)),
            pltpu.SemaphoreType.DMA((chans,)),
            pltpu.SemaphoreType.DMA((chans,)),
            pltpu.SemaphoreType.DMA((9,)),
        ],
        compiler_params=pltpu.CompilerParams(
            collective_id=0, has_side_effects=True, vmem_limit_bytes=36 * 1024 * 1024
        ),
    )(
        stripe_order,
        skip_weight.reshape(1, pencil),
        norm_gain.reshape(n, pencil),
        hyena_key,
        hyena_value,
        hyena_query,
        long_filter,
        query_rows,
        key_rows,
        jnp.asarray(forward_table),
        jnp.asarray(inverse_table),
        jnp.asarray(turns),
    )


def passed_along(block, axis, distance):
    devices = range(lax.axis_size(axis))
    route = [((i - distance) % len(devices), i) for i in devices]
    return lax.ppermute(block, axis, route)


def angle_table(first, second, modulus):
    left = jnp.arange(first, dtype=jnp.int32)[:, None]
    right = jnp.arange(second, dtype=jnp.int32)[None, :]
    theta = 2.0 * math.pi / modulus * (left * right % modulus).astype(jnp.float32)
    return (jnp.cos(theta), jnp.sin(theta))


def transform_tables(length):
    outer = 2 * length // 128
    first_cos, first_sin = angle_table(outer, outer // 2, outer)
    twist_cos, twist_sin = angle_table(outer, 128, 2 * length)
    inner_cos, inner_sin = angle_table(128, 128, 128)
    return (first_cos, first_sin, twist_cos, twist_sin, inner_cos, inner_sin)


def contract(form, left, right):
    return jnp.einsum(form, left, right, precision=lax.Precision.HIGHEST)


def forward(signal, tables):
    first_cos, first_sin, twist_cos, twist_sin, inner_cos, inner_sin = tables
    section_real = contract("kt,cts->cks", first_cos, signal)
    section_imag = -contract("kt,cts->cks", first_sin, signal)
    turned_real = section_real * twist_cos + section_imag * twist_sin
    turned_imag = section_imag * twist_cos - section_real * twist_sin
    out_real = contract("cks,sm->ckm", turned_real, inner_cos) + contract(
        "cks,sm->ckm", turned_imag, inner_sin
    )
    out_imag = contract("cks,sm->ckm", turned_imag, inner_cos) - contract(
        "cks,sm->ckm", turned_real, inner_sin
    )
    return (out_real, out_imag)


def inverse(spectrum_real, spectrum_imag, tables):
    first_cos, first_sin, twist_cos, twist_sin, inner_cos, inner_sin = tables
    back_real = contract("ckm,sm->cks", spectrum_real, inner_cos) - contract(
        "ckm,sm->cks", spectrum_imag, inner_sin
    )
    back_imag = contract("ckm,sm->cks", spectrum_real, inner_sin) + contract(
        "ckm,sm->cks", spectrum_imag, inner_cos
    )
    turned_real = back_real * twist_cos - back_imag * twist_sin
    turned_imag = back_real * twist_sin + back_imag * twist_cos
    signal = contract("kt,cks->cts", first_cos, turned_real) - contract(
        "kt,cks->cts", first_sin, turned_imag
    )
    return signal * (1.0 / (first_cos.shape[0] * 128))


def convolve(signal, filter_parts, tables):
    pencil, length = signal.shape
    widened = signal.astype(jnp.float32).reshape(pencil, length // 128, 128)
    signal_real, signal_imag = forward(widened, tables)
    filter_real, filter_imag = filter_parts
    product_real = signal_real * filter_real - signal_imag * filter_imag
    product_imag = signal_real * filter_imag + signal_imag * filter_real
    return inverse(product_real, product_imag, tables).reshape(pencil, length)


def fold_keys(carry, queries, own_places, key_piece, value_piece, places, scale):
    count = key_piece.shape[0]
    heads = queries.shape[1]
    depth = queries.shape[2]
    block = math.gcd(count, 512)
    place_blocks = places.reshape(count // block, block)
    key_blocks = key_piece.reshape(count // block, block, heads, depth)
    value_blocks = value_piece.reshape(count // block, block, heads, depth)

    def one_block(state, inputs):
        running, totals, sums = state
        key_block, value_block, key_places = inputs
        scores = (
            jnp.einsum("qhd,khd->hqk", queries, key_block, preferred_element_type=jnp.float32)
            * scale
        )
        allowed = key_places[None, None, :] <= own_places[None, :, None]
        scores = jnp.where(allowed, scores, -1e30)
        highest = jnp.maximum(running, jnp.max(scores, axis=2))
        weights = jnp.where(allowed, jnp.exp(scores - highest[:, :, None]), 0.0)
        factor = jnp.exp(running - highest)
        totals = totals * factor + jnp.sum(weights, axis=2)
        update = jnp.einsum(
            "hqk,khd->hqd",
            weights.astype(jnp.bfloat16),
            value_block,
            preferred_element_type=jnp.float32,
        )
        sums = sums * factor[:, :, None] + update
        return ((highest, totals, sums), None)

    carry, unused = lax.scan(one_block, carry, (key_blocks, value_blocks, place_blocks))
    return carry


def general(
    hyena_query,
    hyena_key,
    hyena_value,
    long_filter,
    skip_weight,
    stripe_order,
    query_rows,
    key_rows,
    norm_gain,
):
    stripes = lax.axis_size("seq")
    channels, rows = hyena_query.shape
    pencil, length = long_filter.shape
    sigma = stripe_order.reshape(stripes, rows)[:, 0]
    product = (hyena_key.astype(jnp.float32) * hyena_value.astype(jnp.float32)).astype(jnp.bfloat16)
    tables = transform_tables(length)
    filter_parts = forward(long_filter.reshape(pencil, length // 128, 128), tables)
    spread = lax.all_to_all(product, "seq", split_axis=0, concat_axis=1, tiled=True)
    summed = convolve(spread, filter_parts, tables) + skip_weight[:, None] * spread.astype(
        jnp.float32
    )
    returned = lax.all_to_all(
        summed.astype(jnp.bfloat16), "seq", split_axis=1, concat_axis=0, tiled=True
    ).astype(summed.dtype)
    gated = (hyena_query.astype(jnp.float32) * returned).astype(jnp.bfloat16)
    per_stripe = rows // stripes
    columns = stripes * jnp.arange(per_stripe, dtype=jnp.int32)[None, :] + sigma[:, None]
    arranged = jnp.take(gated, columns.reshape(rows), axis=1).reshape(channels, stripes, per_stripe)
    banded = lax.all_to_all(arranged, "seq", split_axis=1, concat_axis=2, tiled=True).reshape(
        channels, rows
    )
    output_wide = banded.astype(jnp.float32)
    squares = lax.psum(jnp.sum(output_wide * output_wide, axis=0), "chan")
    inverse_rms = lax.rsqrt(squares / D + 1e-05)
    normed = (output_wide * inverse_rms[None, :] * norm_gain[:, None]).astype(jnp.bfloat16)
    value_rows = normed.T
    local_heads = channels // HEAD_DIM
    scale = 1.0 / math.sqrt(HEAD_DIM)
    seq_index = lax.axis_index("seq")
    own_head = seq_index % local_heads
    group_index = seq_index // local_heads
    group_count = stripes // local_heads
    span = local_heads * rows
    stacked_local = jnp.stack((query_rows, key_rows, value_rows)).reshape(
        3, rows, local_heads, HEAD_DIM
    )
    collected = [lax.dynamic_index_in_dim(stacked_local, own_head, 2, keepdims=False)]
    for offset in range(1, local_heads):
        payload = lax.dynamic_index_in_dim(
            stacked_local, (own_head + offset) % local_heads, 2, keepdims=False
        )
        from_below = passed_along(payload, "seq", offset)
        from_above = passed_along(payload, "seq", offset - local_heads)
        collected.append(jnp.where(own_head >= offset, from_below, from_above))
    ordering = (own_head - jnp.arange(local_heads, dtype=jnp.int32)) % local_heads
    sources = jnp.take(jnp.stack(collected), ordering, axis=0)
    combined = sources.transpose(1, 0, 2, 3).reshape(3, span, HEAD_DIM)
    group_places = lax.dynamic_slice_in_dim(stripe_order, group_index * span, span)
    group_queries = combined[0].reshape(span, 1, HEAD_DIM)

    def visit(state, kv_pair, source):
        places = lax.dynamic_slice_in_dim(stripe_order, source * span, span)
        return fold_keys(
            state,
            group_queries,
            group_places,
            kv_pair[0].reshape(span, 1, HEAD_DIM),
            kv_pair[1].reshape(span, 1, HEAD_DIM),
            places,
            scale,
        )

    initial_group = (
        jnp.full((1, span), -1e30, jnp.float32),
        jnp.zeros((1, span), jnp.float32),
        jnp.zeros((1, span, HEAD_DIM), jnp.float32),
    )

    def cycle_turn(turn, loop_state):
        state, kv_pair = loop_state
        state = visit(state, kv_pair, (group_index - turn) % group_count)
        kv_pair = passed_along(kv_pair, "seq", local_heads)
        return (state, kv_pair)

    state, kv_pair = lax.fori_loop(0, group_count - 1, cycle_turn, (initial_group, combined[1:]))
    running, totals, sums = visit(state, kv_pair, (group_index - (group_count - 1)) % group_count)
    result = (sums[0] / totals[0][:, None]).astype(jnp.bfloat16)
    pieces = result.reshape(local_heads, rows, HEAD_DIM)
    returned_heads = [lax.dynamic_index_in_dim(pieces, own_head, 0, keepdims=False)]
    for offset in range(1, local_heads):
        payload = lax.dynamic_index_in_dim(
            pieces, (own_head + offset) % local_heads, 0, keepdims=False
        )
        back_below = passed_along(payload, "seq", offset)
        back_above = passed_along(payload, "seq", offset - local_heads)
        returned_heads.append(jnp.where(own_head >= offset, back_below, back_above))
    by_head = jnp.take(jnp.stack(returned_heads), ordering, axis=0)
    attended = by_head.transpose(1, 0, 2).reshape(rows, channels)
    return (banded, attended)


def local(*arrays):
    pencil = arrays[3].shape[0]
    rows = arrays[0].shape[1]
    stripes = lax.axis_size("seq")
    even = stripes % 2 == 0 and stripes & (stripes - 1) == 0 and 2 * stripes <= HEAD_DIM
    one_head = pencil == HEAD_DIM and even and rows % (16 * TILES) == 0
    return fused(*arrays) if one_head else general(*arrays)


def solution(mesh):
    placed = (
        P("chan", "seq"),
        P("chan", "seq"),
        P("chan", "seq"),
        P(("chan", "seq"), None),
        P(("chan", "seq")),
        P(),
        P("seq", "chan"),
        P("seq", "chan"),
        P("chan"),
    )
    return jax.shard_map(
        local,
        mesh=mesh,
        in_specs=placed,
        out_specs=(P("chan", "seq"), P("seq", "chan")),
        check_vma=False,
    )
```

```python
import functools
import math

import jax
import jax.numpy as jnp
import ml_dtypes
import numpy as np
from jax import lax
from jax.experimental import pallas as pl
from jax.experimental.pallas import tpu as pltpu
from jax.sharding import PartitionSpec as P

D = 4096
HEAD_DIM = 128
TILES = 4
MESH = pl.DeviceIdType.MESH
PRODUCT, QUERIES, KEYS, GATES, BANDED, ATTENDED, SQUARES = range(7)
TRANSPOSED = (((1,), (1,)), ((), ()))


def high_low(table):
    high = table.astype(ml_dtypes.bfloat16)
    low = (table - high.astype(np.float64)).astype(ml_dtypes.bfloat16)
    return np.stack((high, low))


def odd_tables(stripes, rows):
    frequency = np.arange(rows, dtype=np.float64) + 0.5
    angle = 2.0 * np.pi * frequency[:, None] * np.arange(rows)[None, :] / (2 * rows)
    dense = np.concatenate((np.cos(angle), -np.sin(angle)), axis=0)
    twist = 2.0 * np.pi * frequency[:, None] * np.arange(stripes)[None, :] / (2 * rows * stripes)
    turns = np.zeros((rows, 128), np.float32)
    turns[:, :stripes] = np.cos(twist)
    turns[:, stripes : 2 * stripes] = np.sin(twist)
    return high_low(dense), high_low(dense.T), turns


def small_dft(parts, sign):
    count = len(parts)
    if count == 1:
        return parts
    even = small_dft(parts[0::2], sign)
    odd = small_dft(parts[1::2], sign)
    first, second = [], []
    for k in range(count // 2):
        real, imag = odd[k]
        cos = math.cos(2.0 * math.pi * k / count)
        sin = sign * math.sin(2.0 * math.pi * k / count)
        if k == 0:
            turned = (real, imag)
        elif 4 * k == count:
            turned = (-sign * imag, sign * real)
        else:
            turned = (real * cos - imag * sin, real * sin + imag * cos)
        first.append((even[k][0] + turned[0], even[k][1] + turned[1]))
        second.append((even[k][0] - turned[0], even[k][1] - turned[1]))
    return first + second


def dot(left, right):
    return jnp.dot(left, right, preferred_element_type=jnp.float32)


def split(wide):
    high = wide.astype(jnp.bfloat16)
    return high, (wide - high.astype(jnp.float32)).astype(jnp.bfloat16)


def fused_kernel(
    n,
    chans,
    order_ref,
    skip_ref,
    gain_ref,
    hk_hbm,
    hv_hbm,
    hq_hbm,
    filter_hbm,
    q_hbm,
    k_hbm,
    forward_hbm,
    inverse_hbm,
    turns_hbm,
    banded_ref,
    attended_ref,
    hk_ref,
    hv_ref,
    gate_all,
    q_all,
    k_all,
    product_out,
    product_in,
    gate_in,
    q_in,
    k_in,
    filter_ref,
    forward_ref,
    inverse_ref,
    turns_ref,
    upright,
    signal,
    section,
    spectrum,
    back,
    convolved,
    gated,
    gated_out,
    values,
    result,
    squares,
    squares_chan,
    squares_sum,
    squares_seq,
    bias,
    send_sem,
    recv_sem,
    chan_send,
    chan_recv,
    local_sem,
):
    me = lax.axis_index("seq")
    my_chan = lax.axis_index("chan")
    pencil, rows = product_in.shape[1:]
    tile = rows // TILES
    wide_tile = n * tile

    def peer(offset):
        return lax.rem(me + offset, n)

    half = n // 2
    inner = lax.rem(me, half)
    near, across = me - inner, half - (me - inner)
    phase = lax.rem(my_chan + me // 2, 2)
    targets = []
    for turn in range(half):
        far = across + lax.rem(inner + turn, half)
        if turn == half - 1:
            targets.append(far)
        else:
            beside = near + lax.rem(inner + 1 + turn, half)
            targets.append(far * (1 - phase) + beside * phase)
            targets.append(beside * (1 - phase) + far * phase)
    offsets = [lax.rem(target - me + n, n) for target in targets]

    def block(ref, index):
        return ref.at[pl.ds(pl.multiple_of(index * pencil, pencil), pencil), :]

    def column(ref, index):
        return ref.at[:, pl.ds(pl.multiple_of(index * pencil, pencil), pencil)]

    def exchange(kind, source, here):
        return [
            pltpu.make_async_remote_copy(
                src_ref=source(target),
                dst_ref=here,
                send_sem=send_sem.at[kind, offset],
                recv_sem=recv_sem.at[kind, offset],
                device_id={"seq": target},
                device_id_type=MESH,
            )
            for target, offset in zip(targets, offsets)
        ]

    barrier = pltpu.get_barrier_semaphore()
    for offset in range(1, n):
        pl.semaphore_signal(barrier, inc=1, device_id={"seq": peer(offset)}, device_id_type=MESH)
    for offset in range(1, chans):
        other = lax.rem(my_chan + offset, chans)
        pl.semaphore_signal(barrier, inc=1, device_id={"chan": other}, device_id_type=MESH)

    staged = [
        (hk_hbm, hk_ref),
        (hv_hbm, hv_ref),
        (hq_hbm, gate_all),
        (filter_hbm, filter_ref),
        (forward_hbm, forward_ref),
        (inverse_hbm, inverse_ref),
        (turns_hbm, turns_ref),
        (q_hbm, q_all),
        (k_hbm, k_all),
    ]
    staged = [
        pltpu.make_async_copy(source, target, local_sem.at[index])
        for index, (source, target) in enumerate(staged)
    ]
    for copy in staged:
        copy.start()

    products = exchange(PRODUCT, lambda d: product_out.at[d], product_in.at[me])
    queries = exchange(QUERIES, lambda d: column(q_all, d), q_in.at[me])
    keys = exchange(KEYS, lambda d: column(k_all, d), k_in.at[me])
    gates = exchange(GATES, lambda d: block(gate_all, d), gate_in.at[me])

    def product_of(index):
        return (
            block(hk_ref, index)[...].astype(jnp.float32)
            * block(hv_ref, index)[...].astype(jnp.float32)
        ).astype(jnp.bfloat16)

    for copy in staged[:2]:
        copy.wait()
    pl.semaphore_wait(barrier, n - 1 + chans - 1)
    for target, copy in zip(targets, products):
        product_out[target] = product_of(target)
        copy.start()
    staged[2].wait()
    for copy in gates:
        copy.start()
    product_in[me] = product_of(me)
    gate_in[me] = block(gate_all, me)[...]

    for copy in staged[3:]:
        copy.wait()
    q_in[me] = column(q_all, me)[...]
    k_in[me] = column(k_all, me)[...]

    def turned_sections(part):
        cos = turns_ref[part, :]
        parts = []
        for t in range(n):
            real = section[part, t * pencil : (t + 1) * pencil]
            below = pl.ds(pl.multiple_of(rows + part.start, part.size), part.size)
            imag = section[below, t * pencil : (t + 1) * pencil]
            c, s = cos[:, t : t + 1], cos[:, n + t : n + t + 1]
            parts.append((real * c + imag * s, imag * c - real * s))
        return small_dft(parts, -1.0)

    step = 16

    def filter_spectrum(index, unused):
        part = pl.ds(pl.multiple_of(index * step, step), step)
        scale = 1.0 / (rows * n)
        for k, (real, imag) in enumerate(turned_sections(part)):
            spectrum[0, part, k * pencil : (k + 1) * pencil] = real * scale
            spectrum[1, part, k * pencil : (k + 1) * pencil] = imag * scale
        return unused

    def signal_spectrum(index, unused):
        part = pl.ds(pl.multiple_of(index * step, step), step)
        below = pl.ds(pl.multiple_of(rows + index * step, step), step)
        parts = []
        for k, (real, imag) in enumerate(turned_sections(part)):
            other_real = spectrum[0, part, k * pencil : (k + 1) * pencil]
            other_imag = spectrum[1, part, k * pencil : (k + 1) * pencil]
            parts.append(
                (real * other_real - imag * other_imag, real * other_imag + imag * other_real)
            )
        cos = turns_ref[part, :]
        for t, (real, imag) in enumerate(small_dft(parts, 1.0)):
            c, s = cos[:, t : t + 1], cos[:, n + t : n + t + 1]
            lanes = slice(t * pencil, (t + 1) * pencil)
            for place, value in ((part, real * c - imag * s), (below, real * s + imag * c)):
                high, low = split(value)
                back[0, place, lanes] = high
                back[1, place, lanes] = low
        return unused

    for s in range(n):
        upright[s * rows : (s + 1) * rows, :] = filter_ref[:, s * rows : (s + 1) * rows].T
    for t in range(0, n, 2):
        pair = jnp.concatenate(
            [upright[pl.ds(t + u, rows, stride=n), :] for u in range(2)], axis=1
        )
        high, low = split(pair)
        section[:, t * pencil : (t + 2) * pencil] = (
            dot(forward_ref[0], high) + dot(forward_ref[1], high) + dot(forward_ref[0], low)
        )
    lax.fori_loop(0, rows // step, filter_spectrum, 0)
    for copy in queries:
        copy.start()

    def place_of(index, count):
        inner = lax.rem(index, tile)
        place = n * inner
        for s in range(n):
            place = place + jnp.where(index // tile == s, order_ref[s * rows], 0)
        return place

    key_place = place_of(lax.broadcasted_iota(jnp.int32, (8, wide_tile), 1), wide_tile)[:1]
    query_place = place_of(lax.broadcasted_iota(jnp.int32, (wide_tile, 128), 0), wide_tile)[:, :1]
    bias[...] = jnp.where(key_place <= query_place, 0.0, -1e30)

    for copy in products:
        copy.wait()

    def stand_up(source):
        for s in range(n):
            upright[s * rows : (s + 1) * rows, :] = source[s].astype(jnp.float32).T

    stand_up(product_in)
    for t in range(0, n, 2):
        pair = [upright[pl.ds(t + u, rows, stride=n), :] for u in range(2)]
        signal[t] = pair[0]
        signal[t + 1] = pair[1]
        exact = jnp.concatenate(pair, axis=1).astype(jnp.bfloat16)
        section[:, t * pencil : (t + 2) * pencil] = dot(forward_ref[0], exact) + dot(
            forward_ref[1], exact
        )
    lax.fori_loop(0, rows // step, signal_spectrum, 0)
    for t in range(0, n, 2):
        lanes = slice(t * pencil, (t + 2) * pencil)
        high, low = back[0, :, lanes], back[1, :, lanes]
        pair = dot(inverse_ref[0], high) + dot(inverse_ref[1], high) + dot(inverse_ref[0], low)
        for u in range(2):
            convolved[t + u] = (
                pair[:, u * pencil : (u + 1) * pencil] + skip_ref[...] * signal[t + u]
            )

    for copy in gates:
        copy.wait()
    stand_up(gate_in)
    for t in range(n):
        gated[t] = (upright[pl.ds(t, rows, stride=n), :] * convolved[t]).astype(jnp.bfloat16)

    banded = exchange(BANDED, lambda d: gated_out.at[d], block(banded_ref, me))
    ones = jnp.ones((8, pencil), jnp.float32)
    for s in range(n):
        mine = gated[order_ref[s * rows]].astype(jnp.float32)
        values[s] = mine.astype(jnp.bfloat16)
        squares[s : s + 1, :] = lax.dot_general(
            ones,
            mine * mine,
            TRANSPOSED,
            precision=lax.Precision.HIGHEST,
            preferred_element_type=jnp.float32,
        )[:1]
    beside_chan = [
        pltpu.make_async_remote_copy(
            src_ref=squares,
            dst_ref=squares_chan.at[offset],
            send_sem=chan_send.at[offset],
            recv_sem=chan_recv.at[offset],
            device_id={"chan": lax.rem(my_chan + offset, chans)},
            device_id_type=MESH,
        )
        for offset in range(1, chans)
    ]
    for copy in beside_chan:
        copy.start()
    for copy in beside_chan:
        copy.wait()
    squares_sum[...] = functools.reduce(
        jnp.add, [squares[...]] + [squares_chan[offset] for offset in range(1, chans)]
    )
    along = exchange(SQUARES, lambda d: squares_sum, squares_seq.at[me])
    for copy in along:
        copy.start()
    for copy in keys:
        copy.start()
    for s in range(n):
        gated_out[s] = gated[order_ref[s * rows]].astype(jnp.float32).T.astype(jnp.bfloat16)
    squares_seq[me] = squares_sum[...]
    for copy in along:
        copy.wait()
    inverse_rms = lax.rsqrt(
        functools.reduce(jnp.add, [squares_seq[s] for s in range(n)]) / D + 1e-05
    )
    gain = gain_ref[pl.ds(me, 1), :]
    for s in range(n):
        scale = jnp.broadcast_to(inverse_rms[s : s + 1, :], (pencil, rows)).T
        values[s] = (values[s].astype(jnp.float32) * scale * gain).astype(jnp.bfloat16)

    for copy in keys:
        copy.wait_send()
    for copy in banded:
        copy.start()
    block(banded_ref, me)[...] = gated_out[me]
    for copy in queries:
        copy.wait()
    for copy in keys:
        copy.wait_recv()

    factor = math.log2(math.e) / math.sqrt(HEAD_DIM)
    height = half * tile
    attended = exchange(ATTENDED, lambda d: result.at[d], column(attended_ref, me))

    def attend_half(turn, unused):
        h = lax.rem(1 - me // half + turn, 2)
        first = pl.multiple_of(h * half, half)
        for jt in range(TILES):
            query = q_in[pl.ds(first, half), jt * tile : (jt + 1) * tile, :]
            query = query.reshape(height, pencil)
            scores = []
            for kt in range(jt + 1):
                key = k_in[:, kt * tile : (kt + 1) * tile, :].reshape(wide_tile, pencil)
                score = lax.dot_general(
                    query, key, TRANSPOSED, preferred_element_type=jnp.float32
                )
                if kt == jt:
                    score = score + bias[pl.ds(pl.multiple_of(h * height, height), height), :]
                scores.append(score)
            top = functools.reduce(jnp.maximum, [jnp.max(s, axis=1, keepdims=True) for s in scores])
            total = jnp.zeros((height, 1), jnp.float32)
            summed = jnp.zeros((height, pencil), jnp.float32)
            for kt, score in enumerate(scores):
                weight = jnp.exp2((score - top) * factor)
                total = total + jnp.sum(weight, axis=1, keepdims=True)
                value = values[:, kt * tile : (kt + 1) * tile, :].reshape(wide_tile, pencil)
                summed = summed + dot(weight.astype(jnp.bfloat16), value)
            part = (summed / total).astype(jnp.bfloat16)
            result[pl.ds(first, half), jt * tile : (jt + 1) * tile, :] = part.reshape(
                half, tile, pencil
            )
        for target, copy in zip(targets, attended):

            @pl.when(target // half == h)
            def send():
                copy.start()

        return unused

    lax.fori_loop(0, 2, attend_half, 0)
    column(attended_ref, me)[...] = result[me]
    for copy in banded + attended:
        copy.wait()


def fused(
    hyena_query,
    hyena_key,
    hyena_value,
    long_filter,
    skip_weight,
    stripe_order,
    query_rows,
    key_rows,
    norm_gain,
):
    n = lax.axis_size("seq")
    chans = lax.axis_size("chan")
    channels, rows = hyena_query.shape
    pencil = long_filter.shape[0]
    forward_table, inverse_table, turns = odd_tables(n, rows)
    vmem = pl.BlockSpec(memory_space=pltpu.VMEM)
    far = pl.BlockSpec(memory_space=pl.ANY)
    bf16, f32 = jnp.bfloat16, jnp.float32
    wide = n * pencil
    tile = rows // TILES
    return pl.pallas_call(
        functools.partial(fused_kernel, n, chans),
        out_shape=(
            jax.ShapeDtypeStruct((channels, rows), bf16),
            jax.ShapeDtypeStruct((rows, channels), bf16),
        ),
        in_specs=[pl.BlockSpec(memory_space=pltpu.SMEM)] + [vmem] * 2 + [far] * 9,
        out_specs=(vmem, vmem),
        scratch_shapes=[
            pltpu.VMEM((channels, rows), bf16),
            pltpu.VMEM((channels, rows), bf16),
            pltpu.VMEM((channels, rows), bf16),
            pltpu.VMEM((rows, channels), bf16),
            pltpu.VMEM((rows, channels), bf16),
            pltpu.VMEM((n, pencil, rows), bf16),
            pltpu.VMEM((n, pencil, rows), bf16),
            pltpu.VMEM((n, pencil, rows), bf16),
            pltpu.VMEM((n, rows, pencil), bf16),
            pltpu.VMEM((n, rows, pencil), bf16),
            pltpu.VMEM(long_filter.shape, f32),
            pltpu.VMEM(forward_table.shape, bf16),
            pltpu.VMEM(inverse_table.shape, bf16),
            pltpu.VMEM(turns.shape, f32),
            pltpu.VMEM((n * rows, pencil), f32),
            pltpu.VMEM((n, rows, pencil), f32),
            pltpu.VMEM((2 * rows, wide), f32),
            pltpu.VMEM((2, rows, wide), f32),
            pltpu.VMEM((2, 2 * rows, wide), bf16),
            pltpu.VMEM((n, rows, pencil), f32),
            pltpu.VMEM((n, rows, pencil), bf16),
            pltpu.VMEM((n, pencil, rows), bf16),
            pltpu.VMEM((n, rows, pencil), bf16),
            pltpu.VMEM((n, rows, pencil), bf16),
            pltpu.VMEM((n, rows), f32),
            pltpu.VMEM((chans, n, rows), f32),
            pltpu.VMEM((n, rows), f32),
            pltpu.VMEM((n, n, rows), f32),
            pltpu.VMEM((n * tile, n * tile), f32),
            pltpu.SemaphoreType.DMA((7, n)),
            pltpu.SemaphoreType.DMA((7, n)),
            pltpu.SemaphoreType.DMA((chans,)),
            pltpu.SemaphoreType.DMA((chans,)),
            pltpu.SemaphoreType.DMA((9,)),
        ],
        compiler_params=pltpu.CompilerParams(
            collective_id=0, has_side_effects=True, vmem_limit_bytes=60 * 1024 * 1024
        ),
    )(
        stripe_order,
        skip_weight.reshape(1, pencil),
        norm_gain.reshape(n, pencil),
        hyena_key,
        hyena_value,
        hyena_query,
        long_filter,
        query_rows,
        key_rows,
        jnp.asarray(forward_table),
        jnp.asarray(inverse_table),
        jnp.asarray(turns),
    )


def passed_along(block, axis, distance):
    devices = range(lax.axis_size(axis))
    route = [((i - distance) % len(devices), i) for i in devices]
    return lax.ppermute(block, axis, route)


def angle_table(first, second, modulus):
    left = jnp.arange(first, dtype=jnp.int32)[:, None]
    right = jnp.arange(second, dtype=jnp.int32)[None, :]
    theta = 2.0 * math.pi / modulus * (left * right % modulus).astype(jnp.float32)
    return (jnp.cos(theta), jnp.sin(theta))


def transform_tables(length):
    outer = 2 * length // 128
    first_cos, first_sin = angle_table(outer, outer // 2, outer)
    twist_cos, twist_sin = angle_table(outer, 128, 2 * length)
    inner_cos, inner_sin = angle_table(128, 128, 128)
    return (first_cos, first_sin, twist_cos, twist_sin, inner_cos, inner_sin)


def contract(form, left, right):
    return jnp.einsum(form, left, right, precision=lax.Precision.HIGHEST)


def forward(signal, tables):
    first_cos, first_sin, twist_cos, twist_sin, inner_cos, inner_sin = tables
    section_real = contract("kt,cts->cks", first_cos, signal)
    section_imag = -contract("kt,cts->cks", first_sin, signal)
    turned_real = section_real * twist_cos + section_imag * twist_sin
    turned_imag = section_imag * twist_cos - section_real * twist_sin
    out_real = contract("cks,sm->ckm", turned_real, inner_cos) + contract(
        "cks,sm->ckm", turned_imag, inner_sin
    )
    out_imag = contract("cks,sm->ckm", turned_imag, inner_cos) - contract(
        "cks,sm->ckm", turned_real, inner_sin
    )
    return (out_real, out_imag)


def inverse(spectrum_real, spectrum_imag, tables):
    first_cos, first_sin, twist_cos, twist_sin, inner_cos, inner_sin = tables
    back_real = contract("ckm,sm->cks", spectrum_real, inner_cos) - contract(
        "ckm,sm->cks", spectrum_imag, inner_sin
    )
    back_imag = contract("ckm,sm->cks", spectrum_real, inner_sin) + contract(
        "ckm,sm->cks", spectrum_imag, inner_cos
    )
    turned_real = back_real * twist_cos - back_imag * twist_sin
    turned_imag = back_real * twist_sin + back_imag * twist_cos
    signal = contract("kt,cks->cts", first_cos, turned_real) - contract(
        "kt,cks->cts", first_sin, turned_imag
    )
    return signal * (1.0 / (first_cos.shape[0] * 128))


def convolve(signal, filter_parts, tables):
    pencil, length = signal.shape
    widened = signal.astype(jnp.float32).reshape(pencil, length // 128, 128)
    signal_real, signal_imag = forward(widened, tables)
    filter_real, filter_imag = filter_parts
    product_real = signal_real * filter_real - signal_imag * filter_imag
    product_imag = signal_real * filter_imag + signal_imag * filter_real
    return inverse(product_real, product_imag, tables).reshape(pencil, length)


def fold_keys(carry, queries, own_places, key_piece, value_piece, places, scale):
    count = key_piece.shape[0]
    heads = queries.shape[1]
    depth = queries.shape[2]
    block = math.gcd(count, 512)
    place_blocks = places.reshape(count // block, block)
    key_blocks = key_piece.reshape(count // block, block, heads, depth)
    value_blocks = value_piece.reshape(count // block, block, heads, depth)

    def one_block(state, inputs):
        running, totals, sums = state
        key_block, value_block, key_places = inputs
        scores = (
            jnp.einsum("qhd,khd->hqk", queries, key_block, preferred_element_type=jnp.float32)
            * scale
        )
        allowed = key_places[None, None, :] <= own_places[None, :, None]
        scores = jnp.where(allowed, scores, -1e30)
        highest = jnp.maximum(running, jnp.max(scores, axis=2))
        weights = jnp.where(allowed, jnp.exp(scores - highest[:, :, None]), 0.0)
        factor = jnp.exp(running - highest)
        totals = totals * factor + jnp.sum(weights, axis=2)
        update = jnp.einsum(
            "hqk,khd->hqd",
            weights.astype(jnp.bfloat16),
            value_block,
            preferred_element_type=jnp.float32,
        )
        sums = sums * factor[:, :, None] + update
        return ((highest, totals, sums), None)

    carry, unused = lax.scan(one_block, carry, (key_blocks, value_blocks, place_blocks))
    return carry


def general(
    hyena_query,
    hyena_key,
    hyena_value,
    long_filter,
    skip_weight,
    stripe_order,
    query_rows,
    key_rows,
    norm_gain,
):
    stripes = lax.axis_size("seq")
    channels, rows = hyena_query.shape
    pencil, length = long_filter.shape
    sigma = stripe_order.reshape(stripes, rows)[:, 0]
    product = (hyena_key.astype(jnp.float32) * hyena_value.astype(jnp.float32)).astype(jnp.bfloat16)
    tables = transform_tables(length)
    filter_parts = forward(long_filter.reshape(pencil, length // 128, 128), tables)
    spread = lax.all_to_all(product, "seq", split_axis=0, concat_axis=1, tiled=True)
    summed = convolve(spread, filter_parts, tables) + skip_weight[:, None] * spread.astype(
        jnp.float32
    )
    returned = lax.all_to_all(
        summed.astype(jnp.bfloat16), "seq", split_axis=1, concat_axis=0, tiled=True
    ).astype(summed.dtype)
    gated = (hyena_query.astype(jnp.float32) * returned).astype(jnp.bfloat16)
    per_stripe = rows // stripes
    columns = stripes * jnp.arange(per_stripe, dtype=jnp.int32)[None, :] + sigma[:, None]
    arranged = jnp.take(gated, columns.reshape(rows), axis=1).reshape(channels, stripes, per_stripe)
    banded = lax.all_to_all(arranged, "seq", split_axis=1, concat_axis=2, tiled=True).reshape(
        channels, rows
    )
    output_wide = banded.astype(jnp.float32)
    squares = lax.psum(jnp.sum(output_wide * output_wide, axis=0), "chan")
    inverse_rms = lax.rsqrt(squares / D + 1e-05)
    normed = (output_wide * inverse_rms[None, :] * norm_gain[:, None]).astype(jnp.bfloat16)
    value_rows = normed.T
    local_heads = channels // HEAD_DIM
    scale = 1.0 / math.sqrt(HEAD_DIM)
    seq_index = lax.axis_index("seq")
    own_head = seq_index % local_heads
    group_index = seq_index // local_heads
    group_count = stripes // local_heads
    span = local_heads * rows
    stacked_local = jnp.stack((query_rows, key_rows, value_rows)).reshape(
        3, rows, local_heads, HEAD_DIM
    )
    collected = [lax.dynamic_index_in_dim(stacked_local, own_head, 2, keepdims=False)]
    for offset in range(1, local_heads):
        payload = lax.dynamic_index_in_dim(
            stacked_local, (own_head + offset) % local_heads, 2, keepdims=False
        )
        from_below = passed_along(payload, "seq", offset)
        from_above = passed_along(payload, "seq", offset - local_heads)
        collected.append(jnp.where(own_head >= offset, from_below, from_above))
    ordering = (own_head - jnp.arange(local_heads, dtype=jnp.int32)) % local_heads
    sources = jnp.take(jnp.stack(collected), ordering, axis=0)
    combined = sources.transpose(1, 0, 2, 3).reshape(3, span, HEAD_DIM)
    group_places = lax.dynamic_slice_in_dim(stripe_order, group_index * span, span)
    group_queries = combined[0].reshape(span, 1, HEAD_DIM)

    def visit(state, kv_pair, source):
        places = lax.dynamic_slice_in_dim(stripe_order, source * span, span)
        return fold_keys(
            state,
            group_queries,
            group_places,
            kv_pair[0].reshape(span, 1, HEAD_DIM),
            kv_pair[1].reshape(span, 1, HEAD_DIM),
            places,
            scale,
        )

    initial_group = (
        jnp.full((1, span), -1e30, jnp.float32),
        jnp.zeros((1, span), jnp.float32),
        jnp.zeros((1, span, HEAD_DIM), jnp.float32),
    )

    def cycle_turn(turn, loop_state):
        state, kv_pair = loop_state
        state = visit(state, kv_pair, (group_index - turn) % group_count)
        kv_pair = passed_along(kv_pair, "seq", local_heads)
        return (state, kv_pair)

    state, kv_pair = lax.fori_loop(0, group_count - 1, cycle_turn, (initial_group, combined[1:]))
    running, totals, sums = visit(state, kv_pair, (group_index - (group_count - 1)) % group_count)
    result = (sums[0] / totals[0][:, None]).astype(jnp.bfloat16)
    pieces = result.reshape(local_heads, rows, HEAD_DIM)
    returned_heads = [lax.dynamic_index_in_dim(pieces, own_head, 0, keepdims=False)]
    for offset in range(1, local_heads):
        payload = lax.dynamic_index_in_dim(
            pieces, (own_head + offset) % local_heads, 0, keepdims=False
        )
        back_below = passed_along(payload, "seq", offset)
        back_above = passed_along(payload, "seq", offset - local_heads)
        returned_heads.append(jnp.where(own_head >= offset, back_below, back_above))
    by_head = jnp.take(jnp.stack(returned_heads), ordering, axis=0)
    attended = by_head.transpose(1, 0, 2).reshape(rows, channels)
    return (banded, attended)


def local(*arrays):
    pencil = arrays[3].shape[0]
    rows = arrays[0].shape[1]
    stripes = lax.axis_size("seq")
    even = stripes % 2 == 0 and stripes & (stripes - 1) == 0 and 2 * stripes <= HEAD_DIM
    one_head = pencil == HEAD_DIM and even and rows % (16 * TILES) == 0
    return fused(*arrays) if one_head else general(*arrays)


def solution(mesh):
    placed = (
        P("chan", "seq"),
        P("chan", "seq"),
        P("chan", "seq"),
        P(("chan", "seq"), None),
        P(("chan", "seq")),
        P(),
        P("seq", "chan"),
        P("seq", "chan"),
        P("chan"),
    )
    return jax.shard_map(
        local,
        mesh=mesh,
        in_specs=placed,
        out_specs=(P("chan", "seq"), P("seq", "chan")),
        check_vma=False,
    )
```

```python
import functools
import math

import jax
import jax.numpy as jnp
import ml_dtypes
import numpy as np
from jax import lax
from jax.experimental import pallas as pl
from jax.experimental.pallas import tpu as pltpu
from jax.sharding import PartitionSpec as P

D = 4096
HEAD_DIM = 128
TILES = 4
MESH = pl.DeviceIdType.MESH
PRODUCT, QUERIES, KEYS, GATES, BANDED, ATTENDED, SQUARES = range(7)


def high_low(table):
    high = table.astype(ml_dtypes.bfloat16)
    low = (table - high.astype(np.float64)).astype(ml_dtypes.bfloat16)
    return np.stack((high, low))


def odd_tables(stripes, rows):
    frequency = np.arange(rows, dtype=np.float64) + 0.5
    angle = 2.0 * np.pi * frequency[:, None] * np.arange(rows)[None, :] / (2 * rows)
    dense = np.concatenate((np.cos(angle), -np.sin(angle)), axis=0)
    twist = 2.0 * np.pi * frequency[:, None] * np.arange(stripes)[None, :] / (2 * rows * stripes)
    turns = np.zeros((rows, 128), np.float32)
    turns[:, :stripes] = np.cos(twist)
    turns[:, stripes : 2 * stripes] = np.sin(twist)
    return high_low(dense), high_low(dense.T), turns


def small_dft(parts, sign):
    count = len(parts)
    if count == 1:
        return parts
    even = small_dft(parts[0::2], sign)
    odd = small_dft(parts[1::2], sign)
    first, second = [], []
    for k in range(count // 2):
        real, imag = odd[k]
        cos = math.cos(2.0 * math.pi * k / count)
        sin = sign * math.sin(2.0 * math.pi * k / count)
        if k == 0:
            turned = (real, imag)
        elif 4 * k == count:
            turned = (-sign * imag, sign * real)
        else:
            turned = (real * cos - imag * sin, real * sin + imag * cos)
        first.append((even[k][0] + turned[0], even[k][1] + turned[1]))
        second.append((even[k][0] - turned[0], even[k][1] - turned[1]))
    return first + second


def dot(left, right):
    return jnp.dot(left, right, preferred_element_type=jnp.float32)


def split(wide):
    high = wide.astype(jnp.bfloat16)
    return high, (wide - high.astype(jnp.float32)).astype(jnp.bfloat16)


def fused_kernel(
    n,
    chans,
    order_ref,
    skip_ref,
    gain_ref,
    hk_hbm,
    hv_hbm,
    hq_hbm,
    filter_hbm,
    q_hbm,
    k_hbm,
    forward_hbm,
    inverse_hbm,
    turns_hbm,
    banded_ref,
    attended_ref,
    hk_ref,
    hv_ref,
    gate_all,
    q_all,
    k_all,
    product_out,
    product_in,
    gate_in,
    q_in,
    k_in,
    filter_ref,
    forward_ref,
    inverse_ref,
    turns_ref,
    upright,
    signal,
    section,
    spectrum,
    back,
    convolved,
    gated,
    gated_out,
    values,
    result,
    squares,
    squares_chan,
    squares_sum,
    squares_seq,
    bias,
    turned_keys,
    send_sem,
    recv_sem,
    chan_send,
    chan_recv,
    local_sem,
):
    me = lax.axis_index("seq")
    my_chan = lax.axis_index("chan")
    pencil, rows = product_in.shape[1:]
    tile = rows // TILES
    wide_tile = n * tile

    def peer(offset):
        return lax.rem(me + offset, n)

    half = n // 2
    inner = lax.rem(me, half)
    near, across = me - inner, half - (me - inner)
    phase = lax.rem(my_chan + me // 2, 2)
    targets = []
    for turn in range(half):
        far = across + lax.rem(inner + turn, half)
        if turn == half - 1:
            targets.append(far)
        else:
            beside = near + lax.rem(inner + 1 + turn, half)
            targets.append(far * (1 - phase) + beside * phase)
            targets.append(beside * (1 - phase) + far * phase)
    offsets = [lax.rem(target - me + n, n) for target in targets]

    def block(ref, index):
        return ref.at[pl.ds(pl.multiple_of(index * pencil, pencil), pencil), :]

    def column(ref, index):
        return ref.at[:, pl.ds(pl.multiple_of(index * pencil, pencil), pencil)]

    def exchange(kind, source, here):
        return [
            pltpu.make_async_remote_copy(
                src_ref=source(target),
                dst_ref=here,
                send_sem=send_sem.at[kind, offset],
                recv_sem=recv_sem.at[kind, offset],
                device_id={"seq": target},
                device_id_type=MESH,
            )
            for target, offset in zip(targets, offsets)
        ]

    barrier = pltpu.get_barrier_semaphore()
    for offset in range(1, n):
        pl.semaphore_signal(barrier, inc=1, device_id={"seq": peer(offset)}, device_id_type=MESH)
    for offset in range(1, chans):
        other = lax.rem(my_chan + offset, chans)
        pl.semaphore_signal(barrier, inc=1, device_id={"chan": other}, device_id_type=MESH)

    staged = [
        (hk_hbm, hk_ref),
        (hv_hbm, hv_ref),
        (hq_hbm, gate_all),
        (filter_hbm, filter_ref),
        (forward_hbm, forward_ref),
        (inverse_hbm, inverse_ref),
        (turns_hbm, turns_ref),
        (q_hbm, q_all),
        (k_hbm, k_all),
    ]
    staged = [
        pltpu.make_async_copy(source, target, local_sem.at[index])
        for index, (source, target) in enumerate(staged)
    ]
    for copy in staged:
        copy.start()

    products = exchange(PRODUCT, lambda d: product_out.at[d], product_in.at[me])
    queries = exchange(QUERIES, lambda d: column(q_all, d), q_in.at[me])
    keys = exchange(KEYS, lambda d: column(k_all, d), k_in.at[me])
    gates = exchange(GATES, lambda d: block(gate_all, d), gate_in.at[me])

    def product_of(index):
        return (
            block(hk_ref, index)[...].astype(jnp.float32)
            * block(hv_ref, index)[...].astype(jnp.float32)
        ).astype(jnp.bfloat16)

    for copy in staged[:2]:
        copy.wait()
    pl.semaphore_wait(barrier, n - 1 + chans - 1)
    for target, copy in zip(targets, products):
        product_out[target] = product_of(target)
        copy.start()
    staged[2].wait()
    for copy in gates:
        copy.start()
    product_in[me] = product_of(me)
    gate_in[me] = block(gate_all, me)[...]

    for copy in staged[3:]:
        copy.wait()
    q_in[me] = column(q_all, me)[...]
    k_in[me] = column(k_all, me)[...]

    def turned_sections(part):
        cos = turns_ref[part, :]
        parts = []
        for t in range(n):
            real = section[part, t * pencil : (t + 1) * pencil]
            below = pl.ds(pl.multiple_of(rows + part.start, part.size), part.size)
            imag = section[below, t * pencil : (t + 1) * pencil]
            c, s = cos[:, t : t + 1], cos[:, n + t : n + t + 1]
            parts.append((real * c + imag * s, imag * c - real * s))
        return small_dft(parts, -1.0)

    step = 16

    def filter_spectrum(index, unused):
        part = pl.ds(pl.multiple_of(index * step, step), step)
        scale = 1.0 / (rows * n)
        for k, (real, imag) in enumerate(turned_sections(part)):
            spectrum[0, part, k * pencil : (k + 1) * pencil] = real * scale
            spectrum[1, part, k * pencil : (k + 1) * pencil] = imag * scale
        return unused

    def signal_spectrum(index, unused):
        part = pl.ds(pl.multiple_of(index * step, step), step)
        below = pl.ds(pl.multiple_of(rows + index * step, step), step)
        parts = []
        for k, (real, imag) in enumerate(turned_sections(part)):
            other_real = spectrum[0, part, k * pencil : (k + 1) * pencil]
            other_imag = spectrum[1, part, k * pencil : (k + 1) * pencil]
            parts.append(
                (real * other_real - imag * other_imag, real * other_imag + imag * other_real)
            )
        cos = turns_ref[part, :]
        for t, (real, imag) in enumerate(small_dft(parts, 1.0)):
            c, s = cos[:, t : t + 1], cos[:, n + t : n + t + 1]
            lanes = slice(t * pencil, (t + 1) * pencil)
            for place, value in ((part, real * c - imag * s), (below, real * s + imag * c)):
                high, low = split(value)
                back[0, place, lanes] = high
                back[1, place, lanes] = low
        return unused

    for s in range(n):
        upright[s * rows : (s + 1) * rows, :] = filter_ref[:, s * rows : (s + 1) * rows].T
    for t in range(0, n, 2):
        pair = jnp.concatenate(
            [upright[pl.ds(t + u, rows, stride=n), :] for u in range(2)], axis=1
        )
        high, low = split(pair)
        section[:, t * pencil : (t + 2) * pencil] = (
            dot(forward_ref[0], high) + dot(forward_ref[1], high) + dot(forward_ref[0], low)
        )
    lax.fori_loop(0, rows // step, filter_spectrum, 0)
    for copy in queries:
        copy.start()

    def place_of(index):
        place = n * index + order_ref[0]
        for s in range(1, n):
            change = order_ref[s * rows] - order_ref[(s - 1) * rows] - n * tile
            place = place + jnp.where(index >= s * tile, change, 0)
        return place

    key_place = place_of(lax.broadcasted_iota(jnp.int32, (8, wide_tile), 1))[:1]
    query_place = place_of(lax.broadcasted_iota(jnp.int32, (wide_tile, 128), 0))[:, :1]
    bias[...] = jnp.where(key_place <= query_place, 0.0, -1e30)

    for copy in products:
        copy.wait()

    for copy in keys:
        copy.start()

    def stand_up(source):
        for s in range(n):
            upright[s * rows : (s + 1) * rows, :] = source[s].T.astype(jnp.float32)

    stand_up(product_in)
    for t in range(0, n, 2):
        pair = [upright[pl.ds(t + u, rows, stride=n), :] for u in range(2)]
        signal[t] = pair[0]
        signal[t + 1] = pair[1]
        exact = jnp.concatenate(pair, axis=1).astype(jnp.bfloat16)
        section[:, t * pencil : (t + 2) * pencil] = dot(forward_ref[0], exact) + dot(
            forward_ref[1], exact
        )
    lax.fori_loop(0, rows // step, signal_spectrum, 0)
    for t in range(0, n, 2):
        lanes = slice(t * pencil, (t + 2) * pencil)
        high, low = back[0, :, lanes], back[1, :, lanes]
        pair = dot(inverse_ref[0], high) + dot(inverse_ref[1], high) + dot(inverse_ref[0], low)
        for u in range(2):
            convolved[t + u] = (
                pair[:, u * pencil : (u + 1) * pencil] + skip_ref[...] * signal[t + u]
            )

    for copy in gates:
        copy.wait()
    stand_up(gate_in)
    for t in range(n):
        gated[t] = (upright[pl.ds(t, rows, stride=n), :] * convolved[t]).astype(jnp.bfloat16)

    banded = exchange(BANDED, lambda d: gated_out.at[d], block(banded_ref, me))
    lane = lax.broadcasted_iota(jnp.int32, (pencil, pencil), 1)
    summed_squares = jnp.zeros((rows, pencil), jnp.float32)
    for s in range(n):
        mine = gated[order_ref[s * rows]]
        values[s] = mine
        wide = mine.astype(jnp.float32)
        high, low = split(wide * wide)
        pick = jnp.where(lane == s, 1.0, 0.0).astype(jnp.bfloat16)
        summed_squares = summed_squares + dot(high, pick) + dot(low, pick)
    squares[...] = summed_squares.T[:n, :]
    beside_chan = [
        pltpu.make_async_remote_copy(
            src_ref=squares,
            dst_ref=squares_chan.at[offset],
            send_sem=chan_send.at[offset],
            recv_sem=chan_recv.at[offset],
            device_id={"chan": lax.rem(my_chan + offset, chans)},
            device_id_type=MESH,
        )
        for offset in range(1, chans)
    ]
    for copy in beside_chan:
        copy.start()
    for copy in beside_chan:
        copy.wait()
    squares_sum[...] = functools.reduce(
        jnp.add, [squares[...]] + [squares_chan[offset] for offset in range(1, chans)]
    )
    along = exchange(SQUARES, lambda d: squares_sum, squares_seq.at[me])
    for copy in along:
        copy.start()
    for s in range(n):
        gated_out[s] = values[s].T
    squares_seq[me] = squares_sum[...]
    for copy in keys:
        copy.wait_send()
    for copy in banded:
        copy.start()
    block(banded_ref, me)[...] = gated_out[me]
    for copy in queries:
        copy.wait()
    for copy in keys:
        copy.wait_recv()
    for kt in range(TILES):
        key = k_in[:, kt * tile : (kt + 1) * tile, :].reshape(wide_tile, pencil)
        turned_keys[kt] = key.T
    for copy in along:
        copy.wait()
    inverse_rms = lax.rsqrt(
        functools.reduce(jnp.add, [squares_seq[s] for s in range(n)]) / D + 1e-05
    )
    gain = gain_ref[pl.ds(me, 1), :]
    scales = jnp.concatenate([inverse_rms] * (pencil // n), axis=0).T
    for s in range(n):
        values[s] = (values[s].astype(jnp.float32) * scales[:, s : s + 1] * gain).astype(
            jnp.bfloat16
        )

    factor = math.log2(math.e) / math.sqrt(HEAD_DIM)
    height = half * tile
    attended = exchange(ATTENDED, lambda d: result.at[d], column(attended_ref, me))

    def attend_half(turn, unused):
        h = lax.rem(1 - me // half + turn, 2)
        first = pl.multiple_of(h * half, half)
        for jt in range(TILES):
            query = q_in[pl.ds(first, half), jt * tile : (jt + 1) * tile, :]
            query = query.reshape(height, pencil)
            scores = []
            for kt in range(jt + 1):
                score = dot(query, turned_keys[kt])
                if kt == jt:
                    score = score + bias[pl.ds(pl.multiple_of(h * height, height), height), :]
                scores.append(score)
            top = functools.reduce(jnp.maximum, [jnp.max(s, axis=1, keepdims=True) for s in scores])
            total = jnp.zeros((height, 1), jnp.float32)
            summed = jnp.zeros((height, pencil), jnp.float32)
            for kt, score in enumerate(scores):
                weight = jnp.exp2((score - top) * factor)
                total = total + jnp.sum(weight, axis=1, keepdims=True)
                value = values[:, kt * tile : (kt + 1) * tile, :].reshape(wide_tile, pencil)
                summed = summed + dot(weight.astype(jnp.bfloat16), value)
            part = (summed / total).astype(jnp.bfloat16)
            result[pl.ds(first, half), jt * tile : (jt + 1) * tile, :] = part.reshape(
                half, tile, pencil
            )
        for target, copy in zip(targets, attended):

            @pl.when(target // half == h)
            def send():
                copy.start()

        return unused

    lax.fori_loop(0, 2, attend_half, 0)
    column(attended_ref, me)[...] = result[me]
    for copy in banded + attended:
        copy.wait()


def fused(
    hyena_query,
    hyena_key,
    hyena_value,
    long_filter,
    skip_weight,
    stripe_order,
    query_rows,
    key_rows,
    norm_gain,
):
    n = lax.axis_size("seq")
    chans = lax.axis_size("chan")
    channels, rows = hyena_query.shape
    pencil = long_filter.shape[0]
    forward_table, inverse_table, turns = odd_tables(n, rows)
    vmem = pl.BlockSpec(memory_space=pltpu.VMEM)
    far = pl.BlockSpec(memory_space=pl.ANY)
    bf16, f32 = jnp.bfloat16, jnp.float32
    wide = n * pencil
    tile = rows // TILES
    return pl.pallas_call(
        functools.partial(fused_kernel, n, chans),
        out_shape=(
            jax.ShapeDtypeStruct((channels, rows), bf16),
            jax.ShapeDtypeStruct((rows, channels), bf16),
        ),
        in_specs=[pl.BlockSpec(memory_space=pltpu.SMEM)] + [vmem] * 2 + [far] * 9,
        out_specs=(vmem, vmem),
        scratch_shapes=[
            pltpu.VMEM((channels, rows), bf16),
            pltpu.VMEM((channels, rows), bf16),
            pltpu.VMEM((channels, rows), bf16),
            pltpu.VMEM((rows, channels), bf16),
            pltpu.VMEM((rows, channels), bf16),
            pltpu.VMEM((n, pencil, rows), bf16),
            pltpu.VMEM((n, pencil, rows), bf16),
            pltpu.VMEM((n, pencil, rows), bf16),
            pltpu.VMEM((n, rows, pencil), bf16),
            pltpu.VMEM((n, rows, pencil), bf16),
            pltpu.VMEM(long_filter.shape, f32),
            pltpu.VMEM(forward_table.shape, bf16),
            pltpu.VMEM(inverse_table.shape, bf16),
            pltpu.VMEM(turns.shape, f32),
            pltpu.VMEM((n * rows, pencil), f32),
            pltpu.VMEM((n, rows, pencil), f32),
            pltpu.VMEM((2 * rows, wide), f32),
            pltpu.VMEM((2, rows, wide), f32),
            pltpu.VMEM((2, 2 * rows, wide), bf16),
            pltpu.VMEM((n, rows, pencil), f32),
            pltpu.VMEM((n, rows, pencil), bf16),
            pltpu.VMEM((n, pencil, rows), bf16),
            pltpu.VMEM((n, rows, pencil), bf16),
            pltpu.VMEM((n, rows, pencil), bf16),
            pltpu.VMEM((n, rows), f32),
            pltpu.VMEM((chans, n, rows), f32),
            pltpu.VMEM((n, rows), f32),
            pltpu.VMEM((n, n, rows), f32),
            pltpu.VMEM((n * tile, n * tile), f32),
            pltpu.VMEM((TILES, pencil, n * tile), bf16),
            pltpu.SemaphoreType.DMA((7, n)),
            pltpu.SemaphoreType.DMA((7, n)),
            pltpu.SemaphoreType.DMA((chans,)),
            pltpu.SemaphoreType.DMA((chans,)),
            pltpu.SemaphoreType.DMA((9,)),
        ],
        compiler_params=pltpu.CompilerParams(
            collective_id=0, has_side_effects=True, vmem_limit_bytes=60 * 1024 * 1024
        ),
    )(
        stripe_order,
        skip_weight.reshape(1, pencil),
        norm_gain.reshape(n, pencil),
        hyena_key,
        hyena_value,
        hyena_query,
        long_filter,
        query_rows,
        key_rows,
        jnp.asarray(forward_table),
        jnp.asarray(inverse_table),
        jnp.asarray(turns),
    )


def passed_along(block, axis, distance):
    devices = range(lax.axis_size(axis))
    route = [((i - distance) % len(devices), i) for i in devices]
    return lax.ppermute(block, axis, route)


def angle_table(first, second, modulus):
    left = jnp.arange(first, dtype=jnp.int32)[:, None]
    right = jnp.arange(second, dtype=jnp.int32)[None, :]
    theta = 2.0 * math.pi / modulus * (left * right % modulus).astype(jnp.float32)
    return (jnp.cos(theta), jnp.sin(theta))


def transform_tables(length):
    outer = 2 * length // 128
    first_cos, first_sin = angle_table(outer, outer // 2, outer)
    twist_cos, twist_sin = angle_table(outer, 128, 2 * length)
    inner_cos, inner_sin = angle_table(128, 128, 128)
    return (first_cos, first_sin, twist_cos, twist_sin, inner_cos, inner_sin)


def contract(form, left, right):
    return jnp.einsum(form, left, right, precision=lax.Precision.HIGHEST)


def forward(signal, tables):
    first_cos, first_sin, twist_cos, twist_sin, inner_cos, inner_sin = tables
    section_real = contract("kt,cts->cks", first_cos, signal)
    section_imag = -contract("kt,cts->cks", first_sin, signal)
    turned_real = section_real * twist_cos + section_imag * twist_sin
    turned_imag = section_imag * twist_cos - section_real * twist_sin
    out_real = contract("cks,sm->ckm", turned_real, inner_cos) + contract(
        "cks,sm->ckm", turned_imag, inner_sin
    )
    out_imag = contract("cks,sm->ckm", turned_imag, inner_cos) - contract(
        "cks,sm->ckm", turned_real, inner_sin
    )
    return (out_real, out_imag)


def inverse(spectrum_real, spectrum_imag, tables):
    first_cos, first_sin, twist_cos, twist_sin, inner_cos, inner_sin = tables
    back_real = contract("ckm,sm->cks", spectrum_real, inner_cos) - contract(
        "ckm,sm->cks", spectrum_imag, inner_sin
    )
    back_imag = contract("ckm,sm->cks", spectrum_real, inner_sin) + contract(
        "ckm,sm->cks", spectrum_imag, inner_cos
    )
    turned_real = back_real * twist_cos - back_imag * twist_sin
    turned_imag = back_real * twist_sin + back_imag * twist_cos
    signal = contract("kt,cks->cts", first_cos, turned_real) - contract(
        "kt,cks->cts", first_sin, turned_imag
    )
    return signal * (1.0 / (first_cos.shape[0] * 128))


def convolve(signal, filter_parts, tables):
    pencil, length = signal.shape
    widened = signal.astype(jnp.float32).reshape(pencil, length // 128, 128)
    signal_real, signal_imag = forward(widened, tables)
    filter_real, filter_imag = filter_parts
    product_real = signal_real * filter_real - signal_imag * filter_imag
    product_imag = signal_real * filter_imag + signal_imag * filter_real
    return inverse(product_real, product_imag, tables).reshape(pencil, length)


def fold_keys(carry, queries, own_places, key_piece, value_piece, places, scale):
    count = key_piece.shape[0]
    heads = queries.shape[1]
    depth = queries.shape[2]
    block = math.gcd(count, 512)
    place_blocks = places.reshape(count // block, block)
    key_blocks = key_piece.reshape(count // block, block, heads, depth)
    value_blocks = value_piece.reshape(count // block, block, heads, depth)

    def one_block(state, inputs):
        running, totals, sums = state
        key_block, value_block, key_places = inputs
        scores = (
            jnp.einsum("qhd,khd->hqk", queries, key_block, preferred_element_type=jnp.float32)
            * scale
        )
        allowed = key_places[None, None, :] <= own_places[None, :, None]
        scores = jnp.where(allowed, scores, -1e30)
        highest = jnp.maximum(running, jnp.max(scores, axis=2))
        weights = jnp.where(allowed, jnp.exp(scores - highest[:, :, None]), 0.0)
        factor = jnp.exp(running - highest)
        totals = totals * factor + jnp.sum(weights, axis=2)
        update = jnp.einsum(
            "hqk,khd->hqd",
            weights.astype(jnp.bfloat16),
            value_block,
            preferred_element_type=jnp.float32,
        )
        sums = sums * factor[:, :, None] + update
        return ((highest, totals, sums), None)

    carry, unused = lax.scan(one_block, carry, (key_blocks, value_blocks, place_blocks))
    return carry


def general(
    hyena_query,
    hyena_key,
    hyena_value,
    long_filter,
    skip_weight,
    stripe_order,
    query_rows,
    key_rows,
    norm_gain,
):
    stripes = lax.axis_size("seq")
    channels, rows = hyena_query.shape
    pencil, length = long_filter.shape
    sigma = stripe_order.reshape(stripes, rows)[:, 0]
    product = (hyena_key.astype(jnp.float32) * hyena_value.astype(jnp.float32)).astype(jnp.bfloat16)
    tables = transform_tables(length)
    filter_parts = forward(long_filter.reshape(pencil, length // 128, 128), tables)
    spread = lax.all_to_all(product, "seq", split_axis=0, concat_axis=1, tiled=True)
    summed = convolve(spread, filter_parts, tables) + skip_weight[:, None] * spread.astype(
        jnp.float32
    )
    returned = lax.all_to_all(
        summed.astype(jnp.bfloat16), "seq", split_axis=1, concat_axis=0, tiled=True
    ).astype(summed.dtype)
    gated = (hyena_query.astype(jnp.float32) * returned).astype(jnp.bfloat16)
    per_stripe = rows // stripes
    columns = stripes * jnp.arange(per_stripe, dtype=jnp.int32)[None, :] + sigma[:, None]
    arranged = jnp.take(gated, columns.reshape(rows), axis=1).reshape(channels, stripes, per_stripe)
    banded = lax.all_to_all(arranged, "seq", split_axis=1, concat_axis=2, tiled=True).reshape(
        channels, rows
    )
    output_wide = banded.astype(jnp.float32)
    squares = lax.psum(jnp.sum(output_wide * output_wide, axis=0), "chan")
    inverse_rms = lax.rsqrt(squares / D + 1e-05)
    normed = (output_wide * inverse_rms[None, :] * norm_gain[:, None]).astype(jnp.bfloat16)
    value_rows = normed.T
    local_heads = channels // HEAD_DIM
    scale = 1.0 / math.sqrt(HEAD_DIM)
    seq_index = lax.axis_index("seq")
    own_head = seq_index % local_heads
    group_index = seq_index // local_heads
    group_count = stripes // local_heads
    span = local_heads * rows
    stacked_local = jnp.stack((query_rows, key_rows, value_rows)).reshape(
        3, rows, local_heads, HEAD_DIM
    )
    collected = [lax.dynamic_index_in_dim(stacked_local, own_head, 2, keepdims=False)]
    for offset in range(1, local_heads):
        payload = lax.dynamic_index_in_dim(
            stacked_local, (own_head + offset) % local_heads, 2, keepdims=False
        )
        from_below = passed_along(payload, "seq", offset)
        from_above = passed_along(payload, "seq", offset - local_heads)
        collected.append(jnp.where(own_head >= offset, from_below, from_above))
    ordering = (own_head - jnp.arange(local_heads, dtype=jnp.int32)) % local_heads
    sources = jnp.take(jnp.stack(collected), ordering, axis=0)
    combined = sources.transpose(1, 0, 2, 3).reshape(3, span, HEAD_DIM)
    group_places = lax.dynamic_slice_in_dim(stripe_order, group_index * span, span)
    group_queries = combined[0].reshape(span, 1, HEAD_DIM)

    def visit(state, kv_pair, source):
        places = lax.dynamic_slice_in_dim(stripe_order, source * span, span)
        return fold_keys(
            state,
            group_queries,
            group_places,
            kv_pair[0].reshape(span, 1, HEAD_DIM),
            kv_pair[1].reshape(span, 1, HEAD_DIM),
            places,
            scale,
        )

    initial_group = (
        jnp.full((1, span), -1e30, jnp.float32),
        jnp.zeros((1, span), jnp.float32),
        jnp.zeros((1, span, HEAD_DIM), jnp.float32),
    )

    def cycle_turn(turn, loop_state):
        state, kv_pair = loop_state
        state = visit(state, kv_pair, (group_index - turn) % group_count)
        kv_pair = passed_along(kv_pair, "seq", local_heads)
        return (state, kv_pair)

    state, kv_pair = lax.fori_loop(0, group_count - 1, cycle_turn, (initial_group, combined[1:]))
    running, totals, sums = visit(state, kv_pair, (group_index - (group_count - 1)) % group_count)
    result = (sums[0] / totals[0][:, None]).astype(jnp.bfloat16)
    pieces = result.reshape(local_heads, rows, HEAD_DIM)
    returned_heads = [lax.dynamic_index_in_dim(pieces, own_head, 0, keepdims=False)]
    for offset in range(1, local_heads):
        payload = lax.dynamic_index_in_dim(
            pieces, (own_head + offset) % local_heads, 0, keepdims=False
        )
        back_below = passed_along(payload, "seq", offset)
        back_above = passed_along(payload, "seq", offset - local_heads)
        returned_heads.append(jnp.where(own_head >= offset, back_below, back_above))
    by_head = jnp.take(jnp.stack(returned_heads), ordering, axis=0)
    attended = by_head.transpose(1, 0, 2).reshape(rows, channels)
    return (banded, attended)


def local(*arrays):
    pencil = arrays[3].shape[0]
    rows = arrays[0].shape[1]
    stripes = lax.axis_size("seq")
    even = stripes % 2 == 0 and stripes & (stripes - 1) == 0 and 2 * stripes <= HEAD_DIM
    one_head = pencil == HEAD_DIM and even and rows % (16 * TILES) == 0
    return fused(*arrays) if one_head else general(*arrays)


def solution(mesh):
    placed = (
        P("chan", "seq"),
        P("chan", "seq"),
        P("chan", "seq"),
        P(("chan", "seq"), None),
        P(("chan", "seq")),
        P(),
        P("seq", "chan"),
        P("seq", "chan"),
        P("chan"),
    )
    return jax.shard_map(
        local,
        mesh=mesh,
        in_specs=placed,
        out_specs=(P("chan", "seq"), P("seq", "chan")),
        check_vma=False,
    )
```

```python
import functools
import math

import jax
import jax.numpy as jnp
import ml_dtypes
import numpy as np
from jax import lax
from jax.experimental import pallas as pl
from jax.experimental.pallas import tpu as pltpu
from jax.sharding import PartitionSpec as P

D = 4096
HEAD_DIM = 128
TILES = 4
MESH = pl.DeviceIdType.MESH
PRODUCT, QUERIES, KEYS, GATES, BANDED, ATTENDED, SQUARES = range(7)


def high_low(table):
    high = table.astype(ml_dtypes.bfloat16)
    low = (table - high.astype(np.float64)).astype(ml_dtypes.bfloat16)
    return np.stack((high, low))


def odd_tables(stripes, rows):
    frequency = np.arange(rows, dtype=np.float64) + 0.5
    angle = 2.0 * np.pi * frequency[:, None] * np.arange(rows)[None, :] / (2 * rows)
    dense = np.concatenate((np.cos(angle), -np.sin(angle)), axis=0)
    twist = 2.0 * np.pi * frequency[:, None] * np.arange(stripes)[None, :] / (2 * rows * stripes)
    turns = np.stack((np.cos(twist), np.sin(twist))).astype(np.float32)
    turns = np.repeat(turns, HEAD_DIM, axis=2)
    return high_low(dense), high_low(dense.T), turns


def small_dft(parts, sign):
    count = len(parts)
    if count == 1:
        return parts
    even = small_dft(parts[0::2], sign)
    odd = small_dft(parts[1::2], sign)
    first, second = [], []
    for k in range(count // 2):
        real, imag = odd[k]
        cos = math.cos(2.0 * math.pi * k / count)
        sin = sign * math.sin(2.0 * math.pi * k / count)
        if k == 0:
            turned = (real, imag)
        elif 4 * k == count:
            turned = (-sign * imag, sign * real)
        else:
            turned = (real * cos - imag * sin, real * sin + imag * cos)
        first.append((even[k][0] + turned[0], even[k][1] + turned[1]))
        second.append((even[k][0] - turned[0], even[k][1] - turned[1]))
    return first + second


def dot(left, right):
    return jnp.dot(left, right, preferred_element_type=jnp.float32)


def split(wide):
    high = wide.astype(jnp.bfloat16)
    return high, (wide - high.astype(jnp.float32)).astype(jnp.bfloat16)


def fused_kernel(
    n,
    chans,
    order_ref,
    skip_ref,
    gain_ref,
    hk_hbm,
    hv_hbm,
    hq_hbm,
    filter_hbm,
    q_hbm,
    k_hbm,
    forward_hbm,
    inverse_hbm,
    turns_hbm,
    banded_ref,
    attended_ref,
    hk_ref,
    hv_ref,
    gate_all,
    q_all,
    k_all,
    product_out,
    product_in,
    gate_in,
    q_in,
    k_in,
    filter_ref,
    forward_ref,
    inverse_ref,
    turns_ref,
    upright,
    signal,
    section,
    spectrum,
    back,
    convolved,
    gated,
    gated_out,
    values,
    result,
    squares,
    squares_chan,
    squares_sum,
    squares_seq,
    bias,
    turned_keys,
    send_sem,
    recv_sem,
    chan_send,
    chan_recv,
    local_sem,
):
    me = lax.axis_index("seq")
    my_chan = lax.axis_index("chan")
    pencil, rows = product_in.shape[1:]
    tile = rows // TILES
    wide_tile = n * tile

    def peer(offset):
        return lax.rem(me + offset, n)

    half = n // 2
    inner = lax.rem(me, half)
    near, across = me - inner, half - (me - inner)
    phase = lax.rem(my_chan + me // 2, 2)
    targets = []
    for turn in range(half):
        far = across + lax.rem(inner + turn, half)
        if turn == half - 1:
            targets.append(far)
        else:
            beside = near + lax.rem(inner + 1 + turn, half)
            targets.append(far * (1 - phase) + beside * phase)
            targets.append(beside * (1 - phase) + far * phase)
    offsets = [lax.rem(target - me + n, n) for target in targets]

    def block(ref, index):
        return ref.at[pl.ds(pl.multiple_of(index * pencil, pencil), pencil), :]

    def column(ref, index):
        return ref.at[:, pl.ds(pl.multiple_of(index * pencil, pencil), pencil)]

    def exchange(kind, source, here):
        return [
            pltpu.make_async_remote_copy(
                src_ref=source(target),
                dst_ref=here,
                send_sem=send_sem.at[kind, offset],
                recv_sem=recv_sem.at[kind, offset],
                device_id={"seq": target},
                device_id_type=MESH,
            )
            for target, offset in zip(targets, offsets)
        ]

    barrier = pltpu.get_barrier_semaphore()
    for offset in range(1, n):
        pl.semaphore_signal(barrier, inc=1, device_id={"seq": peer(offset)}, device_id_type=MESH)
    for offset in range(1, chans):
        other = lax.rem(my_chan + offset, chans)
        pl.semaphore_signal(barrier, inc=1, device_id={"chan": other}, device_id_type=MESH)

    staged = [
        (hk_hbm, hk_ref),
        (hv_hbm, hv_ref),
        (hq_hbm, gate_all),
        (filter_hbm, filter_ref),
        (forward_hbm, forward_ref),
        (inverse_hbm, inverse_ref),
        (turns_hbm, turns_ref),
        (q_hbm, q_all),
        (k_hbm, k_all),
    ]
    staged = [
        pltpu.make_async_copy(source, target, local_sem.at[index])
        for index, (source, target) in enumerate(staged)
    ]
    for copy in staged:
        copy.start()

    products = exchange(PRODUCT, lambda d: product_out.at[d], product_in.at[me])
    queries = exchange(QUERIES, lambda d: column(q_all, d), q_in.at[me])
    keys = exchange(KEYS, lambda d: column(k_all, d), k_in.at[me])
    gates = exchange(GATES, lambda d: block(gate_all, d), gate_in.at[me])

    def product_of(index):
        return (
            block(hk_ref, index)[...].astype(jnp.float32)
            * block(hv_ref, index)[...].astype(jnp.float32)
        ).astype(jnp.bfloat16)

    for copy in staged[:2]:
        copy.wait()
    pl.semaphore_wait(barrier, n - 1 + chans - 1)
    for target, copy in zip(targets, products):
        product_out[target] = product_of(target)
        copy.start()
    staged[2].wait()
    for copy in gates:
        copy.start()
    product_in[me] = product_of(me)
    gate_in[me] = block(gate_all, me)[...]

    for copy in staged[3:]:
        copy.wait()
    q_in[me] = column(q_all, me)[...]
    k_in[me] = column(k_all, me)[...]

    def turned_sections(part):
        parts = []
        for t in range(n):
            real = section[part, t * pencil : (t + 1) * pencil]
            below = pl.ds(pl.multiple_of(rows + part.start, part.size), part.size)
            imag = section[below, t * pencil : (t + 1) * pencil]
            lanes = slice(t * pencil, (t + 1) * pencil)
            c, s = turns_ref[0, part, lanes], turns_ref[1, part, lanes]
            parts.append((real * c + imag * s, imag * c - real * s))
        return small_dft(parts, -1.0)

    step = 16

    def filter_spectrum(index, unused):
        part = pl.ds(pl.multiple_of(index * step, step), step)
        scale = 1.0 / (rows * n)
        for k, (real, imag) in enumerate(turned_sections(part)):
            spectrum[0, part, k * pencil : (k + 1) * pencil] = real * scale
            spectrum[1, part, k * pencil : (k + 1) * pencil] = imag * scale
        return unused

    def signal_spectrum(index, unused):
        part = pl.ds(pl.multiple_of(index * step, step), step)
        below = pl.ds(pl.multiple_of(rows + index * step, step), step)
        parts = []
        for k, (real, imag) in enumerate(turned_sections(part)):
            other_real = spectrum[0, part, k * pencil : (k + 1) * pencil]
            other_imag = spectrum[1, part, k * pencil : (k + 1) * pencil]
            parts.append(
                (real * other_real - imag * other_imag, real * other_imag + imag * other_real)
            )
        for t, (real, imag) in enumerate(small_dft(parts, 1.0)):
            lanes = slice(t * pencil, (t + 1) * pencil)
            c, s = turns_ref[0, part, lanes], turns_ref[1, part, lanes]
            for place, value in ((part, real * c - imag * s), (below, real * s + imag * c)):
                high, low = split(value)
                back[0, place, lanes] = high
                back[1, place, lanes] = low
        return unused

    for s in range(n):
        upright[s * rows : (s + 1) * rows, :] = filter_ref[:, s * rows : (s + 1) * rows].T
    for t in range(0, n, 2):
        pair = jnp.concatenate(
            [upright[pl.ds(t + u, rows, stride=n), :] for u in range(2)], axis=1
        )
        high, low = split(pair)
        section[:, t * pencil : (t + 2) * pencil] = (
            dot(forward_ref[0], high) + dot(forward_ref[1], high) + dot(forward_ref[0], low)
        )
    lax.fori_loop(0, rows // step, filter_spectrum, 0)
    for copy in queries:
        copy.start()

    def place_of(index):
        place = n * index + order_ref[0]
        for s in range(1, n):
            change = order_ref[s * rows] - order_ref[(s - 1) * rows] - n * tile
            place = place + jnp.where(index >= s * tile, change, 0)
        return place

    key_place = place_of(lax.broadcasted_iota(jnp.int32, (8, wide_tile), 1))[:1]
    query_place = place_of(lax.broadcasted_iota(jnp.int32, (wide_tile, 128), 0))[:, :1]
    bias[...] = jnp.where(key_place <= query_place, 0.0, -1e30)

    for copy in products:
        copy.wait()

    for copy in keys:
        copy.start()

    def stand_up(source):
        for s in range(n):
            upright[s * rows : (s + 1) * rows, :] = source[s].T.astype(jnp.float32)

    stand_up(product_in)
    for t in range(0, n, 2):
        pair = [upright[pl.ds(t + u, rows, stride=n), :] for u in range(2)]
        signal[t] = pair[0]
        signal[t + 1] = pair[1]
        exact = jnp.concatenate(pair, axis=1).astype(jnp.bfloat16)
        section[:, t * pencil : (t + 2) * pencil] = dot(forward_ref[0], exact) + dot(
            forward_ref[1], exact
        )
    lax.fori_loop(0, rows // step, signal_spectrum, 0)
    for t in range(0, n, 2):
        lanes = slice(t * pencil, (t + 2) * pencil)
        high, low = back[0, :, lanes], back[1, :, lanes]
        pair = dot(inverse_ref[0], high) + dot(inverse_ref[1], high) + dot(inverse_ref[0], low)
        for u in range(2):
            convolved[t + u] = (
                pair[:, u * pencil : (u + 1) * pencil] + skip_ref[...] * signal[t + u]
            )

    for copy in gates:
        copy.wait()
    stand_up(gate_in)
    for t in range(n):
        gated[t] = (upright[pl.ds(t, rows, stride=n), :] * convolved[t]).astype(jnp.bfloat16)

    banded = exchange(BANDED, lambda d: gated_out.at[d], block(banded_ref, me))
    lane = lax.broadcasted_iota(jnp.int32, (pencil, pencil), 1)
    summed_squares = jnp.zeros((rows, pencil), jnp.float32)
    for s in range(n):
        mine = gated[order_ref[s * rows]]
        values[s] = jnp.concatenate((mine, jnp.ones_like(mine)), axis=1)
        wide = mine.astype(jnp.float32)
        high, low = split(wide * wide)
        pick = jnp.where(lane == s, 1.0, 0.0).astype(jnp.bfloat16)
        summed_squares = summed_squares + dot(high, pick) + dot(low, pick)
    squares[...] = summed_squares.T[:n, :]
    beside_chan = [
        pltpu.make_async_remote_copy(
            src_ref=squares,
            dst_ref=squares_chan.at[offset],
            send_sem=chan_send.at[offset],
            recv_sem=chan_recv.at[offset],
            device_id={"chan": lax.rem(my_chan + offset, chans)},
            device_id_type=MESH,
        )
        for offset in range(1, chans)
    ]
    for copy in beside_chan:
        copy.start()
    for copy in beside_chan:
        copy.wait()
    squares_sum[...] = functools.reduce(
        jnp.add, [squares[...]] + [squares_chan[offset] for offset in range(1, chans)]
    )
    along = exchange(SQUARES, lambda d: squares_sum, squares_seq.at[me])
    for copy in along:
        copy.start()
    for s in range(n):
        gated_out[s] = values[s, :, :pencil].T
    squares_seq[me] = squares_sum[...]
    for copy in keys:
        copy.wait_send()
    for copy in banded:
        copy.start()
    block(banded_ref, me)[...] = gated_out[me]
    for copy in queries:
        copy.wait()
    for copy in keys:
        copy.wait_recv()
    for kt in range(TILES):
        key = k_in[:, kt * tile : (kt + 1) * tile, :].reshape(wide_tile, pencil)
        turned_keys[kt] = key.T
    for copy in along:
        copy.wait()
    inverse_rms = lax.rsqrt(
        functools.reduce(jnp.add, [squares_seq[s] for s in range(n)]) / D + 1e-05
    )
    gain = gain_ref[pl.ds(me, 1), :]
    scales = jnp.concatenate([inverse_rms] * (pencil // n), axis=0).T
    for s in range(n):
        normed = values[s, :, :pencil].astype(jnp.float32) * scales[:, s : s + 1] * gain
        values[s, :, :pencil] = normed.astype(jnp.bfloat16)

    factor = math.log2(math.e) / math.sqrt(HEAD_DIM)
    height = half * tile
    attended = exchange(ATTENDED, lambda d: result.at[d], column(attended_ref, me))

    def attend_half(turn, unused):
        h = lax.rem(1 - me // half + turn, 2)
        first = pl.multiple_of(h * half, half)
        for jt in range(TILES):
            query = q_in[pl.ds(first, half), jt * tile : (jt + 1) * tile, :]
            query = query.reshape(height, pencil)
            scores = []
            for kt in range(jt + 1):
                score = dot(query, turned_keys[kt])
                if kt == jt:
                    score = score + bias[pl.ds(pl.multiple_of(h * height, height), height), :]
                scores.append(score)
            top = jnp.max(functools.reduce(jnp.maximum, scores), axis=1, keepdims=True)
            summed = jnp.zeros((height, 2 * pencil), jnp.float32)
            for kt, score in enumerate(scores):
                weight = jnp.exp2((score - top) * factor)
                value = values[:, kt * tile : (kt + 1) * tile, :].reshape(wide_tile, 2 * pencil)
                summed = summed + dot(weight.astype(jnp.bfloat16), value)
            part = (summed[:, :pencil] / summed[:, pencil:]).astype(jnp.bfloat16)
            result[pl.ds(first, half), jt * tile : (jt + 1) * tile, :] = part.reshape(
                half, tile, pencil
            )
        for target, copy in zip(targets, attended):

            @pl.when(target // half == h)
            def send():
                copy.start()

        return unused

    lax.fori_loop(0, 2, attend_half, 0)
    column(attended_ref, me)[...] = result[me]
    for copy in banded + attended:
        copy.wait()


def fused(
    hyena_query,
    hyena_key,
    hyena_value,
    long_filter,
    skip_weight,
    stripe_order,
    query_rows,
    key_rows,
    norm_gain,
):
    n = lax.axis_size("seq")
    chans = lax.axis_size("chan")
    channels, rows = hyena_query.shape
    pencil = long_filter.shape[0]
    forward_table, inverse_table, turns = odd_tables(n, rows)
    vmem = pl.BlockSpec(memory_space=pltpu.VMEM)
    far = pl.BlockSpec(memory_space=pl.ANY)
    bf16, f32 = jnp.bfloat16, jnp.float32
    wide = n * pencil
    tile = rows // TILES
    return pl.pallas_call(
        functools.partial(fused_kernel, n, chans),
        out_shape=(
            jax.ShapeDtypeStruct((channels, rows), bf16),
            jax.ShapeDtypeStruct((rows, channels), bf16),
        ),
        in_specs=[pl.BlockSpec(memory_space=pltpu.SMEM)] + [vmem] * 2 + [far] * 9,
        out_specs=(vmem, vmem),
        scratch_shapes=[
            pltpu.VMEM((channels, rows), bf16),
            pltpu.VMEM((channels, rows), bf16),
            pltpu.VMEM((channels, rows), bf16),
            pltpu.VMEM((rows, channels), bf16),
            pltpu.VMEM((rows, channels), bf16),
            pltpu.VMEM((n, pencil, rows), bf16),
            pltpu.VMEM((n, pencil, rows), bf16),
            pltpu.VMEM((n, pencil, rows), bf16),
            pltpu.VMEM((n, rows, pencil), bf16),
            pltpu.VMEM((n, rows, pencil), bf16),
            pltpu.VMEM(long_filter.shape, f32),
            pltpu.VMEM(forward_table.shape, bf16),
            pltpu.VMEM(inverse_table.shape, bf16),
            pltpu.VMEM(turns.shape, f32),
            pltpu.VMEM((n * rows, pencil), f32),
            pltpu.VMEM((n, rows, pencil), f32),
            pltpu.VMEM((2 * rows, wide), f32),
            pltpu.VMEM((2, rows, wide), f32),
            pltpu.VMEM((2, 2 * rows, wide), bf16),
            pltpu.VMEM((n, rows, pencil), f32),
            pltpu.VMEM((n, rows, pencil), bf16),
            pltpu.VMEM((n, pencil, rows), bf16),
            pltpu.VMEM((n, rows, 2 * pencil), bf16),
            pltpu.VMEM((n, rows, pencil), bf16),
            pltpu.VMEM((n, rows), f32),
            pltpu.VMEM((chans, n, rows), f32),
            pltpu.VMEM((n, rows), f32),
            pltpu.VMEM((n, n, rows), f32),
            pltpu.VMEM((n * tile, n * tile), f32),
            pltpu.VMEM((TILES, pencil, n * tile), bf16),
            pltpu.SemaphoreType.DMA((7, n)),
            pltpu.SemaphoreType.DMA((7, n)),
            pltpu.SemaphoreType.DMA((chans,)),
            pltpu.SemaphoreType.DMA((chans,)),
            pltpu.SemaphoreType.DMA((9,)),
        ],
        compiler_params=pltpu.CompilerParams(
            collective_id=0, has_side_effects=True, vmem_limit_bytes=60 * 1024 * 1024
        ),
    )(
        stripe_order,
        skip_weight.reshape(1, pencil),
        norm_gain.reshape(n, pencil),
        hyena_key,
        hyena_value,
        hyena_query,
        long_filter,
        query_rows,
        key_rows,
        jnp.asarray(forward_table),
        jnp.asarray(inverse_table),
        jnp.asarray(turns),
    )


def passed_along(block, axis, distance):
    devices = range(lax.axis_size(axis))
    route = [((i - distance) % len(devices), i) for i in devices]
    return lax.ppermute(block, axis, route)


def angle_table(first, second, modulus):
    left = jnp.arange(first, dtype=jnp.int32)[:, None]
    right = jnp.arange(second, dtype=jnp.int32)[None, :]
    theta = 2.0 * math.pi / modulus * (left * right % modulus).astype(jnp.float32)
    return (jnp.cos(theta), jnp.sin(theta))


def transform_tables(length):
    outer = 2 * length // 128
    first_cos, first_sin = angle_table(outer, outer // 2, outer)
    twist_cos, twist_sin = angle_table(outer, 128, 2 * length)
    inner_cos, inner_sin = angle_table(128, 128, 128)
    return (first_cos, first_sin, twist_cos, twist_sin, inner_cos, inner_sin)


def contract(form, left, right):
    return jnp.einsum(form, left, right, precision=lax.Precision.HIGHEST)


def forward(signal, tables):
    first_cos, first_sin, twist_cos, twist_sin, inner_cos, inner_sin = tables
    section_real = contract("kt,cts->cks", first_cos, signal)
    section_imag = -contract("kt,cts->cks", first_sin, signal)
    turned_real = section_real * twist_cos + section_imag * twist_sin
    turned_imag = section_imag * twist_cos - section_real * twist_sin
    out_real = contract("cks,sm->ckm", turned_real, inner_cos) + contract(
        "cks,sm->ckm", turned_imag, inner_sin
    )
    out_imag = contract("cks,sm->ckm", turned_imag, inner_cos) - contract(
        "cks,sm->ckm", turned_real, inner_sin
    )
    return (out_real, out_imag)


def inverse(spectrum_real, spectrum_imag, tables):
    first_cos, first_sin, twist_cos, twist_sin, inner_cos, inner_sin = tables
    back_real = contract("ckm,sm->cks", spectrum_real, inner_cos) - contract(
        "ckm,sm->cks", spectrum_imag, inner_sin
    )
    back_imag = contract("ckm,sm->cks", spectrum_real, inner_sin) + contract(
        "ckm,sm->cks", spectrum_imag, inner_cos
    )
    turned_real = back_real * twist_cos - back_imag * twist_sin
    turned_imag = back_real * twist_sin + back_imag * twist_cos
    signal = contract("kt,cks->cts", first_cos, turned_real) - contract(
        "kt,cks->cts", first_sin, turned_imag
    )
    return signal * (1.0 / (first_cos.shape[0] * 128))


def convolve(signal, filter_parts, tables):
    pencil, length = signal.shape
    widened = signal.astype(jnp.float32).reshape(pencil, length // 128, 128)
    signal_real, signal_imag = forward(widened, tables)
    filter_real, filter_imag = filter_parts
    product_real = signal_real * filter_real - signal_imag * filter_imag
    product_imag = signal_real * filter_imag + signal_imag * filter_real
    return inverse(product_real, product_imag, tables).reshape(pencil, length)


def fold_keys(carry, queries, own_places, key_piece, value_piece, places, scale):
    count = key_piece.shape[0]
    heads = queries.shape[1]
    depth = queries.shape[2]
    block = math.gcd(count, 512)
    place_blocks = places.reshape(count // block, block)
    key_blocks = key_piece.reshape(count // block, block, heads, depth)
    value_blocks = value_piece.reshape(count // block, block, heads, depth)

    def one_block(state, inputs):
        running, totals, sums = state
        key_block, value_block, key_places = inputs
        scores = (
            jnp.einsum("qhd,khd->hqk", queries, key_block, preferred_element_type=jnp.float32)
            * scale
        )
        allowed = key_places[None, None, :] <= own_places[None, :, None]
        scores = jnp.where(allowed, scores, -1e30)
        highest = jnp.maximum(running, jnp.max(scores, axis=2))
        weights = jnp.where(allowed, jnp.exp(scores - highest[:, :, None]), 0.0)
        factor = jnp.exp(running - highest)
        totals = totals * factor + jnp.sum(weights, axis=2)
        update = jnp.einsum(
            "hqk,khd->hqd",
            weights.astype(jnp.bfloat16),
            value_block,
            preferred_element_type=jnp.float32,
        )
        sums = sums * factor[:, :, None] + update
        return ((highest, totals, sums), None)

    carry, unused = lax.scan(one_block, carry, (key_blocks, value_blocks, place_blocks))
    return carry


def general(
    hyena_query,
    hyena_key,
    hyena_value,
    long_filter,
    skip_weight,
    stripe_order,
    query_rows,
    key_rows,
    norm_gain,
):
    stripes = lax.axis_size("seq")
    channels, rows = hyena_query.shape
    pencil, length = long_filter.shape
    sigma = stripe_order.reshape(stripes, rows)[:, 0]
    product = (hyena_key.astype(jnp.float32) * hyena_value.astype(jnp.float32)).astype(jnp.bfloat16)
    tables = transform_tables(length)
    filter_parts = forward(long_filter.reshape(pencil, length // 128, 128), tables)
    spread = lax.all_to_all(product, "seq", split_axis=0, concat_axis=1, tiled=True)
    summed = convolve(spread, filter_parts, tables) + skip_weight[:, None] * spread.astype(
        jnp.float32
    )
    returned = lax.all_to_all(
        summed.astype(jnp.bfloat16), "seq", split_axis=1, concat_axis=0, tiled=True
    ).astype(summed.dtype)
    gated = (hyena_query.astype(jnp.float32) * returned).astype(jnp.bfloat16)
    per_stripe = rows // stripes
    columns = stripes * jnp.arange(per_stripe, dtype=jnp.int32)[None, :] + sigma[:, None]
    arranged = jnp.take(gated, columns.reshape(rows), axis=1).reshape(channels, stripes, per_stripe)
    banded = lax.all_to_all(arranged, "seq", split_axis=1, concat_axis=2, tiled=True).reshape(
        channels, rows
    )
    output_wide = banded.astype(jnp.float32)
    squares = lax.psum(jnp.sum(output_wide * output_wide, axis=0), "chan")
    inverse_rms = lax.rsqrt(squares / D + 1e-05)
    normed = (output_wide * inverse_rms[None, :] * norm_gain[:, None]).astype(jnp.bfloat16)
    value_rows = normed.T
    local_heads = channels // HEAD_DIM
    scale = 1.0 / math.sqrt(HEAD_DIM)
    seq_index = lax.axis_index("seq")
    own_head = seq_index % local_heads
    group_index = seq_index // local_heads
    group_count = stripes // local_heads
    span = local_heads * rows
    stacked_local = jnp.stack((query_rows, key_rows, value_rows)).reshape(
        3, rows, local_heads, HEAD_DIM
    )
    collected = [lax.dynamic_index_in_dim(stacked_local, own_head, 2, keepdims=False)]
    for offset in range(1, local_heads):
        payload = lax.dynamic_index_in_dim(
            stacked_local, (own_head + offset) % local_heads, 2, keepdims=False
        )
        from_below = passed_along(payload, "seq", offset)
        from_above = passed_along(payload, "seq", offset - local_heads)
        collected.append(jnp.where(own_head >= offset, from_below, from_above))
    ordering = (own_head - jnp.arange(local_heads, dtype=jnp.int32)) % local_heads
    sources = jnp.take(jnp.stack(collected), ordering, axis=0)
    combined = sources.transpose(1, 0, 2, 3).reshape(3, span, HEAD_DIM)
    group_places = lax.dynamic_slice_in_dim(stripe_order, group_index * span, span)
    group_queries = combined[0].reshape(span, 1, HEAD_DIM)

    def visit(state, kv_pair, source):
        places = lax.dynamic_slice_in_dim(stripe_order, source * span, span)
        return fold_keys(
            state,
            group_queries,
            group_places,
            kv_pair[0].reshape(span, 1, HEAD_DIM),
            kv_pair[1].reshape(span, 1, HEAD_DIM),
            places,
            scale,
        )

    initial_group = (
        jnp.full((1, span), -1e30, jnp.float32),
        jnp.zeros((1, span), jnp.float32),
        jnp.zeros((1, span, HEAD_DIM), jnp.float32),
    )

    def cycle_turn(turn, loop_state):
        state, kv_pair = loop_state
        state = visit(state, kv_pair, (group_index - turn) % group_count)
        kv_pair = passed_along(kv_pair, "seq", local_heads)
        return (state, kv_pair)

    state, kv_pair = lax.fori_loop(0, group_count - 1, cycle_turn, (initial_group, combined[1:]))
    running, totals, sums = visit(state, kv_pair, (group_index - (group_count - 1)) % group_count)
    result = (sums[0] / totals[0][:, None]).astype(jnp.bfloat16)
    pieces = result.reshape(local_heads, rows, HEAD_DIM)
    returned_heads = [lax.dynamic_index_in_dim(pieces, own_head, 0, keepdims=False)]
    for offset in range(1, local_heads):
        payload = lax.dynamic_index_in_dim(
            pieces, (own_head + offset) % local_heads, 0, keepdims=False
        )
        back_below = passed_along(payload, "seq", offset)
        back_above = passed_along(payload, "seq", offset - local_heads)
        returned_heads.append(jnp.where(own_head >= offset, back_below, back_above))
    by_head = jnp.take(jnp.stack(returned_heads), ordering, axis=0)
    attended = by_head.transpose(1, 0, 2).reshape(rows, channels)
    return (banded, attended)


def local(*arrays):
    pencil = arrays[3].shape[0]
    rows = arrays[0].shape[1]
    stripes = lax.axis_size("seq")
    even = stripes % 2 == 0 and stripes & (stripes - 1) == 0 and 2 * stripes <= HEAD_DIM
    one_head = pencil == HEAD_DIM and even and rows % (16 * TILES) == 0
    return fused(*arrays) if one_head else general(*arrays)


def solution(mesh):
    placed = (
        P("chan", "seq"),
        P("chan", "seq"),
        P("chan", "seq"),
        P(("chan", "seq"), None),
        P(("chan", "seq")),
        P(),
        P("seq", "chan"),
        P("seq", "chan"),
        P("chan"),
    )
    return jax.shard_map(
        local,
        mesh=mesh,
        in_specs=placed,
        out_specs=(P("chan", "seq"), P("seq", "chan")),
        check_vma=False,
    )
```
